128 devices in a mesh: section: 2 (over core), expert: 16 (over y, x), shard: 4 (over z).
Axes of the slice: x: 4, y: 4, z: 4, core: 2. Of those that a mesh axis runs over, the one named last changes fastest.
Arguments:
- inputs: float32 [2, 16, 256, 768], P(None, 'expert', 'shard'), may hold values from -6 to 6
- cotangent: float32 [2, 16, 256, 768], P(None, 'expert', 'shard'), may hold values from -6 to 6
- w_qkv: bfloat16 [2, 768, 2304], P('section', 'shard'), may hold values from -0.21875 to 0.21875
- w_attn: bfloat16 [2, 768, 768], P('section', 'shard'), may hold values from -0.875 to 0.875
- gain_one: bfloat16 [2, 768], P('section', 'shard'), may hold values from 0.5 to 1.5
- gain_two: bfloat16 [2, 768], P('section', 'shard'), may hold values from 0.5 to 1.5
- router: bfloat16 [2, 768, 32], P('section', 'shard'), may hold values from -0.15625 to 0.15625
- w_in: bfloat16 [2, 32, 768, 3072], P('section', 'expert', None, 'shard'), may hold values from -0.21875 to 0.21875
- w_out: bfloat16 [2, 32, 3072, 768], P('section', 'expert', 'shard'), may hold values from -0.109375 to 0.109375
- routes: int32 [2, 2, 16, 4, 64, 2], P('section', None, 'expert', 'shard'), may hold values from 0 to 31, all different within a row; in each aligned block of 64 rows (0 to 63, 64 to 127, ..., all dimensions but the last counted through in order) at most 5 rows name the same one
Outputs:
- activations: float32 [2, 2, 16, 256, 768], P('section', None, 'expert', 'shard')
- input_grads: float32 [2, 2, 16, 256, 768], P('section', None, 'expert', 'shard')
- grad_qkv: float32 [2, 768, 2304], P('section', ('expert', 'shard'))
- grad_attn: float32 [2, 768, 768], P('section', ('expert', 'shard'))
- grad_gain_one: float32 [2, 768], P('section', ('expert', 'shard'))
- grad_gain_two: float32 [2, 768], P('section', ('expert', 'shard'))
- grad_router: float32 [2, 768, 32], P('section', ('expert', 'shard'))
- grad_in: float32 [2, 32, 768, 3072], P('section', 'expert', None, 'shard')
- grad_out: float32 [2, 32, 3072, 768], P('section', 'expert', 'shard')
The draws below stay inside these ranges and needn't reach their ends.
Inputs may be any that keep to these rules, and one draw needn't show every extreme that they name: `routes`: each token names two different experts. In each aligned block of 64 tokens (one section, micro-batch, image group and position group) no expert is named more than 5 times, a bound that some block reaches.
All inputs are finite; a program needn't handle non-finite values.
Results may differ from the reference program's by a relative error of at most 0.03.
Values may be sent and summed in bfloat16 or wider, within the bound.
No kernel may reach another device: no remote copies, remote signals or barrier semaphores. Data moves between devices by JAX's collectives and lax.ppermute only.
A program may use at most 192 MiB of HBM per device.

```python
import math
import jax
import jax.numpy as jnp
import numpy as np
from jax import lax

D = 768
HEADS = 12
HDIM = 64
FF = 3072
IMG = 1
SEQ_DEV = 64
MICRO = 2
EXPERTS = 32
SEQ = 256
IMAGES = 16
T_DEV = 64
CAP = 5
N_EXPERT = 16
N_SHARD = 4


def level_of(key, extent, shards, smallest, top_value):
    def one(dim, parts):
        draws = jax.random.uniform(jax.random.fold_in(jax.random.fold_in(key, 6), dim), (parts,), jnp.float32, smallest / len(shards), top_value / len(shards))
        return jnp.repeat(jnp.exp(draws), extent[dim] // parts).reshape((-1,) + (1,) * (len(extent) - dim - 1))

    level = one(*shards[0])
    for cut in shards[1:]:
        level = level * one(*cut)
    return level


def shared_out(rng, own, number, rows, amount, top, reach, slope):
    order = jax.random.permutation(rng, amount)
    heavy_load, common = shares(amount, rows * top, reach, slope, True), shares(amount, rows * top, reach, slope, False)
    places = jnp.arange(amount)

    def named(sizes, offset_by):
        used = int((sizes > 0).sum())
        fixed = max(1, used // 4)
        shifted = fixed + (places - fixed + offset_by * (used - fixed)) % max(1, amount - fixed)
        return jnp.zeros((amount,), jnp.int32).at[order[jnp.where(places < fixed, places, shifted)]].set(jnp.asarray(sizes, jnp.int32))

    sizes = jnp.where(number % 4 == 0, named(heavy_load, number // 4), named(common, number - number // 4 - 1))
    mixed = jax.random.permutation(jax.random.fold_in(own, 3), amount)
    donor, sink = mixed[0:amount // 2 * 2:2], mixed[1:amount // 2 * 2:2]
    room = jnp.minimum(sizes[donor] - 1, reach - sizes[sink]) // 2
    room = jnp.where((donor == order[0]) | (sink == order[0]) | (sizes[sink] == 0), 0, jnp.maximum(room, 0))
    shifted = jax.random.randint(jax.random.fold_in(own, 4), (amount // 2,), 0, 1 << 20) % (room + 1)
    sizes = sizes.at[donor].add(-shifted).at[sink].add(shifted)
    labels = jnp.searchsorted(jnp.cumsum(sizes), jnp.arange(rows * top), side="right").astype(jnp.int32)
    table = labels.reshape(top, rows).T
    table = table[jax.random.permutation(jax.random.fold_in(own, 1), rows)]
    offset_by = jax.random.randint(jax.random.fold_in(own, 2), (rows, 1), 0, top)
    return jnp.take_along_axis(table, (jnp.arange(top)[None, :] + offset_by) % top, axis=1)


def shares(count, total, reach, slope, full):
    portions = [(1 << 20) // math.isqrt(grade ** slope) + 1 for grade in range(1, count + 1)]
    largest = reach if full else min(reach, max(-(-total // count), total * portions[0] // sum(portions)))
    least = 1 if total - largest >= count - 1 else 0
    counts, surplus = [largest] + [least] * (count - 1), total - largest - least * (count - 1)
    while surplus > 0:
        movable = [i for i in range(1, count) if counts[i] < largest] or [i for i in range(1, count) if counts[i] < reach]
        mass, budget = sum([portions[i] for i in movable]), surplus
        for i in movable:
            extra = min(reach - counts[i], max(1, budget * portions[i] // mass), surplus)
            counts[i] = counts[i] + extra
            surplus = surplus - extra
    return np.array(counts)


def noise(key, extent, scale, bound, split=(), kind=jnp.bfloat16):
    values = jax.random.normal(key, extent, jnp.float32) * scale
    if len(split) > 0:
        values = level_of(key, extent, split, -0.22, 0.18) * values
    return jnp.clip(values, min=-bound, max=bound).astype(kind)


def setup_inputs(seed: int = 0) -> dict:
    streams_of = jax.random.split(jax.random.key(seed), 11)
    inputs = noise(streams_of[0], (MICRO, IMAGES, SEQ, D), 1.0, 6.0, ((1, 16), (2, 4)), jnp.float32)
    cotangent = noise(streams_of[1], (MICRO, IMAGES, SEQ, D), 1.0, 6.0, ((1, 16), (2, 4)), jnp.float32)
    w_qkv = noise(streams_of[2], (2, D, 3 * D), D ** -0.5, 0.21875, ((0, 2), (1, 4)))
    w_attn = noise(streams_of[3], (2, D, D), (D // 16) ** -0.5, 0.875, ((0, 2), (1, 4)))
    gain_one = jnp.clip(1.0 + 0.1 * jax.random.normal(streams_of[4], (2, D), jnp.float32), 0.5, 1.5).astype(jnp.bfloat16)
    gain_two = jnp.clip(1.0 + 0.1 * jax.random.normal(streams_of[5], (2, D), jnp.float32), 0.5, 1.5).astype(jnp.bfloat16)
    router = noise(streams_of[6], (2, D, EXPERTS), (2 * D) ** -0.5, 0.15625, ((0, 2), (1, 4)))
    w_in = noise(streams_of[7], (2, EXPERTS, D, FF), D ** -0.5, 0.21875, ((0, 2), (1, 16), (3, 4)))
    w_out = noise(streams_of[8], (2, EXPERTS, FF, D), FF ** -0.5, 0.109375, ((0, 2), (1, 16), (2, 4)))
    routes_keys = jax.random.split(jax.random.fold_in(streams_of[9], 1), 2 * MICRO * N_EXPERT * N_SHARD * T_DEV // T_DEV)
    routes_turns = jax.random.permutation(jax.random.fold_in(streams_of[9], 3), 2 * MICRO * N_EXPERT * N_SHARD * T_DEV // T_DEV)
    routes = jax.vmap(lambda own, number: shared_out(jax.random.fold_in(streams_of[9], 2), own, number, T_DEV, EXPERTS, 2, CAP, 1))(routes_keys, routes_turns).reshape((2, MICRO, N_EXPERT, N_SHARD, T_DEV, 2))
    return dict(inputs=inputs, cotangent=cotangent, w_qkv=w_qkv, w_attn=w_attn, gain_one=gain_one, gain_two=gain_two, router=router, w_in=w_in, w_out=w_out, routes=routes)


@jax.custom_vjp
def low(v):
    return lax.optimization_barrier(v.astype(jnp.bfloat16)).astype(jnp.float32)

@jax.custom_vjp
def low_back(v):
    return v

def low_keep(v):
    return (low(v), None)

def low_pass(kept, grad):
    return (grad,)

def back_keep(v):
    return (v, None)

def back_low(kept, grad):
    return (low(grad),)
low.defvjp(low_keep, low_pass)
low_back.defvjp(back_keep, back_low)
precise = lax.Precision.HIGHEST

def layer_norm(token_rows, gain_vec):
    row_mean = lax.optimization_barrier(jnp.mean(token_rows, -1, keepdims=True))
    centered = token_rows - row_mean
    spread = lax.optimization_barrier(jnp.mean(centered * centered, -1, keepdims=True))
    return centered * lax.rsqrt(spread + 1e-06) * gain_vec

def slot_table(route_ids, experts, capacity):
    leading = route_ids.shape[:-2]
    flat_ids = route_ids.reshape(leading + (-1,))
    onehot = (flat_ids[..., None] == jnp.arange(experts, dtype=jnp.int32)).astype(jnp.int32)
    before = jnp.cumsum(onehot, -2) - onehot
    slot_ids = lax.optimization_barrier(jnp.sum(before * onehot, -1))
    slot_index = flat_ids * capacity + slot_ids
    placement = (slot_index[..., None] == jnp.arange(experts * capacity, dtype=jnp.int32)).astype(jnp.float32)
    return placement.reshape(route_ids.shape + (experts * capacity,))

def to_devices(field):
    return field.reshape(N_EXPERT, IMG, N_SHARD, SEQ_DEV, D).transpose(0, 2, 1, 3, 4).reshape(N_EXPERT, N_SHARD, T_DEV, D)

def from_devices(field):
    return field.reshape(N_EXPERT, N_SHARD, IMG, SEQ_DEV, D).transpose(0, 2, 1, 3, 4).reshape(IMAGES, SEQ, D)

def moe_block(state, w_qkv, w_attn, gain_one, gain_two, router, w_in, w_out, route_ids):
    normed = low(layer_norm(state, gain_one))
    projected = low_back(low(jnp.matmul(normed, w_qkv, precision=precise)))
    query = projected[..., :D].reshape(IMAGES, SEQ, HEADS, HDIM)
    key_all = projected[..., D:2 * D].reshape(IMAGES, SEQ, HEADS, HDIM)
    value_all = projected[..., 2 * D:].reshape(IMAGES, SEQ, HEADS, HDIM)
    score_scale = 1.0 / math.sqrt(HDIM)
    scores = low_back(jnp.einsum('isha,itha->ihst', query, key_all, precision=precise) * score_scale)
    attn_probs = low(jax.nn.softmax(scores, -1))
    attended = jnp.einsum('ihst,itha->isha', attn_probs, value_all, precision=precise).reshape(IMAGES, SEQ, D)
    attended = low_back(low(attended))
    middle = state + jnp.matmul(attended, w_attn, precision=precise)
    normed_b = low(layer_norm(middle, gain_two))
    token_rows = to_devices(normed_b)
    logits = jnp.matmul(token_rows, router, precision=precise)
    select = (route_ids[..., None] == jnp.arange(EXPERTS, dtype=jnp.int32)).astype(jnp.float32)
    chosen = lax.optimization_barrier(jnp.sum(select * logits[..., None, :], -1))
    gate_values = jax.nn.softmax(chosen, -1)
    placement = slot_table(route_ids, EXPERTS, CAP)
    taken_slots = lax.optimization_barrier(jnp.sum(placement, -2))
    outgoing = low_back(jnp.einsum('gjtc,gjtd->gjcd', taken_slots, token_rows, precision=precise))
    per_expert = outgoing.reshape(N_EXPERT * N_SHARD, EXPERTS, CAP, D).transpose(1, 0, 2, 3)
    per_expert = per_expert.reshape(EXPERTS, N_EXPERT * N_SHARD * CAP, D)
    expert_up = low_back(jnp.einsum('end,edf->enf', per_expert, w_in, precision=precise))
    hidden = low(jax.nn.gelu(expert_up, approximate=False))
    result = low_back(low(jnp.einsum('enf,efd->end', hidden, w_out, precision=precise)))
    returned = result.reshape(EXPERTS, N_EXPERT * N_SHARD, CAP, D).transpose(1, 0, 2, 3)
    returned = returned.reshape(N_EXPERT, N_SHARD, EXPERTS * CAP, D)
    mixing = lax.optimization_barrier(jnp.sum(placement * gate_values[..., None], -2))
    combined = jnp.einsum('gjtc,gjcd->gjtd', mixing, returned, precision=precise)
    return middle + from_devices(combined)

def reference(inputs, cotangent, w_qkv, w_attn, gain_one, gain_two, router, w_in, w_out, routes):
    params = tuple((weight.astype(jnp.float32) for weight in (w_qkv, w_attn, gain_one, gain_two, router, w_in, w_out)))
    section_delta = jnp.zeros_like(inputs)

    def two_sections(inputs, section_delta, params):
        firsts = []
        seconds = []
        for micro_index in range(MICRO):
            first_out = moe_block(inputs[micro_index], *[weight[0] for weight in params], routes[0, micro_index])
            second_in = low_back(low(first_out + section_delta[micro_index]))
            second_out = moe_block(second_in, *[weight[1] for weight in params], routes[1, micro_index])
            firsts.append(first_out)
            seconds.append(second_out)
        return (jnp.stack(firsts), jnp.stack(seconds))
    (firsts, seconds), pullback = jax.vjp(two_sections, inputs, section_delta, params)
    grad_inputs, grad_delta, grad_params = pullback((jnp.zeros_like(firsts), cotangent))
    activations = jnp.stack([firsts, seconds])
    input_grads = jnp.stack([grad_inputs, grad_delta])
    return (activations, input_grads, grad_params[0], grad_params[1], grad_params[2], grad_params[3], grad_params[4], grad_params[5], grad_params[6])
```

```python
import functools
import math

import jax
import jax.numpy as jnp
from jax import lax
from jax.experimental import pallas as pl
from jax.experimental.pallas import tpu as pltpu
from jax.sharding import PartitionSpec as P

F32 = jnp.float32
BF16 = jnp.bfloat16
D = 768
HEADS_OWN = 3
HDIM = 64
T = 64
CAP = 5
CHUNKS = 6
ROWS = 2 * CAP
N_EXPERT = 16
N_SHARD = 4
N_ALL = N_EXPERT * N_SHARD
SIDE = 64
BLOCK = N_EXPERT * SIDE
GROUP = N_EXPERT * CAP
ORDERED = CHUNKS * 2 * GROUP
EPS = 1e-06
SCALE = 1.0 / math.sqrt(HDIM)


def dot(a, b):
    return lax.dot_general(a, b, (((1,), (0,)), ((), ())), preferred_element_type=F32)


def dot_nt(a, b):
    return lax.dot_general(a, b, (((1,), (1,)), ((), ())), preferred_element_type=F32)


def dot_tn(a, b):
    return lax.dot_general(a, b, (((0,), (0,)), ((), ())), preferred_element_type=F32)


def iota(shape, dim):
    return lax.broadcasted_iota(jnp.int32, shape, dim)


def call(body, outs, ins, scratch=(), anywhere=(), scalars=1):
    specs = []
    for place in range(len(ins)):
        if place < scalars:
            specs.append(pl.BlockSpec(memory_space=pltpu.SMEM))
        elif place in anywhere:
            specs.append(pl.BlockSpec(memory_space=pl.ANY))
        else:
            specs.append(pl.BlockSpec(memory_space=pltpu.VMEM))
    return pl.pallas_call(
        body,
        out_shape=tuple(jax.ShapeDtypeStruct(shape, kind) for shape, kind in outs),
        in_specs=specs,
        out_specs=tuple(pl.BlockSpec(memory_space=pltpu.VMEM) for _ in outs),
        scratch_shapes=list(scratch),
        compiler_params=pltpu.CompilerParams(vmem_limit_bytes=48 * 1024 * 1024),
    )(*ins)


def fetch(mine, own, other, target, sem):
    @pl.when(mine)
    def _():
        pltpu.make_async_copy(own, target, sem).start()

    @pl.when(jnp.logical_not(mine))
    def _():
        pltpu.make_async_copy(other, target, sem).start()


def arrive(own, target, sem):
    pltpu.make_async_copy(own, target, sem).wait()


def norm_parts(rows):
    centered = rows - jnp.mean(rows, -1, keepdims=True)
    inverse = lax.rsqrt(jnp.mean(centered * centered, -1, keepdims=True) + EPS)
    return centered * inverse, inverse


def norm_back(grad, gain, unit, inverse):
    scaled = grad * gain
    return inverse * (
        scaled
        - jnp.mean(scaled, -1, keepdims=True)
        - unit * jnp.mean(scaled * unit, -1, keepdims=True)
    )


def split_pair(values):
    upper = values.astype(BF16)
    return upper, (values - upper.astype(F32)).astype(BF16)


def slots_in_row(route_row):
    named = (iota((32, 2 * T), 0) == route_row).astype(F32)
    earlier = ((iota((2 * T, 2 * T), 0) & (T - 1)) < (iota((2 * T, 2 * T), 1) & (T - 1))).astype(BF16)
    before = dot(named.astype(BF16), earlier)
    return route_row * CAP + jnp.sum(before * named, 0, keepdims=True).astype(jnp.int32)


def slots_in_column(route_column):
    named = (iota((2 * T, 32), 1) == route_column).astype(F32)
    earlier = ((iota((2 * T, 2 * T), 1) & (T - 1)) < (iota((2 * T, 2 * T), 0) & (T - 1))).astype(BF16)
    before = dot(earlier, named.astype(BF16))
    return route_column * CAP + jnp.sum(before * named, 1, keepdims=True).astype(jnp.int32)


def packed_place(index):
    within = index & (SIDE - 1)
    chunk = (within * 205) >> 11
    return (index >> 6) * ROWS + within - chunk * ROWS, chunk


def to_packed(slot_row, rows):
    slot, chunk = packed_place(iota((BLOCK, 2 * T), 0))
    hit = slot == slot_row
    total = None
    for c in range(CHUNKS):
        mask = jnp.where(hit & (chunk == c), 1.0, 0.0).astype(BF16)
        part = dot(mask, rows[:, c * 128 : (c + 1) * 128])
        total = part if total is None else total + part
    return total.astype(BF16)


def from_packed(slot_column, packed):
    slot, chunk = packed_place(iota((2 * T, BLOCK), 1))
    hit = slot == slot_column
    parts = []
    for c in range(CHUNKS):
        mask = jnp.where(hit & (chunk == c), 1.0, 0.0).astype(BF16)
        parts.append(dot(mask, packed))
    return jnp.concatenate(parts, 1)


def send_to_holders(packed, out_ref):
    blocks = packed.reshape(N_EXPERT, SIDE, 128)
    for s in range(N_SHARD):
        out_ref[:, s] = blocks


def sum_of_holders(in_ref):
    total = in_ref[:, 0].astype(F32)
    for s in range(1, N_SHARD):
        total = total + in_ref[:, s].astype(F32)
    return total.astype(BF16).reshape(BLOCK, 128)


def order_rows(order, packed_ref, store):
    for pair in range(2):
        low, high = 2 * pair * BLOCK, (2 * pair + 1) * BLOCK
        both = jnp.concatenate(
            [packed_ref[low : low + BLOCK, :], packed_ref[high : high + BLOCK, :]], 1
        )
        ordered = dot(order, both).astype(BF16)
        for half in range(2):
            group = 2 * pair + half
            for c in range(CHUNKS):
                for j in range(2):
                    start = c * 2 * GROUP + j * GROUP
                    store(j, group, c, ordered[start : start + GROUP, half * 128 : half * 128 + 128])


def unorder_rows(back_order, staged_ref, out_ref):
    for pair in range(2):
        both = jnp.concatenate([staged_ref[2 * pair], staged_ref[2 * pair + 1]], 1)
        packed = dot(back_order, both).astype(BF16)
        low, high = 2 * pair * BLOCK, (2 * pair + 1) * BLOCK
        out_ref[low : low + BLOCK, :] = packed[:, :128]
        out_ref[high : high + BLOCK, :] = packed[:, 128:]


def stage_rows(j, rows, staged_ref):
    for group in range(N_SHARD):
        for c in range(CHUNKS):
            start = c * 2 * GROUP + j * GROUP
            staged_ref[group, start : start + GROUP, :] = rows[
                group * GROUP : (group + 1) * GROUP, c * 128 : (c + 1) * 128
            ]


def head_mask(h):
    lane = iota((1, 256), 1)
    return ((lane >= h * HDIM) & (lane < (h + 1) * HDIM)).astype(BF16)


def pack_weights(ids, w, out):
    me = ids[1]
    for s in range(N_SHARD):
        place = (s - me) & (N_SHARD - 1)
        for j in range(3):
            piece = w[:, j * D + s * 192 : j * D + s * 192 + 192]
            out[place, :, j * 256 : j * 256 + 256] = jnp.concatenate(
                [piece, jnp.zeros((192, 64), BF16)], 1
            )


def join_weights(ids, p0, p1, p2, p3, out):
    me = ids[1]
    for k, piece in enumerate((p0, p1, p2, p3)):
        out[(me - k) & (N_SHARD - 1)] = piece[...]


def join_small(ids, p0, p1, p2, p3, out, held):
    mine, me = ids[0], ids[1]
    for k, piece in enumerate((p0, p1, p2, p3)):
        for o in range(2):
            section = mine if o == 0 else 1 - mine
            held[section, (me - k) & (N_SHARD - 1)] = piece[o]
    out[...] = jnp.zeros(out.shape, BF16)
    for section in range(2):
        for a in range(N_SHARD):
            out[section, 64:128, a * 192 : (a + 1) * 192] = held[section, a]


def first_norm(section, ids, h, small, out):
    unit, _ = norm_parts(h[...])
    out[...] = (unit * small[section, 96:97, :].astype(F32)).astype(BF16)


def attention(section, ids, x0, x1, x2, x3, own_w, other_w, own_a, other_a, o0, o1, o2, o3, kept, projected, w, a, sems):
    mine = ids[0] == section
    fetch(mine, own_w, other_w, w, sems.at[0])
    fetch(mine, own_a, other_a, a, sems.at[1])
    x = jnp.concatenate([x0[...], x1[...], x2[...], x3[...]], 0)
    kept[:, :D] = x
    arrive(own_w, w, sems.at[0])
    whole = dot(x, w[...].reshape(D, D)).astype(BF16)
    projected[...] = whole
    query, key, value = whole[:, :256], whole[:, 256:512], whole[:, 512:]
    attended = None
    for h in range(HEADS_OWN):
        mask = head_mask(h)
        scores = dot_nt(query * mask, key) * SCALE
        raised = jnp.exp(scores - jnp.max(scores, -1, keepdims=True))
        probs = (raised / jnp.sum(raised, -1, keepdims=True)).astype(BF16)
        part = dot(probs, value * mask)
        attended = part if attended is None else attended + part
    attended = attended.astype(BF16)
    kept[:, D:] = attended
    arrive(own_a, a, sems.at[1])
    result = dot(attended[:, :192], a[...]).astype(BF16)
    for k, out in enumerate((o0, o1, o2, o3)):
        out[...] = result[k * T : (k + 1) * T, :]


def dispatch(section, ids, h, o0, o1, o2, o3, small, route_row, route_column, out, middle_out, normed_out, gates_out):
    middle = h[...] + (
        (o0[...].astype(F32) + o1[...].astype(F32)) + (o2[...].astype(F32) + o3[...].astype(F32))
    )
    middle_out[...] = middle
    unit, _ = norm_parts(middle)
    normed = (unit * small[section, 97:98, :].astype(F32)).astype(BF16)
    normed_out[...] = normed
    packed = to_packed(slots_in_row(route_row[...]), jnp.concatenate([normed, normed], 0))
    send_to_holders(packed, out)
    logits = dot_nt(normed, small[section])
    logits = jnp.concatenate([logits, logits], 0)
    named = iota((2 * T, 128), 1) == route_column[...] + 64
    chosen = jnp.sum(jnp.where(named, logits, 0.0), 1, keepdims=True)
    one, two = chosen[:T], chosen[T:]
    top = jnp.maximum(one, two)
    one, two = jnp.exp(one - top), jnp.exp(two - top)
    total = one + two
    gates_out[0] = jnp.broadcast_to(one / total, (T, 128))
    gates_out[1] = jnp.broadcast_to(two / total, (T, 128))


def expert_forward(section, ids, arrived, order, back_order, own_in, other_in, own_out, other_out, out, kept, slope, w_in, w_out, staged, sems):
    mine = ids[0] == section
    for j in range(2):
        fetch(mine, own_in.at[j], other_in.at[j], w_in.at[j], sems.at[0, j])
        fetch(mine, own_out.at[j], other_out.at[j], w_out.at[j], sems.at[1, j])

    def store(j, group, c, rows):
        kept[0, j, group * GROUP : (group + 1) * GROUP, c * 128 : (c + 1) * 128] = rows

    order_rows(order[...], arrived, store)
    for j in range(2):
        arrive(own_in.at[j], w_in.at[j], sems.at[0, j])
        up = dot(kept[0, j], w_in[j])
        share = 0.5 * (1.0 + lax.erf(up * math.sqrt(0.5)))
        hidden = (up * share).astype(BF16)
        kept[1, j] = hidden
        slope[j] = (share + up * jnp.exp(-0.5 * up * up) * (1.0 / math.sqrt(2.0 * math.pi))).astype(BF16)
        arrive(own_out.at[j], w_out.at[j], sems.at[1, j])
        stage_rows(j, dot(hidden, w_out[j]).astype(BF16), staged)
    unorder_rows(back_order[...], staged, out)


def combined(returned, gates, route_column, taken, middle):
    rows = from_packed(slots_in_column(route_column[...]), sum_of_holders(returned))
    taken[...] = rows.astype(BF16)
    return middle[...] + gates[0][:, :1] * rows[:T] + gates[1][:, :1] * rows[T:]


def combine_next(ids, returned, gates, route_column, middle, small, result, taken, h, normed):
    value = combined(returned, gates, route_column, taken, middle)
    result[...] = value
    rounded = value.astype(BF16).astype(F32)
    h[...] = rounded
    unit, _ = norm_parts(rounded)
    normed[...] = (unit * small[1, 96:97, :].astype(F32)).astype(BF16)


def gate_backward(section, grad, gates, taken, route_row, route_column, small, out, grad_logits, part):
    first, second = gates[0][:, :1], gates[1][:, :1]
    rows = jnp.concatenate([(grad * first).astype(BF16), (grad * second).astype(BF16)], 0)
    send_to_holders(to_packed(slots_in_row(route_row[...]), rows), out)
    gate_one = jnp.sum(grad * taken[:T, :].astype(F32), 1, keepdims=True)
    gate_two = jnp.sum(grad * taken[T:, :].astype(F32), 1, keepdims=True)
    mean = first * gate_one + second * gate_two
    lanes = iota((T, 128), 1) - 64
    column = route_column[...]
    logits = jnp.where(lanes == column[:T], first * (gate_one - mean), 0.0) + jnp.where(
        lanes == column[T:], second * (gate_two - mean), 0.0
    )
    upper, lower = split_pair(logits)
    grad_logits[0] = upper
    grad_logits[1] = lower
    part[...] = dot(upper, small[section]) + dot(lower, small[section])


def start_backward(section, ids, grad, gates, taken, route_row, route_column, small, out, grad_logits, part):
    gate_backward(section, grad[...], gates, taken, route_row, route_column, small, out, grad_logits, part)


def expert_backward(section, ids, arrived, order, back_order, slope, own_in, other_in, own_out, other_out, out, kept, w_in, w_out, staged, sems):
    mine = ids[0] == section
    for j in range(2):
        fetch(mine, own_out.at[j], other_out.at[j], w_out.at[j], sems.at[1, j])
        fetch(mine, own_in.at[j], other_in.at[j], w_in.at[j], sems.at[0, j])

    def store(j, group, c, rows):
        kept[0, j, group * GROUP : (group + 1) * GROUP, c * 128 : (c + 1) * 128] = rows

    order_rows(order[...], arrived, store)
    for j in range(2):
        arrive(own_out.at[j], w_out.at[j], sems.at[1, j])
        grad_up = (dot_nt(kept[0, j], w_out[j]) * slope[j].astype(F32)).astype(BF16)
        kept[1, j] = grad_up
        arrive(own_in.at[j], w_in.at[j], sems.at[0, j])
        stage_rows(j, dot_nt(grad_up, w_in[j]).astype(BF16), staged)
    unorder_rows(back_order[...], staged, out)


def middle_backward(section, ids, returned, route_column, grad, part, middle, normed, grad_logits, small, grad_middle, sent, routed):
    rows = from_packed(slots_in_column(route_column[...]), sum_of_holders(returned))
    grad_normed = part[...] + rows[:T] + rows[T:]
    unit, inverse = norm_parts(middle[...])
    value = grad[...] + norm_back(grad_normed, small[section, 97:98, :].astype(F32), unit, inverse)
    grad_middle[...] = value
    sent[...] = value.astype(BF16)
    upper, lower = split_pair(jnp.sum(grad_normed * unit, 0, keepdims=True))
    routed[:T, :D] = normed[...]
    routed[:T, D : D + 128] = grad_logits[0]
    routed[:T, D + 128 :] = grad_logits[1]
    place = iota((16, D), 0)
    routed[T:, :D] = jnp.where(place == 0, upper, jnp.where(place == 1, lower, 0.0)).astype(BF16)
    named = (iota((16, 128), 1) == 97) & (iota((16, 128), 0) < 2)
    routed[T:, D : D + 128] = jnp.where(named, 1.0, 0.0).astype(BF16)
    routed[T:, D + 128 :] = jnp.zeros((16, 128), BF16)


def attention_backward(section, ids, g0, g1, g2, g3, kept, projected, small, own_w, other_w, own_a, other_a, n0, n1, n2, n3, packed, w, a, sems):
    mine = ids[0] == section
    fetch(mine, own_w, other_w, w, sems.at[0])
    fetch(mine, own_a, other_a, a.at[pl.ds(0, 192), :], sems.at[1])
    a[192:, :] = jnp.zeros((64, D), BF16)
    grad = jnp.concatenate([g0[...], g1[...], g2[...], g3[...]], 0)
    packed[:256, D:] = grad
    arrive(own_a, a.at[pl.ds(0, 192), :], sems.at[1])
    grad_attended = dot_nt(grad, a[...]).astype(BF16)
    query, key, value = projected[:, :256], projected[:, 256:512], projected[:, 512:]
    grad_query, grad_key, grad_value = None, None, None
    for h in range(HEADS_OWN):
        mask = head_mask(h)
        query_part, grad_part = query * mask, grad_attended * mask
        scores = dot_nt(query_part, key) * SCALE
        raised = jnp.exp(scores - jnp.max(scores, -1, keepdims=True))
        probs = raised / jnp.sum(raised, -1, keepdims=True)
        grad_probs = dot_nt(grad_part, value)
        grad_scores = probs * (grad_probs - jnp.sum(grad_probs * probs, -1, keepdims=True))
        grad_scores = grad_scores.astype(BF16)
        parts = (
            dot(grad_scores, key * mask),
            dot_tn(grad_scores, query_part),
            dot_tn(probs.astype(BF16), grad_part),
        )
        if h == 0:
            grad_query, grad_key, grad_value = parts
        else:
            grad_query, grad_key, grad_value = (
                grad_query + parts[0],
                grad_key + parts[1],
                grad_value + parts[2],
            )
    grad_projected = jnp.concatenate([grad_query * SCALE, grad_key * SCALE, grad_value], 1).astype(BF16)
    packed[:256, :D] = grad_projected
    arrive(own_w, w, sems.at[0])
    grad_normed = dot_nt(grad_projected, w[...].reshape(D, D))
    gain = jnp.sum(grad_normed * kept[:, :D].astype(F32), 0, keepdims=True)
    upper, lower = split_pair(gain / small[section, 96:97, :].astype(F32))
    place = iota((16, D), 0)
    packed[256:, :D] = jnp.where(place == 0, upper, jnp.where(place == 1, lower, 0.0)).astype(BF16)
    named = (iota((16, D), 1) == 96) & (iota((16, D), 0) < 2)
    packed[256:, D:] = jnp.where(named, 1.0, 0.0).astype(BF16)
    result = grad_normed.astype(BF16)
    for k, out in enumerate((n0, n1, n2, n3)):
        out[...] = result[k * T : (k + 1) * T, :]


def input_grad(section, n0, n1, n2, n3, h, grad_middle, small):
    grad_normed = (n0[...].astype(F32) + n1[...].astype(F32)) + (n2[...].astype(F32) + n3[...].astype(F32))
    unit, inverse = norm_parts(h[...])
    return grad_middle[...] + norm_back(grad_normed, small[section, 96:97, :].astype(F32), unit, inverse)


def input_backward_next(ids, n0, n1, n2, n3, h, grad_middle, small, gates, taken, route_row, route_column, grad_out, out, grad_logits, part):
    grad = input_grad(1, n0, n1, n2, n3, h, grad_middle, small).astype(BF16).astype(F32)
    grad_out[...] = grad
    gate_backward(0, grad, gates, taken, route_row, route_column, small, out, grad_logits, part)


def input_backward_last(ids, n0, n1, n2, n3, h, grad_middle, small, grad_out):
    grad_out[...] = input_grad(0, n0, n1, n2, n3, h, grad_middle, small)


def expert_weight_grads(ids, f0, f1, rf0, rf1, b0, b1, rb0, rb1, grad_in, grad_out, fwd, bwd, sems):
    j = pl.program_id(0)
    mine = ids[0] == 0
    fetch(mine, f0.at[:, j], f1.at[:, j], fwd.at[0], sems.at[0])
    fetch(mine, rf0.at[:, j], rf1.at[:, j], fwd.at[1], sems.at[1])
    fetch(mine, b0.at[:, j], b1.at[:, j], bwd.at[0], sems.at[2])
    fetch(mine, rb0.at[:, j], rb1.at[:, j], bwd.at[1], sems.at[3])
    arrive(f0.at[:, j], fwd.at[0], sems.at[0])
    arrive(rf0.at[:, j], fwd.at[1], sems.at[1])
    arrive(b0.at[:, j], bwd.at[0], sems.at[2])
    arrive(rb0.at[:, j], bwd.at[1], sems.at[3])
    grad_in[0] = dot_tn(fwd[0, 0], bwd[0, 1]) + dot_tn(fwd[1, 0], bwd[1, 1])
    grad_out[0] = dot_tn(fwd[0, 1], bwd[0, 0]) + dot_tn(fwd[1, 1], bwd[1, 0])


def shared_weight_grads(ids, k0, k1, rk0, rk1, p0, p1, rp0, rp1, r0, r1, rr0, rr1, out, kept, packed, routed, sems):
    mine = ids[0] == 0
    copies = (
        (k0, k1, kept.at[0]),
        (rk0, rk1, kept.at[1]),
        (p0, p1, packed.at[0]),
        (rp0, rp1, packed.at[1]),
        (r0, r1, routed.at[0]),
        (rr0, rr1, routed.at[1]),
    )
    for n, (own, other, target) in enumerate(copies):
        fetch(mine, own, other, target, sems.at[n])
    for n, (own, other, target) in enumerate(copies):
        arrive(own, target, sems.at[n])
    grad_qkv = dot_tn(kept[0, :, :D], packed[0, :256, :D]) + dot_tn(kept[1, :, :D], packed[1, :256, :D])
    grad_attn = dot_tn(kept[0, :, D:], packed[0, :256, D:]) + dot_tn(kept[1, :, D:], packed[1, :256, D:])
    extra = None
    for m in range(2):
        rows = routed[m, :, :D]
        part = (
            dot_tn(rows, routed[m, :, D : D + 128])
            + dot_tn(rows, routed[m, :, D + 128 :])
            + dot_tn(packed[m, 256:, :D], packed[m, 256:, D : D + 128])
        )
        extra = part if extra is None else extra + part
    middle = grad_qkv[:, 128:256] + extra
    out[:, :48, :128] = grad_qkv[:, :128].astype(BF16).reshape(N_EXPERT, 48, 128)
    out[:, :48, 128:256] = middle.astype(BF16).reshape(N_EXPERT, 48, 128)
    out[:, :48, 256:] = grad_qkv[:, 256:].astype(BF16).reshape(N_EXPERT, 48, 512)
    row, column = iota((256, 256), 0), iota((256, 256), 1)
    spread = ((row & 15) < 12) & (column == (row >> 4) * 12 + (row & 15))
    spread = jnp.where(spread, 1.0, 0.0).astype(BF16)
    out[:, 48:, :] = dot(spread, grad_attn.astype(BF16)).astype(BF16).reshape(N_EXPERT, 16, D)


def sum_shared(ids, arrived, out, attn, total):
    me = ids[1]
    summed = arrived[0].astype(F32)
    for n in range(1, N_EXPERT):
        summed = summed + arrived[n].astype(F32)
    total[...] = summed
    for s in range(N_SHARD):
        out[(s - me) & (N_SHARD - 1), :12, :] = total[s * 12 : s * 12 + 12, :]
    attn[...] = total[48:, :]


def place_shared(ids, q0, q1, q2, q3, qkv, extra, held):
    me = ids[1]
    for k, piece in enumerate((q0, q1, q2, q3)):
        held[(me - k) & (N_SHARD - 1)] = piece[...]
    total = None
    for a in range(N_SHARD):
        for j in range(3):
            qkv[:, j * D + a * 192 : j * D + a * 192 + 192] = held[a, :12, j * 256 : j * 256 + 192]
        part = held[a, :12, 128:256]
        total = part if total is None else total + part
    extra[...] = total


def along(value, axis, by):
    count = lax.axis_size(axis)
    return lax.ppermute(value, axis, [(i, (i + by) % count) for i in range(count)])


def gather_shards(value):
    return [value] + [along(value, "shard", k) for k in range(1, N_SHARD)]


def return_shards(pieces):
    return [pieces[0]] + [along(pieces[k], "shard", -k) for k in range(1, N_SHARD)]


def exchange(value):
    return lax.all_to_all(value, ("expert", "shard"), 0, 0, tiled=True)


def swap(value):
    return lax.ppermute(value, "section", [(0, 1), (1, 0)])


def up(value):
    return lax.ppermute(value, "section", [(0, 1)])


def down(value):
    return lax.ppermute(value, "section", [(1, 0)])


def dma(*shape):
    return pltpu.SemaphoreType.DMA(shape)


def local(inputs, cotangent, w_qkv, w_attn, gain_one, gain_two, router, w_in, w_out, routes):
    section = lax.axis_index("section")
    me = lax.axis_index("shard")
    first = section == 0
    ids = jnp.stack([section, me]).astype(jnp.int32)

    thin = jnp.concatenate(
        [router[0].T, gain_one, gain_two, jnp.zeros((30, router.shape[1]), BF16)], 0
    )
    thin = jnp.stack([thin, swap(thin)])
    small = call(
        join_small,
        [((2, 128, D), BF16)],
        [ids, *gather_shards(thin)],
        [pltpu.VMEM((2, N_SHARD, 64, 192), BF16)],
    )[0]
    pieces = call(pack_weights, [((N_SHARD, 192, D), BF16)], [ids, w_qkv[0]])[0]
    own_w = call(
        join_weights,
        [((N_SHARD, 192, D), BF16)],
        [ids, pieces[0], *[along(pieces[k], "shard", k) for k in range(1, N_SHARD)]],
    )[0]
    other_w = swap(own_w)
    own_a = w_attn[0]
    other_a = swap(own_a)
    own_in, own_out = w_in[0], w_out[0]
    other_in, other_out = swap(own_in), swap(own_out)
    weights = (own_w, other_w, own_a, other_a)
    experts = (own_in, other_in, own_out, other_out)

    local_routes = routes[0, :, 0, 0]
    own_routes = lax.dynamic_index_in_dim(local_routes, section, 0, False)
    other_routes = swap(lax.dynamic_index_in_dim(local_routes, 1 - section, 0, False))
    flat = [
        jnp.where(first, own_routes, other_routes).T.reshape(1, 2 * T),
        jnp.where(first, other_routes, own_routes).T.reshape(1, 2 * T),
    ]
    columns = [value.reshape(2 * T, 1) for value in flat]

    place = jnp.arange(ORDERED, dtype=jnp.int32)
    within = place % (2 * GROUP)
    source = (
        ((within % GROUP) // CAP) * SIDE
        + (place // (2 * GROUP)) * ROWS
        + (within // GROUP) * CAP
        + within % CAP
    )
    order = (source[:, None] == jnp.arange(BLOCK, dtype=jnp.int32)[None, :]).astype(BF16)
    back_order = (source[None, :] == jnp.arange(BLOCK, dtype=jnp.int32)[:, None]).astype(BF16)

    packed_shape = ((N_EXPERT, N_SHARD, SIDE, 128), BF16)
    rows_shape = ((T, D), BF16)
    wide_shape = ((T, D), F32)
    flat_shape = ((N_ALL * SIDE, 128), BF16)
    per_expert = N_SHARD * GROUP

    def crossed(value):
        return exchange(value.reshape(N_ALL, SIDE, 128))

    def forward_part(s, h, normed):
        o0, o1, o2, o3, kept, projected = call(
            functools.partial(attention, s),
            [rows_shape] * 4 + [((256, D + 256), BF16), ((256, D), BF16)],
            [ids, *gather_shards(normed), *weights],
            [pltpu.VMEM((N_SHARD, 192, D), BF16), pltpu.VMEM((192, D), BF16), dma(2)],
            anywhere=(5, 6, 7, 8),
        )
        sent, middle, normed_b, gates = call(
            functools.partial(dispatch, s),
            [packed_shape, wide_shape, rows_shape, ((2, T, 128), F32)],
            [ids, h, *return_shards([o0, o1, o2, o3]), small, flat[s], columns[s]],
        )
        arrived = crossed(sent).reshape(N_ALL * SIDE, 128)
        sent, expert_kept, slope = call(
            functools.partial(expert_forward, s),
            [flat_shape, ((2, 2, per_expert, D), BF16), ((2, per_expert, D), BF16)],
            [ids, arrived, order, back_order, *experts],
            [
                pltpu.VMEM((2, D, D), BF16),
                pltpu.VMEM((2, D, D), BF16),
                pltpu.VMEM((N_SHARD, ORDERED, 128), BF16),
                dma(2, 2),
            ],
            anywhere=(4, 5, 6, 7),
        )
        returned = crossed(sent).reshape(N_EXPERT, N_SHARD, SIDE, 128)
        return returned, (kept, projected, middle, normed_b, gates, expert_kept, slope)

    def backward_part(s, grad, arrived, part, grad_logits, h, state):
        kept, projected, middle, normed_b, gates, expert_kept, slope = state
        sent, expert_grads = call(
            functools.partial(expert_backward, s),
            [flat_shape, ((2, 2, per_expert, D), BF16)],
            [ids, arrived.reshape(N_ALL * SIDE, 128), order, back_order, slope, *experts],
            [
                pltpu.VMEM((2, D, D), BF16),
                pltpu.VMEM((2, D, D), BF16),
                pltpu.VMEM((N_SHARD, ORDERED, 128), BF16),
                dma(2, 2),
            ],
            anywhere=(5, 6, 7, 8),
        )
        returned = crossed(sent).reshape(N_EXPERT, N_SHARD, SIDE, 128)
        grad_middle, sent, routed = call(
            functools.partial(middle_backward, s),
            [wide_shape, rows_shape, ((T + 16, D + 256), BF16)],
            [ids, returned, columns[s], grad, part, middle, normed_b, grad_logits, small],
        )
        n0, n1, n2, n3, packed = call(
            functools.partial(attention_backward, s),
            [rows_shape] * 4 + [((256 + 16, 2 * D), BF16)],
            [ids, *gather_shards(sent), kept, projected, small, *weights],
            [pltpu.VMEM((N_SHARD, 192, D), BF16), pltpu.VMEM((256, D), BF16), dma(2)],
            anywhere=(8, 9, 10, 11),
        )
        return return_shards([n0, n1, n2, n3]), grad_middle, expert_grads, routed, packed

    h_one = lax.dynamic_index_in_dim(inputs, section, 0, False).reshape(T, D)
    normed = call(functools.partial(first_norm, 0), [rows_shape], [ids, h_one, small])[0]
    returned, state_one = forward_part(0, h_one, normed)
    result_one, taken_one, h_two, normed = call(
        combine_next,
        [wide_shape, ((2 * T, D), BF16), wide_shape, rows_shape],
        [ids, returned, state_one[4], columns[0], state_one[2], small],
    )
    returned, state_two = forward_part(1, h_two, normed)
    result_two, taken_two = call(
        combine_last,
        [wide_shape, ((2 * T, D), BF16)],
        [ids, returned, state_two[4], columns[1], state_two[2]],
    )

    logits_shape = ((2, T, 128), BF16)
    seed = lax.dynamic_index_in_dim(cotangent, section, 0, False).reshape(T, D)
    sent, grad_logits, part = call(
        functools.partial(start_backward, 1),
        [packed_shape, logits_shape, wide_shape],
        [ids, seed, state_two[4], taken_two, flat[1], columns[1], small],
    )
    pieces, grad_middle, expert_grads_two, routed_two, packed_two = backward_part(
        1, seed, crossed(sent), part, grad_logits, h_two, state_two
    )
    grad_two, sent, grad_logits, part = call(
        input_backward_next,
        [wide_shape, packed_shape, logits_shape, wide_shape],
        [ids, *pieces, h_two, grad_middle, small, state_one[4], taken_one, flat[0], columns[0]],
    )
    pieces, grad_middle, expert_grads_one, routed_one, packed_one = backward_part(
        0, grad_two, crossed(sent), part, grad_logits, h_one, state_one
    )

    payload = call(
        shared_weight_grads,
        [((N_EXPERT, 64, D), BF16)],
        [
            ids,
            state_one[0], state_two[0], down(state_one[0]), up(state_two[0]),
            packed_one, packed_two, down(packed_one), up(packed_two),
            routed_one, routed_two, down(routed_one), up(routed_two),
        ],
        [
            pltpu.VMEM((2, 256, D + 256), BF16),
            pltpu.VMEM((2, 256 + 16, 2 * D), BF16),
            pltpu.VMEM((2, T + 16, D + 256), BF16),
            dma(6),
        ],
        anywhere=tuple(range(1, 13)),
    )[0]
    summed = lax.all_to_all(payload, "expert", 0, 0, tiled=True)
    shares, attn = call(
        sum_shared,
        [((N_SHARD, 16, D), F32), ((16, D), F32)],
        [ids, summed],
        [pltpu.VMEM((64, D), F32)],
    )
    grad_qkv, extra = call(
        place_shared,
        [((12, 3 * D), F32), ((12, 128), F32)],
        [ids, shares[0], *[along(shares[k], "shard", k) for k in range(1, N_SHARD)]],
        [pltpu.VMEM((N_SHARD, 16, D), F32)],
    )
    pairs = [
        (e * N_SHARD + s, (N_SHARD * s + e // N_SHARD) * N_SHARD + e % N_SHARD)
        for e in range(N_EXPERT)
        for s in range(N_SHARD)
    ]
    grad_attn = lax.ppermute(attn, ("expert", "shard"), pairs)[:12]

    grad_one = call(
        input_backward_last, [wide_shape], [ids, *pieces, h_one, grad_middle, small]
    )[0]
    block = pl.BlockSpec(memory_space=pl.ANY)
    half = pl.BlockSpec((1, D, D), lambda j: (j, 0, 0))
    grad_in, grad_out = pl.pallas_call(
        expert_weight_grads,
        grid=(2,),
        out_shape=(jax.ShapeDtypeStruct((2, D, D), F32), jax.ShapeDtypeStruct((2, D, D), F32)),
        in_specs=[pl.BlockSpec(memory_space=pltpu.SMEM)] + [block] * 8,
        out_specs=(half, half),
        scratch_shapes=[
            pltpu.VMEM((2, 2, per_expert, D), BF16),
            pltpu.VMEM((2, 2, per_expert, D), BF16),
            dma(4),
        ],
        compiler_params=pltpu.CompilerParams(vmem_limit_bytes=48 * 1024 * 1024),
    )(
        ids,
        state_one[5], state_two[5], down(state_one[5]), up(state_two[5]),
        expert_grads_one, expert_grads_two, down(expert_grads_one), up(expert_grads_two),
    )

    def by_micro(one, two):
        return jnp.where(first, jnp.stack([one, down(one)]), jnp.stack([up(two), two])).reshape(
            1, 2, 1, T, D
        )

    return (
        by_micro(result_one, result_two),
        by_micro(grad_one, grad_two),
        grad_qkv[None],
        grad_attn[None],
        extra[:, 96][None],
        extra[:, 97][None],
        extra[:, 64:96][None],
        grad_in[None],
        grad_out[None],
    )


def combine_last(ids, returned, gates, route_column, middle, result, taken):
    result[...] = combined(returned, gates, route_column, taken, middle)


def solution(mesh):
    return jax.shard_map(
        local,
        mesh=mesh,
        in_specs=(
            P(None, "expert", "shard", None),
            P(None, "expert", "shard", None),
            P("section", "shard", None),
            P("section", "shard", None),
            P("section", "shard"),
            P("section", "shard"),
            P("section", "shard", None),
            P("section", "expert", None, "shard"),
            P("section", "expert", "shard", None),
            P("section", None, "expert", "shard", None, None),
        ),
        out_specs=(
            P("section", None, "expert", "shard", None),
            P("section", None, "expert", "shard", None),
            P("section", ("expert", "shard"), None),
            P("section", ("expert", "shard"), None),
            P("section", ("expert", "shard")),
            P("section", ("expert", "shard")),
            P("section", ("expert", "shard"), None),
            P("section", "expert", None, "shard"),
            P("section", "expert", "shard", None),
        ),
        check_vma=False,
    )
```

```python
import functools
import math

import jax
import jax.numpy as jnp
from jax import lax
from jax.experimental import pallas as pl
from jax.experimental.pallas import tpu as pltpu
from jax.sharding import PartitionSpec as P

F32 = jnp.float32
BF16 = jnp.bfloat16
D = 768
HEADS_OWN = 3
HDIM = 64
T = 64
CAP = 5
CHUNKS = 6
ROWS = 2 * CAP
N_EXPERT = 16
N_SHARD = 4
N_ALL = N_EXPERT * N_SHARD
SIDE = 64
BLOCK = N_EXPERT * SIDE
GROUP = N_EXPERT * CAP
ORDERED = CHUNKS * 2 * GROUP
META = 128
EPS = 1e-06
SCALE = 1.0 / math.sqrt(HDIM)


def dot(a, b):
    return lax.dot_general(a, b, (((1,), (0,)), ((), ())), preferred_element_type=F32)


def dot_nt(a, b):
    return lax.dot_general(a, b, (((1,), (1,)), ((), ())), preferred_element_type=F32)


def dot_tn(a, b):
    return lax.dot_general(a, b, (((0,), (0,)), ((), ())), preferred_element_type=F32)


def iota(shape, dim):
    return lax.broadcasted_iota(jnp.int32, shape, dim)


def call(body, outs, ins, scratch=(), anywhere=(), scalars=1, mib=12, outs_anywhere=()):
    specs = []
    for place in range(len(ins)):
        if place < scalars:
            specs.append(pl.BlockSpec(memory_space=pltpu.SMEM))
        elif place in anywhere:
            specs.append(pl.BlockSpec(memory_space=pltpu.HBM))
        else:
            specs.append(pl.BlockSpec(memory_space=pltpu.VMEM))
    return pl.pallas_call(
        body,
        out_shape=tuple(jax.ShapeDtypeStruct(shape, kind) for shape, kind in outs),
        in_specs=specs,
        out_specs=tuple(
            pl.BlockSpec(memory_space=pltpu.HBM if place in outs_anywhere else pltpu.VMEM)
            for place in range(len(outs))
        ),
        scratch_shapes=list(scratch),
        compiler_params=pltpu.CompilerParams(vmem_limit_bytes=mib * 1024 * 1024),
    )(*ins)


def fetch(mine, own, other, target, sem):
    @pl.when(mine)
    def _():
        pltpu.make_async_copy(own, target, sem).start()

    @pl.when(jnp.logical_not(mine))
    def _():
        pltpu.make_async_copy(other, target, sem).start()


def arrive(own, target, sem):
    pltpu.make_async_copy(own, target, sem).wait()


def move(source, target, sem):
    pltpu.make_async_copy(source, target, sem).start()


def norm_parts(rows):
    centered = rows - jnp.mean(rows, -1, keepdims=True)
    inverse = lax.rsqrt(jnp.mean(centered * centered, -1, keepdims=True) + EPS)
    return centered * inverse, inverse


def norm_back(grad, gain, unit, inverse):
    scaled = grad * gain
    return inverse * (
        scaled
        - jnp.mean(scaled, -1, keepdims=True)
        - unit * jnp.mean(scaled * unit, -1, keepdims=True)
    )


def split_pair(values):
    upper = values.astype(BF16)
    return upper, (values - upper.astype(F32)).astype(BF16)


def row_of(column):
    size = column.shape[0]
    diagonal = iota((size, size), 0) == iota((size, size), 1)
    return jnp.sum(jnp.where(diagonal, column, 0.0), 0, keepdims=True)


def slots_of(route_column):
    named = (iota((2 * T, 32), 1) == route_column).astype(F32)
    earlier = ((iota((2 * T, 2 * T), 1) & (T - 1)) < (iota((2 * T, 2 * T), 0) & (T - 1))).astype(BF16)
    before = dot(earlier, named.astype(BF16))
    return route_column.astype(F32) * CAP + jnp.sum(before * named, 1, keepdims=True)


def packed_place(index):
    within = index & (SIDE - 1)
    chunk = (within * 205) >> 11
    return (index >> 6) * ROWS + within - chunk * ROWS, chunk


def to_packed(slot_row, rows):
    slot, chunk = packed_place(iota((BLOCK, 2 * T), 0))
    hit = slot.astype(F32) == slot_row
    total = None
    for c in range(CHUNKS):
        mask = jnp.where(hit & (chunk == c), 1.0, 0.0).astype(BF16)
        part = dot(mask, rows[:, c * 128 : (c + 1) * 128])
        total = part if total is None else total + part
    return total.astype(BF16)


def from_packed(slot_column, packed):
    slot, chunk = packed_place(iota((2 * T, BLOCK), 1))
    hit = slot.astype(F32) == slot_column
    parts = []
    for c in range(CHUNKS):
        mask = jnp.where(hit & (chunk == c), 1.0, 0.0).astype(BF16)
        parts.append(dot(mask, packed))
    return jnp.concatenate(parts, 1)


def send_to_holders(packed, out_ref, start):
    blocks = packed.reshape(N_EXPERT, SIDE, 128)
    for s in range(N_SHARD):
        out_ref[:, s, start : start + SIDE, :] = blocks


def sum_of_holders(in_ref, start):
    total = in_ref[:, 0, start : start + SIDE, :].astype(F32)
    for s in range(1, N_SHARD):
        total = total + in_ref[:, s, start : start + SIDE, :].astype(F32)
    return total.astype(BF16).reshape(BLOCK, 128)


def group_of(packed_ref, group, start):
    rows = packed_ref[group * N_EXPERT : (group + 1) * N_EXPERT, start : start + SIDE, :]
    return rows.reshape(BLOCK, 128)


def order_pair(order, first, second):
    return dot(order, jnp.concatenate([first, second], 1)).astype(BF16)


def place_rows(ordered, half, group, kept_ref):
    for c in range(CHUNKS):
        for j in range(2):
            start = c * 2 * GROUP + j * GROUP
            kept_ref[j, group * GROUP : (group + 1) * GROUP, c * 128 : (c + 1) * 128] = ordered[
                start : start + GROUP, half * 128 : half * 128 + 128
            ]


def stage_rows(j, rows, staged_ref):
    for group in range(N_SHARD):
        for c in range(CHUNKS):
            start = c * 2 * GROUP + j * GROUP
            staged_ref[group, start : start + GROUP, :] = rows[
                group * GROUP : (group + 1) * GROUP, c * 128 : (c + 1) * 128
            ]


def unorder_pair(back_order, first, second, out_ref, places):
    packed = dot(back_order, jnp.concatenate([first, second], 1)).astype(BF16)
    for half, (group, start) in enumerate(places):
        out_ref[group * N_EXPERT : (group + 1) * N_EXPERT, start : start + SIDE, :] = packed[
            :, half * 128 : half * 128 + 128
        ].reshape(N_EXPERT, SIDE, 128)


def head_mask(h):
    lane = iota((1, 256), 1)
    return ((lane >= h * HDIM) & (lane < (h + 1) * HDIM)).astype(BF16)


def fold(value):
    half = value.shape[0] // 2
    return jnp.concatenate([value[:half, :], value[half:, :]], 1)


def unfold(value):
    return jnp.concatenate([value[:, :64], value[:, 64:]], 0)


def begin(ids, inputs, w, gain_one, gain_two, router, p0, p1, p2, p3, h, held, thin_one, thin_two, sems):
    mine, me = ids[0], ids[1]
    move(inputs.at[mine, 0], h, sems.at[0])
    for j in range(3):
        move(w.at[:, pl.ds(j * D, D)], held.at[j], sems.at[1 + j])
    move(gain_one, thin_one, sems.at[4])
    move(gain_two, thin_two, sems.at[5])
    arrive(gain_one, thin_one, sems.at[4])
    arrive(gain_two, thin_two, sems.at[5])
    rows = iota((32, 192), 0)
    gains = jnp.where(rows == 0, thin_one[...].astype(F32), jnp.where(rows == 1, thin_two[...].astype(F32), 0.0))
    thin = jnp.concatenate([router[...], gains.astype(BF16)], 0)
    arrive(inputs.at[mine, 0], h, sems.at[0])
    unit, _ = norm_parts(h[...])
    unit = unit.astype(BF16)
    for j in range(3):
        arrive(w.at[:, pl.ds(j * D, D)], held.at[j], sems.at[1 + j])
    for piece in (p0, p1, p2, p3):
        piece[864:928, :] = thin[:, :128]
        piece[928:960, :] = fold(thin[:, 128:])
        for c in range(CHUNKS):
            piece[960 + 64 * c : 1024 + 64 * c, :] = unit[:, c * 128 : (c + 1) * 128]
    for s in range(N_SHARD):
        for k, piece in enumerate((p0, p1, p2, p3)):

            @pl.when(((s - me) & (N_SHARD - 1)) == k)
            def _(s=s, piece=piece):
                parts = [held[j, :, s * 192 : s * 192 + 192] for j in range(3)]
                for j in range(3):
                    piece[192 * j : 192 * j + 192, :] = parts[j][:, :128]
                piece[576:768, :] = jnp.concatenate([parts[0][:, 128:], parts[1][:, 128:]], 1)
                piece[768:864, :] = fold(parts[2][:, 128:])


def join(ids, p0, p1, p2, p3, out, units, held):
    me = ids[1]
    none = jnp.zeros((192, 64), BF16)
    for k, piece in enumerate((p0, p1, p2, p3)):
        place = (me - k) & (N_SHARD - 1)
        rest = piece[576:768, :]
        rests = (rest[:, :64], rest[:, 64:], unfold(piece[768:864, :]))
        for j in range(3):
            out[place, :, 256 * j : 256 * j + 128] = piece[192 * j : 192 * j + 192, :]
            out[place, :, 256 * j + 128 : 256 * j + 256] = jnp.concatenate([rests[j], none], 1)
        held[place, :, :128] = piece[864:928, :]
        held[place, :, 128:] = jnp.concatenate([unfold(piece[928:960, :]), none[:64]], 1)
        for c in range(CHUNKS):
            units[k * T : (k + 1) * T, c * 128 : (c + 1) * 128] = piece[960 + 64 * c : 1024 + 64 * c, :]
    out[4] = jnp.zeros((192, D), BF16)
    for a in range(N_SHARD):
        out[4, 64:128, a * 192 : (a + 1) * 192] = held[a, :, :192]


def attend(x, w, a, kept, projected, outs):
    kept[:, :D] = x
    whole = dot(x, w[...].reshape(D, D)).astype(BF16)
    projected[...] = whole
    query, key, value = whole[:, :256], whole[:, 256:512], whole[:, 512:]
    attended = None
    for h in range(HEADS_OWN):
        mask = head_mask(h)
        scores = dot_nt(query * mask, key) * SCALE
        raised = jnp.exp(scores - jnp.max(scores, -1, keepdims=True))
        probs = (raised / jnp.sum(raised, -1, keepdims=True)).astype(BF16)
        part = dot(probs, value * mask)
        attended = part if attended is None else attended + part
    attended = attended.astype(BF16)
    kept[:, D:] = attended
    result = dot(attended[:, :192], a[...]).astype(BF16)
    for k, out in enumerate(outs):
        out[...] = result[k * T : (k + 1) * T, :]


def attention_one(ids, units, own_w, other_w, own_a, other_a, inputs, o0, o1, o2, o3, kept, projected, small, h, w, a, sems):
    mine = ids[0] == 0
    rows, extra = pl.ds(0, 4), pl.ds(0, 128)
    fetch(mine, own_w.at[4, extra], other_w.at[4, extra], small.at[0], sems.at[2])
    fetch(mine, own_w.at[rows], other_w.at[rows], w, sems.at[0])
    fetch(mine, own_a, other_a, a, sems.at[1])
    fetch(mine, other_w.at[4, extra], own_w.at[4, extra], small.at[1], sems.at[3])
    move(inputs.at[ids[0], 0], h, sems.at[4])
    arrive(own_w.at[4, extra], small.at[0], sems.at[2])
    x = (units[...].astype(F32) * small[0, 96:97, :].astype(F32)).astype(BF16)
    arrive(own_w.at[rows], w, sems.at[0])
    arrive(own_a, a, sems.at[1])
    attend(x, w, a, kept, projected, (o0, o1, o2, o3))
    arrive(own_w.at[4, extra], small.at[1], sems.at[3])
    arrive(inputs.at[ids[0], 0], h, sems.at[4])


def attention_two(ids, x0, x1, x2, x3, own_w, other_w, own_a, other_a, o0, o1, o2, o3, kept, projected, w, a, sems):
    mine = ids[0] == 1
    rows = pl.ds(0, 4)
    fetch(mine, own_w.at[rows], other_w.at[rows], w, sems.at[0])
    fetch(mine, own_a, other_a, a, sems.at[1])
    x = jnp.concatenate([x0[...], x1[...], x2[...], x3[...]], 0)
    arrive(own_w.at[rows], w, sems.at[0])
    arrive(own_a, a, sems.at[1])
    attend(x, w, a, kept, projected, (o0, o1, o2, o3))


def dispatch(section, ids, h, o0, o1, o2, o3, small, own_routes, other_routes, *refs):
    if section == 1:
        seed, out, held = refs
        start = h[...].astype(BF16).astype(F32)
    else:
        out, held = refs
        start = h[...]
    middle = start + (
        (o0[...].astype(F32) + o1[...].astype(F32)) + (o2[...].astype(F32) + o3[...].astype(F32))
    )
    held[:T, META:] = middle
    held[T:, META:] = jnp.zeros((T + 8, D), F32)
    unit, _ = norm_parts(middle)
    normed = (unit * small[section, 97:98, :].astype(F32)).astype(BF16)
    route = jnp.where(ids[0] == section, own_routes[ids[0]], other_routes[ids[0]])
    column = jnp.concatenate([route[:, 0:1], route[:, 1:2]], 0)
    slot_column = slots_of(column)
    slot_row = row_of(slot_column)
    send_to_holders(to_packed(slot_row, jnp.concatenate([normed, normed], 0)), out, 0)
    logits = dot_nt(normed, small[section])
    logits = jnp.concatenate([logits, logits], 0)
    lanes = iota((2 * T, 128), 1)
    chosen = jnp.sum(jnp.where(lanes == column + 64, logits, 0.0), 1, keepdims=True)
    one, two = chosen[:T], chosen[T:]
    top = jnp.maximum(one, two)
    one, two = jnp.exp(one - top), jnp.exp(two - top)
    total = one + two
    gates = jnp.concatenate([one / total, two / total], 0)
    held[: 2 * T, :META] = jnp.where(
        lanes == 0, gates, jnp.where(lanes == 1, slot_column, column.astype(F32) + 64.0)
    )
    held[2 * T :, :META] = jnp.broadcast_to(slot_row, (8, META))
    if section == 1:
        grad = seed[ids[0], 0]
        rows = jnp.concatenate([grad, grad], 0) * gates
        send_to_holders(to_packed(slot_row, rows.astype(BF16)), out, SIDE)


def load_experts(section, ids, own_in, other_in, own_out, other_out, w_in, w_out, sems):
    mine = ids[0] == section
    for j in range(2):
        fetch(mine, own_in.at[j], other_in.at[j], w_in.at[j], sems.at[0, j])
        fetch(mine, own_out.at[j], other_out.at[j], w_out.at[j], sems.at[1, j])


def expert_forward(ids, arrived, order, back_order, own_in, other_in, own_out, other_out, out, kept, slope, w_in, w_out, staged, sems):
    load_experts(0, ids, own_in, other_in, own_out, other_out, w_in, w_out, sems)
    for pair in (0, 2):
        ordered = order_pair(order[...], group_of(arrived, pair, 0), group_of(arrived, pair + 1, 0))
        place_rows(ordered, 0, pair, kept.at[0])
        place_rows(ordered, 1, pair + 1, kept.at[0])
    for j in range(2):
        arrive(own_in.at[j], w_in.at[j], sems.at[0, j])
        up = dot(kept[0, j], w_in[j])
        share = 0.5 * (1.0 + lax.erf(up * math.sqrt(0.5)))
        hidden = (up * share).astype(BF16)
        kept[1, j] = hidden
        slope[j] = (share + up * jnp.exp(-0.5 * up * up) * (1.0 / math.sqrt(2.0 * math.pi))).astype(BF16)
        arrive(own_out.at[j], w_out.at[j], sems.at[1, j])
        stage_rows(j, dot(hidden, w_out[j]).astype(BF16), staged)
    for pair in (0, 2):
        unorder_pair(back_order[...], staged[pair], staged[pair + 1], out, ((pair, 0), (pair + 1, 0)))


def expert_both(ids, arrived, order, back_order, own_in, other_in, own_out, other_out, out, kept, w_in, w_out, staged, staged_back, sems):
    load_experts(1, ids, own_in, other_in, own_out, other_out, w_in, w_out, sems)
    for group in range(N_SHARD):
        ordered = order_pair(order[...], group_of(arrived, group, 0), group_of(arrived, group, SIDE))
        place_rows(ordered, 0, group, kept.at[0])
        place_rows(ordered, 1, group, kept.at[2])
    for j in range(2):
        arrive(own_in.at[j], w_in.at[j], sems.at[0, j])
        up = dot(kept[0, j], w_in[j])
        share = 0.5 * (1.0 + lax.erf(up * math.sqrt(0.5)))
        hidden = (up * share).astype(BF16)
        kept[1, j] = hidden
        arrive(own_out.at[j], w_out.at[j], sems.at[1, j])
        slope = share + up * jnp.exp(-0.5 * up * up) * (1.0 / math.sqrt(2.0 * math.pi))
        grad_up = (dot_nt(kept[2, j], w_out[j]) * slope).astype(BF16)
        kept[3, j] = grad_up
        stage_rows(j, dot(hidden, w_out[j]).astype(BF16), staged)
        stage_rows(j, dot_nt(grad_up, w_in[j]).astype(BF16), staged_back)
    for group in range(N_SHARD):
        unorder_pair(back_order[...], staged[group], staged_back[group], out, ((group, 0), (group, SIDE)))


def expert_backward(ids, arrived, order, back_order, slope_in, fwd, own_in, other_in, own_out, other_out, out, kept, w_in, w_out, staged, slope, sems):
    load_experts(0, ids, own_in, other_in, own_out, other_out, w_in, w_out, sems)
    move(slope_in, slope, sems.at[2, 0])
    move(fwd, kept.at[pl.ds(0, 2)], sems.at[2, 1])
    for pair in (0, 2):
        ordered = order_pair(order[...], group_of(arrived, pair, 0), group_of(arrived, pair + 1, 0))
        place_rows(ordered, 0, pair, kept.at[2])
        place_rows(ordered, 1, pair + 1, kept.at[2])
    arrive(slope_in, slope, sems.at[2, 0])
    for j in range(2):
        arrive(own_out.at[j], w_out.at[j], sems.at[1, j])
        grad_up = (dot_nt(kept[2, j], w_out[j]) * slope[j].astype(F32)).astype(BF16)
        kept[3, j] = grad_up
        arrive(own_in.at[j], w_in.at[j], sems.at[0, j])
        stage_rows(j, dot_nt(grad_up, w_in[j]).astype(BF16), staged)
    for pair in (0, 2):
        unorder_pair(back_order[...], staged[pair], staged[pair + 1], out, ((pair, 0), (pair + 1, 0)))
    arrive(fwd, kept.at[pl.ds(0, 2)], sems.at[2, 1])


def mixed(rows, held):
    weighted = rows * held[: 2 * T, 0:1]
    return held[:T, META:] + weighted[:T] + weighted[T:]


def combine_next(ids, returned, held, small, result, taken, normed):
    rows = from_packed(held[: 2 * T, 1:2], sum_of_holders(returned, 0))
    taken[...] = rows.astype(BF16)
    total = mixed(rows, held)
    result[...] = total
    unit, _ = norm_parts(total.astype(BF16).astype(F32))
    normed[...] = (unit * small[1, 96:97, :].astype(F32)).astype(BF16)


def middle_grads(section, rows, grad_rows, grad, meta, small, grad_middle, sent, routed):
    gates = meta[: 2 * T, 0:1]
    gate_grads = jnp.sum(jnp.concatenate([grad, grad], 0) * rows, 1, keepdims=True)
    weighted = gates * gate_grads
    mean = weighted[:T] + weighted[T:]
    chosen = gates * (gate_grads - jnp.concatenate([mean, mean], 0))
    lanes = iota((2 * T, 128), 1).astype(F32)
    spread = jnp.where(lanes == meta[: 2 * T, 2:3], chosen, 0.0)
    logits_upper, logits_lower = split_pair(spread[:T] + spread[T:])
    part = dot(logits_upper, small[section]) + dot(logits_lower, small[section])
    grad_normed = part + grad_rows[:T] + grad_rows[T:]
    unit, inverse = norm_parts(meta[:T, META:])
    gain = small[section, 97:98, :].astype(F32)
    value = grad + norm_back(grad_normed, gain, unit, inverse)
    grad_middle[...] = value
    sent[...] = value.astype(BF16)
    upper, lower = split_pair(jnp.sum(grad_normed * unit, 0, keepdims=True))
    routed[:T, :D] = (unit * gain).astype(BF16)
    routed[:T, D : D + 128] = logits_upper
    routed[:T, D + 128 :] = logits_lower
    place = iota((16, D), 0)
    routed[T:, :D] = jnp.where(place == 0, upper, jnp.where(place == 1, lower, 0.0)).astype(BF16)
    named = (iota((16, 128), 1) == 97) & (iota((16, 128), 0) < 2)
    routed[T:, D : D + 128] = jnp.where(named, 1.0, 0.0).astype(BF16)
    routed[T:, D + 128 :] = jnp.zeros((16, 128), BF16)


def turn(ids, returned, held, seed, small, result, grad_middle, sent, routed):
    slot = held[: 2 * T, 1:2]
    rows = from_packed(slot, sum_of_holders(returned, 0))
    result[...] = mixed(rows, held)
    grad_rows = from_packed(slot, sum_of_holders(returned, SIDE))
    middle_grads(1, rows, grad_rows, seed[ids[0], 0], held, small, grad_middle, sent, routed)


def middle_backward(ids, returned, held, grad, taken, small, grad_middle, sent, routed):
    grad_rows = from_packed(held[: 2 * T, 1:2], sum_of_holders(returned, 0))
    middle_grads(0, taken[...].astype(F32), grad_rows, grad[...], held, small, grad_middle, sent, routed)


def attention_backward(section, ids, g0, g1, g2, g3, routed, small, kept, projected, own_w, other_w, own_a, other_a, n0, n1, n2, n3, packed, w, a, sems):
    mine = ids[0] == section
    rows = pl.ds(0, 4)
    fetch(mine, own_a, other_a, a.at[pl.ds(0, 192), :], sems.at[1])
    fetch(mine, own_w.at[rows], other_w.at[rows], w, sems.at[0])
    packed[:256, 2 * D :] = kept[...]
    packed[256:, 2 * D :] = jnp.zeros((96, D + 256), BF16)
    a[192:, :] = jnp.zeros((64, D), BF16)
    packed[272:, : D + 256] = routed[...]
    packed[272:, D + 256 : 2 * D] = jnp.zeros((80, D - 256), BF16)
    grad = jnp.concatenate([g0[...], g1[...], g2[...], g3[...]], 0)
    packed[:256, D : 2 * D] = grad
    arrive(own_a, a.at[pl.ds(0, 192), :], sems.at[1])
    grad_attended = dot_nt(grad, a[...]).astype(BF16)
    query, key, value = projected[:, :256], projected[:, 256:512], projected[:, 512:]
    grad_query, grad_key, grad_value = None, None, None
    for h in range(HEADS_OWN):
        mask = head_mask(h)
        query_part, grad_part = query * mask, grad_attended * mask
        scores = dot_nt(query_part, key) * SCALE
        raised = jnp.exp(scores - jnp.max(scores, -1, keepdims=True))
        probs = raised / jnp.sum(raised, -1, keepdims=True)
        grad_probs = dot_nt(grad_part, value)
        grad_scores = probs * (grad_probs - jnp.sum(grad_probs * probs, -1, keepdims=True))
        grad_scores = grad_scores.astype(BF16)
        parts = (
            dot(grad_scores, key * mask),
            dot_tn(grad_scores, query_part),
            dot_tn(probs.astype(BF16), grad_part),
        )
        if h == 0:
            grad_query, grad_key, grad_value = parts
        else:
            grad_query, grad_key, grad_value = (
                grad_query + parts[0],
                grad_key + parts[1],
                grad_value + parts[2],
            )
    grad_projected = jnp.concatenate([grad_query * SCALE, grad_key * SCALE, grad_value], 1).astype(BF16)
    packed[:256, :D] = grad_projected
    arrive(own_w.at[rows], w, sems.at[0])
    grad_normed = dot_nt(grad_projected, w[...].reshape(D, D))
    result = grad_normed.astype(BF16)
    for k, out in enumerate((n0, n1, n2, n3)):
        out[...] = result[k * T : (k + 1) * T, :]
    gain = jnp.sum(grad_normed * kept[:, :D].astype(F32), 0, keepdims=True)
    upper, lower = split_pair(gain / small[section, 96:97, :].astype(F32))
    place = iota((16, D), 0)
    packed[256:272, :D] = jnp.where(place == 0, upper, jnp.where(place == 1, lower, 0.0)).astype(BF16)
    named = (iota((16, D), 1) == 96) & (iota((16, D), 0) < 2)
    packed[256:272, D : 2 * D] = jnp.where(named, 1.0, 0.0).astype(BF16)


def input_grad(section, n0, n1, n2, n3, h, grad_middle, small):
    grad_normed = (n0[...].astype(F32) + n1[...].astype(F32)) + (n2[...].astype(F32) + n3[...].astype(F32))
    unit, inverse = norm_parts(h)
    return grad_middle[...] + norm_back(grad_normed, small[section, 96:97, :].astype(F32), unit, inverse)


def input_backward_next(ids, n0, n1, n2, n3, grad_middle, small, result, held, grad_out, out):
    h = result[...].astype(BF16).astype(F32)
    grad = input_grad(1, n0, n1, n2, n3, h, grad_middle, small).astype(BF16).astype(F32)
    grad_out[...] = grad
    rows = jnp.concatenate([grad, grad], 0) * held[: 2 * T, 0:1]
    send_to_holders(to_packed(held[2 * T : 2 * T + 1, :META], rows.astype(BF16)), out, 0)


def input_backward_last(ids, n0, n1, n2, n3, inputs, grad_middle, small, grad_two, one, two, stays, leaves):
    grad_one = input_grad(0, n0, n1, n2, n3, inputs[ids[0], 0], grad_middle, small)
    mine = ids[0] == 0
    stays[0] = jnp.where(mine, one[...], two[...])
    leaves[0] = jnp.where(mine, two[...], one[...])
    stays[1] = jnp.where(mine, grad_one, grad_two[...])
    leaves[1] = jnp.where(mine, grad_two[...], grad_one)


def expert_weight_grads(ids, one, r_one, two, r_two, grad_in, grad_out, held, result, sems, out_sems):
    mine = ids[0] == 0
    pairs = ((0, 0, 3), (1, 1, 2))
    for j in range(2):
        for _, a, b in pairs:
            for n in (a, b):
                fetch(mine, one.at[n, j], two.at[n, j], held.at[n, j, pl.ds(0, 320), :], sems.at[n, j, 0])
                fetch(mine, r_one.at[n, j], r_two.at[n, j], held.at[n, j, pl.ds(320, 320), :], sems.at[n, j, 1])
    for j in range(2):
        for place, a, b in pairs:
            for n in (a, b):
                arrive(one.at[n, j], held.at[n, j, pl.ds(0, 320), :], sems.at[n, j, 0])
                arrive(one.at[n, j], held.at[n, j, pl.ds(320, 320), :], sems.at[n, j, 1])
            result[place, j] = dot_tn(held[a, j], held[b, j])
            move(result.at[place, j], (grad_in, grad_out)[place].at[j], out_sems.at[place, j])
    for j in range(2):
        for place, _, _ in pairs:
            arrive(result.at[place, j], (grad_in, grad_out)[place].at[j], out_sems.at[place, j])


def shared_weight_grads(ids, p0, p1, rp0, rp1, out, packed, sems):
    mine = ids[0] == 0
    fetch(mine, p0, p1, packed.at[0], sems.at[0])
    fetch(mine, rp0, rp1, packed.at[1], sems.at[1])
    arrive(p0, packed.at[0], sems.at[0])
    arrive(p0, packed.at[1], sems.at[1])
    grad_qkv, grad_attn, extra = None, None, None
    for m in range(2):
        whole = (
            dot_tn(packed[m, :256, 2 * D : 3 * D], packed[m, :256, :D]),
            dot_tn(packed[m, :256, 3 * D :], packed[m, :256, D : 2 * D]),
            dot_tn(packed[m, 272:, :D], packed[m, 272:, D : D + 128])
            + dot_tn(packed[m, 272:, :D], packed[m, 272:, D + 128 : D + 256])
            + dot_tn(packed[m, 256:272, :D], packed[m, 256:272, D : D + 128]),
        )
        if m == 0:
            grad_qkv, grad_attn, extra = whole
        else:
            grad_qkv, grad_attn, extra = grad_qkv + whole[0], grad_attn + whole[1], extra + whole[2]
    middle = grad_qkv[:, 128:256] + extra
    out[:, :48, :128] = grad_qkv[:, :128].astype(BF16).reshape(N_EXPERT, 48, 128)
    out[:, :48, 128:256] = middle.astype(BF16).reshape(N_EXPERT, 48, 128)
    out[:, :48, 256:] = grad_qkv[:, 256:].astype(BF16).reshape(N_EXPERT, 48, 512)
    row, column = iota((256, 256), 0), iota((256, 256), 1)
    spread = ((row & 15) < 12) & (column == (row >> 4) * 12 + (row & 15))
    spread = jnp.where(spread, 1.0, 0.0).astype(BF16)
    out[:, 48:, :] = dot(spread, grad_attn.astype(BF16)).astype(BF16).reshape(N_EXPERT, 16, D)


def sum_shared(ids, arrived, out, attn, total):
    me = ids[1]
    summed = arrived[0].astype(F32)
    for n in range(1, N_EXPERT):
        summed = summed + arrived[n].astype(F32)
    total[...] = summed
    for s in range(N_SHARD):
        out[(s - me) & (N_SHARD - 1), :12, :] = total[s * 12 : s * 12 + 12, :]
    attn[...] = total[48:, :]


def finish(ids, q0, q1, q2, q3, attn_in, stays, arrives, qkv, attn, one, two, router, acts, grads, held):
    mine, me = ids[0], ids[1]
    acts[mine] = stays[0]
    acts[1 - mine] = arrives[0]
    grads[mine] = stays[1]
    grads[1 - mine] = arrives[1]
    attn[...] = attn_in[:12, :]
    for k, piece in enumerate((q0, q1, q2, q3)):
        held[(me - k) & (N_SHARD - 1)] = piece[...]
    total = None
    for a in range(N_SHARD):
        for j in range(3):
            qkv[:, j * D + a * 192 : j * D + a * 192 + 192] = held[a, :12, j * 256 : j * 256 + 192]
        part = held[a, :12, 128:256]
        total = part if total is None else total + part
    diagonal = iota((12, 12), 0) == iota((12, 12), 1)
    one[...] = jnp.sum(jnp.where(diagonal, total[:, 96:97], 0.0), 0, keepdims=True)
    two[...] = jnp.sum(jnp.where(diagonal, total[:, 97:98], 0.0), 0, keepdims=True)
    router[...] = total[:, 64:96]


def along(value, axis, by):
    count = lax.axis_size(axis)
    return lax.ppermute(value, axis, [(i, (i + by) % count) for i in range(count)])


def gather_shards(value):
    return [value] + [along(value, "shard", k) for k in range(1, N_SHARD)]


def return_shards(pieces):
    return [pieces[0]] + [along(pieces[k], "shard", -k) for k in range(1, N_SHARD)]


def send_shards(pieces):
    return [pieces[0]] + [along(pieces[k], "shard", k) for k in range(1, N_SHARD)]


def exchange(value):
    rows = value.size // (N_ALL * 128)
    return lax.all_to_all(value.reshape(N_ALL, rows, 128), ("expert", "shard"), 0, 0, tiled=True)


def swap(value):
    return lax.ppermute(value, "section", [(0, 1), (1, 0)])


def up(value):
    return lax.ppermute(value, "section", [(0, 1)])


def down(value):
    return lax.ppermute(value, "section", [(1, 0)])


def after(first, *values):
    return lax.optimization_barrier((first, *values))


def dma(*shape):
    return pltpu.SemaphoreType.DMA(shape)


def local(inputs, cotangent, w_qkv, w_attn, gain_one, gain_two, router, w_in, w_out, routes):
    section = lax.axis_index("section")
    me = lax.axis_index("shard")
    ids = jnp.stack([section, me]).astype(jnp.int32)
    rows_shape = ((T, D), BF16)
    wide_shape = ((T, D), F32)
    per_expert = N_SHARD * GROUP
    w_scratch = pltpu.VMEM((N_SHARD, 192, D), BF16)
    expert_scratch = [pltpu.VMEM((2, D, D), BF16), pltpu.VMEM((2, D, D), BF16)]
    staged_scratch = pltpu.VMEM((N_SHARD, ORDERED, 128), BF16)

    place = jnp.arange(ORDERED, dtype=jnp.int32)
    within = place % (2 * GROUP)
    source = (
        ((within % GROUP) // CAP) * SIDE
        + (place // (2 * GROUP)) * ROWS
        + (within // GROUP) * CAP
        + within % CAP
    )
    order = (source[:, None] == jnp.arange(BLOCK, dtype=jnp.int32)[None, :]).astype(BF16)
    back_order = (source[None, :] == jnp.arange(BLOCK, dtype=jnp.int32)[:, None]).astype(BF16)

    p0, p1, p2, p3 = call(
        begin,
        [((1344, 128), BF16)] * 4,
        [ids, inputs, w_qkv[0], gain_one, gain_two, router[0].T],
        [pltpu.VMEM((T, D), F32), pltpu.VMEM((3, 192, D), BF16), pltpu.VMEM((1, 192), BF16), pltpu.VMEM((1, 192), BF16), dma(6)],
        anywhere=(1, 2, 3, 4),
        mib=56,
    )
    p0, p1, p2, p3, order, back_order = after(*send_shards([p0, p1, p2, p3]), order, back_order)
    own_w, units = call(
        join,
        [((5, 192, D), BF16), ((4 * T, D), BF16)],
        [ids, p0, p1, p2, p3],
        [pltpu.VMEM((N_SHARD, 64, 256), BF16)],
    )
    other_w = swap(own_w)
    own_a, own_routes, own_w = after(w_attn[0], routes.reshape(2, T, 2), own_w)
    other_a, other_routes = swap(own_a), swap(own_routes)
    weights = (own_w, other_w, own_a, other_a)
    attention_scratch = [w_scratch, pltpu.VMEM((192, D), BF16), dma(5)]

    o0, o1, o2, o3, kept_one, projected_one, small, h_one = call(
        attention_one,
        [rows_shape] * 4 + [((256, D + 256), BF16), ((256, D), BF16), ((2, 128, D), BF16), wide_shape],
        [ids, units, *weights, inputs],
        attention_scratch,
        anywhere=(2, 3, 4, 5, 6),
        mib=56,
    )
    own_in, own_out, o0 = after(w_in[0], w_out[0], o0)
    other_in, other_out = swap(own_in), swap(own_out)
    experts = (own_in, other_in, own_out, other_out)
    packed_shape = ((N_EXPERT, N_SHARD, SIDE, 128), BF16)
    state_shape = ((2 * T + 8, META + D), F32)
    half_shape = ((2, 2, per_expert, D), BF16)
    slope_shape = ((2, per_expert, D), BF16)
    both_shape = ((4, 2, per_expert, D), BF16)
    sent, state_one = call(
        functools.partial(dispatch, 0),
        [packed_shape, state_shape],
        [ids, h_one, *return_shards([o0, o1, o2, o3]), small, own_routes, other_routes],
    )
    sent, fwd_one, slope = call(
        expert_forward,
        [((N_ALL, SIDE, 128), BF16), half_shape, slope_shape],
        [ids, exchange(sent), order, back_order, *experts],
        [*expert_scratch, staged_scratch, dma(2, 2)],
        anywhere=(4, 5, 6, 7),
        mib=24,
    )
    result_one, taken, normed = call(
        combine_next,
        [wide_shape, ((2 * T, D), BF16), rows_shape],
        [ids, exchange(sent).reshape(packed_shape[0]), state_one, small],
    )

    o0, o1, o2, o3, kept_two, projected_two = call(
        attention_two,
        [rows_shape] * 4 + [((256, D + 256), BF16), ((256, D), BF16)],
        [ids, *gather_shards(normed), *weights],
        attention_scratch,
        anywhere=(5, 6, 7, 8),
        mib=24,
    )
    double_shape = ((N_EXPERT, N_SHARD, 2 * SIDE, 128), BF16)
    sent, state_two = call(
        functools.partial(dispatch, 1),
        [double_shape, state_shape],
        [ids, result_one, *return_shards([o0, o1, o2, o3]), small, own_routes, other_routes, cotangent],
    )
    sent, both_two = call(
        expert_both,
        [((N_ALL, 2 * SIDE, 128), BF16), both_shape],
        [ids, exchange(sent), order, back_order, *experts],
        [*expert_scratch, staged_scratch, staged_scratch, dma(2, 2)],
        anywhere=(4, 5, 6, 7),
        mib=28,
    )
    routed_shape = ((T + 16, D + 256), BF16)
    returned, r_both_two = after(exchange(sent), up(both_two))
    result_two, grad_middle, sent, routed = call(
        turn,
        [wide_shape, wide_shape, rows_shape, routed_shape],
        [ids, returned.reshape(double_shape[0]), state_two, cotangent, small],
    )

    def attention_grads(s, rows, kept, projected, routed):
        return call(
            functools.partial(attention_backward, s),
            [rows_shape] * 4 + [((352, 3 * D + 256), BF16)],
            [ids, *rows, routed, small, kept, projected, *weights],
            [w_scratch, pltpu.VMEM((256, D), BF16), dma(2)],
            anywhere=(9, 10, 11, 12),
            mib=24,
        )

    n0, n1, n2, n3, packed_two = attention_grads(1, gather_shards(sent), kept_two, projected_two, routed)
    grad_two, sent = call(
        input_backward_next,
        [wide_shape, packed_shape],
        [ids, *return_shards([n0, n1, n2, n3]), grad_middle, small, result_one, state_one],
    )

    arrived, r_packed_two = after(exchange(sent), up(packed_two))
    sent, both_one = call(
        expert_backward,
        [((N_ALL, SIDE, 128), BF16), both_shape],
        [ids, arrived, order, back_order, slope, fwd_one, *experts],
        [*expert_scratch, staged_scratch, pltpu.VMEM(*slope_shape), dma(3, 2)],
        anywhere=(4, 5, 6, 7, 8, 9),
        mib=28,
    )
    returned, r_both_one = after(exchange(sent), down(both_one))
    grad_middle, sent, routed = call(
        middle_backward,
        [wide_shape, rows_shape, routed_shape],
        [ids, returned.reshape(packed_shape[0]), state_one, grad_two, taken, small],
    )
    n0, n1, n2, n3, packed_one = attention_grads(0, gather_shards(sent), kept_one, projected_one, routed)

    pieces = return_shards([n0, n1, n2, n3])
    payload = call(
        shared_weight_grads,
        [((N_EXPERT, 64, D), BF16)],
        [ids, packed_one, packed_two, down(packed_one), r_packed_two],
        [pltpu.VMEM((2, 352, 3 * D + 256), BF16), dma(2)],
        anywhere=(1, 2, 3, 4),
        mib=24,
    )[0]
    payload, *pieces = after(payload, *pieces)
    summed = lax.all_to_all(payload, "expert", 0, 0, tiled=True)
    stays, leaves = call(
        input_backward_last,
        [((2, T, D), F32)] * 2,
        [ids, *pieces, inputs, grad_middle, small, grad_two, result_one, result_two],
    )
    grad_in, grad_out = call(
        expert_weight_grads,
        [((2, D, D), F32)] * 2,
        [ids, both_one, r_both_one, both_two, r_both_two],
        [pltpu.VMEM((4, 2, 2 * per_expert, D), BF16), pltpu.VMEM((2, 2, D, D), F32), dma(4, 2, 2), dma(2, 2)],
        anywhere=(1, 2, 3, 4),
        outs_anywhere=(0, 1),
        mib=56,
    )
    summed, leaves, grad_in = after(summed, leaves, grad_in)
    arrives = swap(leaves)
    shares, attn = call(
        sum_shared,
        [((N_SHARD, 16, D), F32), ((16, D), F32)],
        [ids, summed],
        [pltpu.VMEM((64, D), F32)],
    )
    pairs = [
        (e * N_SHARD + s, (N_SHARD * s + e // N_SHARD) * N_SHARD + e % N_SHARD)
        for e in range(N_EXPERT)
        for s in range(N_SHARD)
    ]
    grad_qkv, grad_attn, grad_one, grad_two, grad_router, acts, grads = call(
        finish,
        [
            ((12, 3 * D), F32),
            ((12, D), F32),
            ((1, 12), F32),
            ((1, 12), F32),
            ((12, 32), F32),
            ((2, T, D), F32),
            ((2, T, D), F32),
        ],
        [ids, *send_shards(shares), lax.ppermute(attn, ("expert", "shard"), pairs), stays, arrives],
        [pltpu.VMEM((N_SHARD, 16, D), F32)],
    )
    return (
        acts.reshape(1, 2, 1, T, D),
        grads.reshape(1, 2, 1, T, D),
        grad_qkv[None],
        grad_attn[None],
        grad_one,
        grad_two,
        grad_router[None],
        grad_in[None],
        grad_out[None],
    )


def solution(mesh):
    return jax.shard_map(
        local,
        mesh=mesh,
        in_specs=(
            P(None, "expert", "shard", None),
            P(None, "expert", "shard", None),
            P("section", "shard", None),
            P("section", "shard", None),
            P("section", "shard"),
            P("section", "shard"),
            P("section", "shard", None),
            P("section", "expert", None, "shard"),
            P("section", "expert", "shard", None),
            P("section", None, "expert", "shard", None, None),
        ),
        out_specs=(
            P("section", None, "expert", "shard", None),
            P("section", None, "expert", "shard", None),
            P("section", ("expert", "shard"), None),
            P("section", ("expert", "shard"), None),
            P("section", ("expert", "shard")),
            P("section", ("expert", "shard")),
            P("section", ("expert", "shard"), None),
            P("section", "expert", None, "shard"),
            P("section", "expert", "shard", None),
        ),
        check_vma=False,
    )
```

```python
import functools
import math

import jax
import jax.numpy as jnp
from jax import lax
from jax.experimental import pallas as pl
from jax.experimental.pallas import tpu as pltpu
from jax.sharding import PartitionSpec as P

F32 = jnp.float32
BF16 = jnp.bfloat16
D = 768
HEADS_OWN = 3
HDIM = 64
T = 64
CAP = 5
CHUNKS = 6
N_EXPERT = 16
N_SHARD = 4
N_ALL = N_EXPERT * N_SHARD
SIDE = 32
BLOCK = 2 * N_EXPERT * SIDE
GROUP = N_EXPERT * CAP
ORDERED = CHUNKS * GROUP
HALF = D // 2
META = 128
EPS = 1e-06
SCALE = 1.0 / math.sqrt(HDIM)


def dot(a, b):
    return lax.dot_general(a, b, (((1,), (0,)), ((), ())), preferred_element_type=F32)


def dot_nt(a, b):
    return lax.dot_general(a, b, (((1,), (1,)), ((), ())), preferred_element_type=F32)


def dot_tn(a, b):
    return lax.dot_general(a, b, (((0,), (0,)), ((), ())), preferred_element_type=F32)


def iota(shape, dim):
    return lax.broadcasted_iota(jnp.int32, shape, dim)


def call(body, outs, ins, scratch=(), anywhere=(), scalars=1, mib=12, outs_anywhere=(), aliases=None):
    specs = []
    for place in range(len(ins)):
        if place < scalars:
            specs.append(pl.BlockSpec(memory_space=pltpu.SMEM))
        elif place in anywhere:
            specs.append(pl.BlockSpec(memory_space=pltpu.HBM))
        else:
            specs.append(pl.BlockSpec(memory_space=pltpu.VMEM))
    return pl.pallas_call(
        body,
        out_shape=tuple(jax.ShapeDtypeStruct(shape, kind) for shape, kind in outs),
        in_specs=specs,
        out_specs=tuple(
            pl.BlockSpec(memory_space=pltpu.HBM if place in outs_anywhere else pltpu.VMEM)
            for place in range(len(outs))
        ),
        scratch_shapes=list(scratch),
        input_output_aliases=aliases or {},
        compiler_params=pltpu.CompilerParams(vmem_limit_bytes=mib * 1024 * 1024),
    )(*ins)


def fetch(mine, own, other, target, sem):
    @pl.when(mine)
    def _():
        pltpu.make_async_copy(own, target, sem).start()

    @pl.when(jnp.logical_not(mine))
    def _():
        pltpu.make_async_copy(other, target, sem).start()


def arrive(own, target, sem):
    pltpu.make_async_copy(own, target, sem).wait()


def move(source, target, sem):
    pltpu.make_async_copy(source, target, sem).start()


def norm_parts(rows):
    centered = rows - jnp.mean(rows, -1, keepdims=True)
    inverse = lax.rsqrt(jnp.mean(centered * centered, -1, keepdims=True) + EPS)
    return centered * inverse, inverse


def norm_back(grad, gain, unit, inverse):
    scaled = grad * gain
    return inverse * (
        scaled
        - jnp.mean(scaled, -1, keepdims=True)
        - unit * jnp.mean(scaled * unit, -1, keepdims=True)
    )


def split_pair(values):
    upper = values.astype(BF16)
    return upper, (values - upper.astype(F32)).astype(BF16)


def row_of(column):
    size = column.shape[0]
    diagonal = iota((size, size), 0) == iota((size, size), 1)
    return jnp.sum(jnp.where(diagonal, column, 0.0), 0, keepdims=True)


def slots_of(route_column):
    named = (iota((2 * T, 32), 1) == route_column).astype(F32)
    earlier = ((iota((2 * T, 2 * T), 1) & (T - 1)) < (iota((2 * T, 2 * T), 0) & (T - 1))).astype(BF16)
    before = dot(earlier, named.astype(BF16))
    return route_column.astype(F32) * CAP + jnp.sum(before * named, 1, keepdims=True)


def packed_place(index):
    within = index & (SIDE - 1)
    chunk = (within * 205) >> 10
    return (index >> 5) * CAP + within - chunk * CAP, chunk


def to_packed(slot_row, rows):
    slot, chunk = packed_place(iota((BLOCK, 2 * T), 0))
    hit = slot.astype(F32) == slot_row
    total = None
    for c in range(CHUNKS):
        mask = jnp.where(hit & (chunk == c), 1.0, 0.0).astype(BF16)
        part = dot(mask, rows[:, c * 128 : (c + 1) * 128])
        total = part if total is None else total + part
    return total.astype(BF16)


def from_packed(slot_column, packed):
    slot, chunk = packed_place(iota((2 * T, BLOCK), 1))
    hit = slot.astype(F32) == slot_column
    parts = []
    for c in range(CHUNKS):
        mask = jnp.where(hit & (chunk == c), 1.0, 0.0).astype(BF16)
        parts.append(dot(mask, packed))
    return jnp.concatenate(parts, 1)


def send_to_holders(packed, out_ref, start):
    blocks = packed.reshape(N_EXPERT, 2, SIDE, 128)
    for s in range(N_SHARD):
        out_ref[:, s, start : start + SIDE, :] = blocks[:, s % 2]


def sum_of_holders(in_ref, start):
    parts = []
    for j in range(2):
        total = in_ref[:, j, start : start + SIDE, :].astype(F32)
        total = total + in_ref[:, j + 2, start : start + SIDE, :].astype(F32)
        parts.append(total.astype(BF16).reshape(N_EXPERT, 1, SIDE, 128))
    return jnp.concatenate(parts, 1).reshape(BLOCK, 128)


def group_of(packed_ref, group, start):
    rows = packed_ref[group * N_EXPERT : (group + 1) * N_EXPERT, start : start + SIDE, :]
    return rows.reshape(N_EXPERT * SIDE, 128)


def order_pair(order, first, second):
    return dot(order, jnp.concatenate([first, second], 1)).astype(BF16)


def place_rows(ordered, half, group, kept_ref):
    for c in range(CHUNKS):
        kept_ref[group * GROUP : (group + 1) * GROUP, c * 128 : (c + 1) * 128] = ordered[
            c * GROUP : (c + 1) * GROUP, half * 128 : half * 128 + 128
        ]


def stage_rows(rows, staged_ref):
    for group in range(N_SHARD):
        for c in range(CHUNKS):
            staged_ref[group, c * GROUP : (c + 1) * GROUP, :] = rows[
                group * GROUP : (group + 1) * GROUP, c * 128 : (c + 1) * 128
            ]


def unorder_pair(back_order, first, second, out_ref, places):
    packed = dot(back_order, jnp.concatenate([first, second], 1)).astype(BF16)
    for half, (group, start) in enumerate(places):
        out_ref[group * N_EXPERT : (group + 1) * N_EXPERT, start : start + SIDE, :] = packed[
            :, half * 128 : half * 128 + 128
        ].reshape(N_EXPERT, SIDE, 128)


def head_mask(h):
    lane = iota((1, 256), 1)
    return ((lane >= h * HDIM) & (lane < (h + 1) * HDIM)).astype(BF16)


def fold(value):
    half = value.shape[0] // 2
    return jnp.concatenate([value[:half, :], value[half:, :]], 1)


def unfold(value):
    return jnp.concatenate([value[:, :64], value[:, 64:]], 0)


def begin(ids, inputs, w, gain_one, gain_two, router, p0, p1, p2, p3, h, held, thin_one, thin_two, sems):
    mine, me = ids[0], ids[1]
    move(inputs.at[mine, 0], h, sems.at[0])
    for j in range(3):
        move(w.at[:, pl.ds(j * D, D)], held.at[j], sems.at[1 + j])
    move(gain_one, thin_one, sems.at[4])
    move(gain_two, thin_two, sems.at[5])
    arrive(gain_one, thin_one, sems.at[4])
    arrive(gain_two, thin_two, sems.at[5])
    rows = iota((32, 192), 0)
    gains = jnp.where(rows == 0, thin_one[...].astype(F32), jnp.where(rows == 1, thin_two[...].astype(F32), 0.0))
    thin = jnp.concatenate([router[...], gains.astype(BF16)], 0)
    arrive(inputs.at[mine, 0], h, sems.at[0])
    unit, _ = norm_parts(h[...])
    unit = unit.astype(BF16)
    for j in range(3):
        arrive(w.at[:, pl.ds(j * D, D)], held.at[j], sems.at[1 + j])
    for piece in (p0, p1, p2, p3):
        piece[864:928, :] = thin[:, :128]
        piece[928:960, :] = fold(thin[:, 128:])
        for c in range(CHUNKS):
            piece[960 + 64 * c : 1024 + 64 * c, :] = unit[:, c * 128 : (c + 1) * 128]
    for s in range(N_SHARD):
        for k, piece in enumerate((p0, p1, p2, p3)):

            @pl.when(((s - me) & (N_SHARD - 1)) == k)
            def _(s=s, piece=piece):
                parts = [held[j, :, s * 192 : s * 192 + 192] for j in range(3)]
                for j in range(3):
                    piece[192 * j : 192 * j + 192, :] = parts[j][:, :128]
                piece[576:768, :] = jnp.concatenate([parts[0][:, 128:], parts[1][:, 128:]], 1)
                piece[768:864, :] = fold(parts[2][:, 128:])


def join(ids, p0, p1, p2, p3, out, units, held):
    me = ids[1]
    none = jnp.zeros((192, 64), BF16)
    for k, piece in enumerate((p0, p1, p2, p3)):
        place = (me - k) & (N_SHARD - 1)
        rest = piece[576:768, :]
        rests = (rest[:, :64], rest[:, 64:], unfold(piece[768:864, :]))
        for j in range(3):
            out[place, :, 256 * j : 256 * j + 128] = piece[192 * j : 192 * j + 192, :]
            out[place, :, 256 * j + 128 : 256 * j + 256] = jnp.concatenate([rests[j], none], 1)
        held[place, :, :128] = piece[864:928, :]
        held[place, :, 128:] = jnp.concatenate([unfold(piece[928:960, :]), none[:64]], 1)
        for c in range(CHUNKS):
            units[k * T : (k + 1) * T, c * 128 : (c + 1) * 128] = piece[960 + 64 * c : 1024 + 64 * c, :]
    out[4] = jnp.zeros((192, D), BF16)
    for a in range(N_SHARD):
        out[4, 64:128, a * 192 : (a + 1) * 192] = held[a, :, :192]


def attend(x, w, a, kept, projected, outs):
    kept[:, :D] = x
    whole = dot(x, w[...].reshape(D, D)).astype(BF16)
    projected[...] = whole
    query, key, value = whole[:, :256], whole[:, 256:512], whole[:, 512:]
    attended = None
    for h in range(HEADS_OWN):
        mask = head_mask(h)
        scores = dot_nt(query * mask, key) * SCALE
        raised = jnp.exp(scores - jnp.max(scores, -1, keepdims=True))
        probs = (raised / jnp.sum(raised, -1, keepdims=True)).astype(BF16)
        part = dot(probs, value * mask)
        attended = part if attended is None else attended + part
    attended = attended.astype(BF16)
    kept[:, D:] = attended
    result = dot(attended[:, :192], a[...]).astype(BF16)
    for k, out in enumerate(outs):
        out[...] = result[k * T : (k + 1) * T, :]


def attention_one(ids, units, own_w, other_w, own_a, other_a, inputs, o0, o1, o2, o3, kept, projected, small, h, w, a, sems):
    mine = ids[0] == 0
    rows, extra = pl.ds(0, 4), pl.ds(0, 128)
    fetch(mine, own_w.at[4, extra], other_w.at[4, extra], small.at[0], sems.at[2])
    fetch(mine, own_w.at[rows], other_w.at[rows], w, sems.at[0])
    fetch(mine, own_a, other_a, a, sems.at[1])
    fetch(mine, other_w.at[4, extra], own_w.at[4, extra], small.at[1], sems.at[3])
    move(inputs.at[ids[0], 0], h, sems.at[4])
    arrive(own_w.at[4, extra], small.at[0], sems.at[2])
    x = (units[...].astype(F32) * small[0, 96:97, :].astype(F32)).astype(BF16)
    arrive(own_w.at[rows], w, sems.at[0])
    arrive(own_a, a, sems.at[1])
    attend(x, w, a, kept, projected, (o0, o1, o2, o3))
    arrive(own_w.at[4, extra], small.at[1], sems.at[3])
    arrive(inputs.at[ids[0], 0], h, sems.at[4])


def attention_two(ids, x0, x1, x2, x3, own_w, other_w, own_a, other_a, o0, o1, o2, o3, kept, projected, w, a, sems):
    mine = ids[0] == 1
    rows = pl.ds(0, 4)
    fetch(mine, own_w.at[rows], other_w.at[rows], w, sems.at[0])
    fetch(mine, own_a, other_a, a, sems.at[1])
    x = jnp.concatenate([x0[...], x1[...], x2[...], x3[...]], 0)
    arrive(own_w.at[rows], w, sems.at[0])
    arrive(own_a, a, sems.at[1])
    attend(x, w, a, kept, projected, (o0, o1, o2, o3))


def dispatch(section, ids, h, o0, o1, o2, o3, small, own_routes, other_routes, *refs):
    if section == 1:
        seed, out, held = refs
        start = h[...].astype(BF16).astype(F32)
    else:
        out, held = refs
        start = h[...]
    middle = start + (
        (o0[...].astype(F32) + o1[...].astype(F32)) + (o2[...].astype(F32) + o3[...].astype(F32))
    )
    held[:T, META:] = middle
    held[T:, META:] = jnp.zeros((T + 8, D), F32)
    unit, _ = norm_parts(middle)
    normed = (unit * small[section, 97:98, :].astype(F32)).astype(BF16)
    route = jnp.where(ids[0] == section, own_routes[ids[0]], other_routes[ids[0]])
    column = jnp.concatenate([route[:, 0:1], route[:, 1:2]], 0)
    slot_column = slots_of(column)
    slot_row = row_of(slot_column)
    send_to_holders(to_packed(slot_row, jnp.concatenate([normed, normed], 0)), out, 0)
    logits = dot_nt(normed, small[section])
    logits = jnp.concatenate([logits, logits], 0)
    lanes = iota((2 * T, 128), 1)
    chosen = jnp.sum(jnp.where(lanes == column + 64, logits, 0.0), 1, keepdims=True)
    one, two = chosen[:T], chosen[T:]
    top = jnp.maximum(one, two)
    one, two = jnp.exp(one - top), jnp.exp(two - top)
    total = one + two
    gates = jnp.concatenate([one / total, two / total], 0)
    held[: 2 * T, :META] = jnp.where(
        lanes == 0, gates, jnp.where(lanes == 1, slot_column, column.astype(F32) + 64.0)
    )
    held[2 * T :, :META] = jnp.broadcast_to(slot_row, (8, META))
    if section == 1:
        grad = seed[ids[0], 0]
        rows = jnp.concatenate([grad, grad], 0) * gates
        send_to_holders(to_packed(slot_row, rows.astype(BF16)), out, SIDE)


def split_experts(ids, w_in, w_out, keep, after, before, sems):
    j = ids[1] & 1
    other = 1 - j
    low, high = pl.ds(0, HALF), pl.ds(HALF, HALF)
    copies = [(w_in.at[j], keep.at[0]), (w_out.at[j], keep.at[1])]
    for part, target in ((low, after), (high, before)):
        copies.append((w_in.at[other, :, part], target.at[:, low]))
        copies.append((w_out.at[other, part, low], target.at[low, high]))
        copies.append((w_out.at[other, part, high], target.at[high, high]))
    for n, (source, target) in enumerate(copies):
        move(source, target, sems.at[n])
    for n, (source, target) in enumerate(copies):
        arrive(source, target, sems.at[n])


def expert_copies(keep, before, after, w_in, w_out):
    low, high = pl.ds(0, HALF), pl.ds(HALF, HALF)
    inner = [(keep, lambda r: r.at[0], w_in.at[:, pl.ds(0, D)])]
    outer = [(keep, lambda r: r.at[1], w_out.at[pl.ds(0, D), :])]
    for n, pair in enumerate((before, after)):
        place = pl.ds(D + n * HALF, HALF)
        inner.append((pair, lambda r: r.at[:, low], w_in.at[:, place]))
        outer.append((pair, lambda r: r.at[low, high], w_out.at[place, low]))
        outer.append((pair, lambda r: r.at[high, high], w_out.at[place, high]))
    return inner, outer


def load_experts(copies, mine, sems):
    for n, ((own, other), part, target) in enumerate(copies):
        fetch(mine, part(own), part(other), target, sems.at[n])


def wait_experts(copies, sems):
    for n, ((own, _), part, target) in enumerate(copies):
        arrive(part(own), target, sems.at[n])


def gelu_parts(up):
    share = 0.5 * (1.0 + lax.erf(up * math.sqrt(0.5)))
    return (up * share).astype(BF16), share + up * jnp.exp(-0.5 * up * up) * (1.0 / math.sqrt(2.0 * math.pi))


def expert_forward(ids, arrived, order, back_order, k0, k1, b0, b1, a0, a1, out, kept, slope, w_in, w_out, staged, sems_in, sems_out):
    inner, outer = expert_copies((k0, k1), (b0, b1), (a0, a1), w_in, w_out)
    load_experts(inner, ids[0] == 0, sems_in)
    load_experts(outer, ids[0] == 0, sems_out)
    for pair in (0, 2):
        ordered = order_pair(order[...], group_of(arrived, pair, 0), group_of(arrived, pair + 1, 0))
        place_rows(ordered, 0, pair, kept.at[0])
        place_rows(ordered, 1, pair + 1, kept.at[0])
    wait_experts(inner, sems_in)
    result = None
    for q in range(2):
        hidden, scale = gelu_parts(dot(kept[0], w_in[:, q * D : (q + 1) * D]))
        kept[1 + q] = hidden
        slope[q] = scale.astype(BF16)
        if q == 0:
            wait_experts(outer, sems_out)
        part = dot(hidden, w_out[q * D : (q + 1) * D, :])
        result = part if result is None else result + part
    stage_rows(result.astype(BF16), staged)
    for pair in (0, 2):
        unorder_pair(back_order[...], staged[pair], staged[pair + 1], out, ((pair, 0), (pair + 1, 0)))


def expert_both(ids, arrived, order, back_order, k0, k1, b0, b1, a0, a1, out, kept, w_in, w_out, staged, staged_back, sems_in, sems_out):
    inner, outer = expert_copies((k0, k1), (b0, b1), (a0, a1), w_in, w_out)
    load_experts(inner, ids[0] == 1, sems_in)
    load_experts(outer, ids[0] == 1, sems_out)
    for group in range(N_SHARD):
        ordered = order_pair(order[...], group_of(arrived, group, 0), group_of(arrived, group, SIDE))
        place_rows(ordered, 0, group, kept.at[0])
        place_rows(ordered, 1, group, kept.at[3])
    wait_experts(inner, sems_in)
    wait_experts(outer, sems_out)
    result, back = None, None
    for q in range(2):
        part_in, part_out = w_in[:, q * D : (q + 1) * D], w_out[q * D : (q + 1) * D, :]
        hidden, scale = gelu_parts(dot(kept[0], part_in))
        kept[1 + q] = hidden
        grad_up = (dot_nt(kept[3], part_out) * scale).astype(BF16)
        kept[4 + q] = grad_up
        parts = (dot(hidden, part_out), dot_nt(grad_up, part_in))
        result = parts[0] if q == 0 else result + parts[0]
        back = parts[1] if q == 0 else back + parts[1]
    stage_rows(result.astype(BF16), staged)
    stage_rows(back.astype(BF16), staged_back)
    for group in range(N_SHARD):
        unorder_pair(back_order[...], staged[group], staged_back[group], out, ((group, 0), (group, SIDE)))


def expert_backward(ids, arrived, order, back_order, slope_in, fwd, k0, k1, b0, b1, a0, a1, out, kept, w_in, w_out, staged, slope, sems_in, sems_out, sems):
    inner, outer = expert_copies((k0, k1), (b0, b1), (a0, a1), w_in, w_out)
    load_experts(outer, ids[0] == 0, sems_out)
    load_experts(inner, ids[0] == 0, sems_in)
    move(slope_in, slope, sems.at[0])
    move(fwd, kept.at[pl.ds(0, 3)], sems.at[1])
    for pair in (0, 2):
        ordered = order_pair(order[...], group_of(arrived, pair, 0), group_of(arrived, pair + 1, 0))
        place_rows(ordered, 0, pair, kept.at[3])
        place_rows(ordered, 1, pair + 1, kept.at[3])
    arrive(slope_in, slope, sems.at[0])
    wait_experts(outer, sems_out)
    back = None
    for q in range(2):
        grad_up = (dot_nt(kept[3], w_out[q * D : (q + 1) * D, :]) * slope[q].astype(F32)).astype(BF16)
        kept[4 + q] = grad_up
        if q == 0:
            wait_experts(inner, sems_in)
        part = dot_nt(grad_up, w_in[:, q * D : (q + 1) * D])
        back = part if q == 0 else back + part
    stage_rows(back.astype(BF16), staged)
    for pair in (0, 2):
        unorder_pair(back_order[...], staged[pair], staged[pair + 1], out, ((pair, 0), (pair + 1, 0)))
    arrive(fwd, kept.at[pl.ds(0, 3)], sems.at[1])


def mixed(rows, held):
    weighted = rows * held[: 2 * T, 0:1]
    return held[:T, META:] + weighted[:T] + weighted[T:]


def combine_next(ids, returned, held, small, result, taken, normed):
    rows = from_packed(held[: 2 * T, 1:2], sum_of_holders(returned, 0))
    taken[...] = rows.astype(BF16)
    total = mixed(rows, held)
    result[...] = total
    unit, _ = norm_parts(total.astype(BF16).astype(F32))
    normed[...] = (unit * small[1, 96:97, :].astype(F32)).astype(BF16)


def middle_grads(section, rows, grad_rows, grad, meta, small, grad_middle, sent, routed):
    gates = meta[: 2 * T, 0:1]
    gate_grads = jnp.sum(jnp.concatenate([grad, grad], 0) * rows, 1, keepdims=True)
    weighted = gates * gate_grads
    mean = weighted[:T] + weighted[T:]
    chosen = gates * (gate_grads - jnp.concatenate([mean, mean], 0))
    lanes = iota((2 * T, 128), 1).astype(F32)
    spread = jnp.where(lanes == meta[: 2 * T, 2:3], chosen, 0.0)
    logits_upper, logits_lower = split_pair(spread[:T] + spread[T:])
    part = dot(logits_upper, small[section]) + dot(logits_lower, small[section])
    grad_normed = part + grad_rows[:T] + grad_rows[T:]
    unit, inverse = norm_parts(meta[:T, META:])
    gain = small[section, 97:98, :].astype(F32)
    value = grad + norm_back(grad_normed, gain, unit, inverse)
    grad_middle[...] = value
    sent[...] = value.astype(BF16)
    upper, lower = split_pair(jnp.sum(grad_normed * unit, 0, keepdims=True))
    routed[:T, :D] = (unit * gain).astype(BF16)
    routed[:T, D : D + 128] = logits_upper
    routed[:T, D + 128 :] = logits_lower
    place = iota((16, D), 0)
    routed[T:, :D] = jnp.where(place == 0, upper, jnp.where(place == 1, lower, 0.0)).astype(BF16)
    named = (iota((16, 128), 1) == 97) & (iota((16, 128), 0) < 2)
    routed[T:, D : D + 128] = jnp.where(named, 1.0, 0.0).astype(BF16)
    routed[T:, D + 128 :] = jnp.zeros((16, 128), BF16)


def turn(ids, returned, held, seed, small, result, grad_middle, sent, routed):
    slot = held[: 2 * T, 1:2]
    rows = from_packed(slot, sum_of_holders(returned, 0))
    result[...] = mixed(rows, held)
    grad_rows = from_packed(slot, sum_of_holders(returned, SIDE))
    middle_grads(1, rows, grad_rows, seed[ids[0], 0], held, small, grad_middle, sent, routed)


def middle_backward(ids, returned, held, grad, taken, small, grad_middle, sent, routed):
    grad_rows = from_packed(held[: 2 * T, 1:2], sum_of_holders(returned, 0))
    middle_grads(0, taken[...].astype(F32), grad_rows, grad[...], held, small, grad_middle, sent, routed)


def attention_backward(section, ids, g0, g1, g2, g3, routed, small, kept, projected, own_w, other_w, own_a, other_a, n0, n1, n2, n3, packed, w, a, sems):
    mine = ids[0] == section
    rows = pl.ds(0, 4)
    fetch(mine, own_a, other_a, a.at[pl.ds(0, 192), :], sems.at[1])
    fetch(mine, own_w.at[rows], other_w.at[rows], w, sems.at[0])
    packed[:256, 2 * D :] = kept[...]
    packed[256:, 2 * D :] = jnp.zeros((96, D + 256), BF16)
    a[192:, :] = jnp.zeros((64, D), BF16)
    packed[272:, : D + 256] = routed[...]
    packed[272:, D + 256 : 2 * D] = jnp.zeros((80, D - 256), BF16)
    grad = jnp.concatenate([g0[...], g1[...], g2[...], g3[...]], 0)
    packed[:256, D : 2 * D] = grad
    arrive(own_a, a.at[pl.ds(0, 192), :], sems.at[1])
    grad_attended = dot_nt(grad, a[...]).astype(BF16)
    query, key, value = projected[:, :256], projected[:, 256:512], projected[:, 512:]
    grad_query, grad_key, grad_value = None, None, None
    for h in range(HEADS_OWN):
        mask = head_mask(h)
        query_part, grad_part = query * mask, grad_attended * mask
        scores = dot_nt(query_part, key) * SCALE
        raised = jnp.exp(scores - jnp.max(scores, -1, keepdims=True))
        probs = raised / jnp.sum(raised, -1, keepdims=True)
        grad_probs = dot_nt(grad_part, value)
        grad_scores = probs * (grad_probs - jnp.sum(grad_probs * probs, -1, keepdims=True))
        grad_scores = grad_scores.astype(BF16)
        parts = (
            dot(grad_scores, key * mask),
            dot_tn(grad_scores, query_part),
            dot_tn(probs.astype(BF16), grad_part),
        )
        if h == 0:
            grad_query, grad_key, grad_value = parts
        else:
            grad_query, grad_key, grad_value = (
                grad_query + parts[0],
                grad_key + parts[1],
                grad_value + parts[2],
            )
    grad_projected = jnp.concatenate([grad_query * SCALE, grad_key * SCALE, grad_value], 1).astype(BF16)
    packed[:256, :D] = grad_projected
    arrive(own_w.at[rows], w, sems.at[0])
    grad_normed = dot_nt(grad_projected, w[...].reshape(D, D))
    result = grad_normed.astype(BF16)
    for k, out in enumerate((n0, n1, n2, n3)):
        out[...] = result[k * T : (k + 1) * T, :]
    gain = jnp.sum(grad_normed * kept[:, :D].astype(F32), 0, keepdims=True)
    upper, lower = split_pair(gain / small[section, 96:97, :].astype(F32))
    place = iota((16, D), 0)
    packed[256:272, :D] = jnp.where(place == 0, upper, jnp.where(place == 1, lower, 0.0)).astype(BF16)
    named = (iota((16, D), 1) == 96) & (iota((16, D), 0) < 2)
    packed[256:272, D : 2 * D] = jnp.where(named, 1.0, 0.0).astype(BF16)


def input_grad(section, n0, n1, n2, n3, h, grad_middle, small):
    grad_normed = (n0[...].astype(F32) + n1[...].astype(F32)) + (n2[...].astype(F32) + n3[...].astype(F32))
    unit, inverse = norm_parts(h)
    return grad_middle[...] + norm_back(grad_normed, small[section, 96:97, :].astype(F32), unit, inverse)


def input_backward_next(ids, n0, n1, n2, n3, grad_middle, small, result, held, grad_out, out):
    h = result[...].astype(BF16).astype(F32)
    grad = input_grad(1, n0, n1, n2, n3, h, grad_middle, small).astype(BF16).astype(F32)
    grad_out[...] = grad
    rows = jnp.concatenate([grad, grad], 0) * held[: 2 * T, 0:1]
    send_to_holders(to_packed(held[2 * T : 2 * T + 1, :META], rows.astype(BF16)), out, 0)


def input_backward_last(ids, n0, n1, n2, n3, inputs, grad_middle, small, grad_two, one, two, stays, leaves):
    grad_one = input_grad(0, n0, n1, n2, n3, inputs[ids[0], 0], grad_middle, small)
    mine = ids[0] == 0
    stays[0] = jnp.where(mine, one[...], two[...])
    leaves[0] = jnp.where(mine, two[...], one[...])
    stays[1] = jnp.where(mine, grad_one, grad_two[...])
    leaves[1] = jnp.where(mine, grad_two[...], grad_one)


def gather_operands(parts, mine, one, r_one, two, r_two, held, sems):
    for n, part in enumerate(parts):
        fetch(mine, one.at[part], two.at[part], held.at[n, pl.ds(0, 320), :], sems.at[n, 0])
        fetch(mine, r_one.at[part], r_two.at[part], held.at[n, pl.ds(320, 320), :], sems.at[n, 1])


def wait_operands(places, one, held, sems):
    for n in places:
        arrive(one.at[0], held.at[n, pl.ds(0, 320), :], sems.at[n, 0])
        arrive(one.at[0], held.at[n, pl.ds(320, 320), :], sems.at[n, 1])


def outer_grads(ids, one, r_one, two, r_two, before, after, held, sems):
    gather_operands((0, 5, 2, 3), ids[0] == 0, one, r_one, two, r_two, held, sems)
    wait_operands((0, 1), one, held, sems)
    value = dot_tn(held[0], held[1]).astype(BF16)
    before[:, :HALF] = value[:, :HALF]
    after[:, :HALF] = value[:, HALF:]
    wait_operands((2, 3), one, held, sems)
    value = dot_tn(held[2], held[3]).astype(BF16)
    before[:HALF, HALF:] = value[:HALF, :HALF]
    before[HALF:, HALF:] = value[:HALF, HALF:]
    after[:HALF, HALF:] = value[HALF:, :HALF]
    after[HALF:, HALF:] = value[HALF:, HALF:]


def inner_grads(ids, one, r_one, two, r_two, grad_in, grad_out, held, result, sems, out_sems):
    j = ids[1] & 1
    gather_operands((0, 4, 1, 3), ids[0] == 0, one, r_one, two, r_two, held, sems)
    for n, grad in enumerate((grad_in, grad_out)):
        wait_operands((2 * n, 2 * n + 1), one, held, sems)
        result[n] = dot_tn(held[2 * n], held[2 * n + 1])
        move(result.at[n], grad.at[j], out_sems.at[n])
    for n, grad in enumerate((grad_in, grad_out)):
        arrive(result.at[n], grad.at[j], out_sems.at[n])


def fill_grads(ids, low, high, _in, _out, grad_in, grad_out, result, sems):
    other = 1 - (ids[1] & 1)
    for n, piece in enumerate((low, high)):
        place = slice(n * HALF, (n + 1) * HALF)
        result[0, :, place] = piece[:, :HALF].astype(F32)
        result[1, place, :HALF] = piece[:HALF, HALF:].astype(F32)
        result[1, place, HALF:] = piece[HALF:, HALF:].astype(F32)
    for n, grad in enumerate((grad_in, grad_out)):
        move(result.at[n], grad.at[other], sems.at[n])
    for n, grad in enumerate((grad_in, grad_out)):
        arrive(result.at[n], grad.at[other], sems.at[n])


def shared_weight_grads(ids, p0, p1, rp0, rp1, out, packed, sems):
    mine = ids[0] == 0
    fetch(mine, p0, p1, packed.at[0], sems.at[0])
    fetch(mine, rp0, rp1, packed.at[1], sems.at[1])
    arrive(p0, packed.at[0], sems.at[0])
    arrive(p0, packed.at[1], sems.at[1])
    grad_qkv, grad_attn, extra = None, None, None
    for m in range(2):
        whole = (
            dot_tn(packed[m, :256, 2 * D : 3 * D], packed[m, :256, :D]),
            dot_tn(packed[m, :256, 3 * D :], packed[m, :256, D : 2 * D]),
            dot_tn(packed[m, 272:, :D], packed[m, 272:, D : D + 128])
            + dot_tn(packed[m, 272:, :D], packed[m, 272:, D + 128 : D + 256])
            + dot_tn(packed[m, 256:272, :D], packed[m, 256:272, D : D + 128]),
        )
        if m == 0:
            grad_qkv, grad_attn, extra = whole
        else:
            grad_qkv, grad_attn, extra = grad_qkv + whole[0], grad_attn + whole[1], extra + whole[2]
    middle = grad_qkv[:, 128:256] + extra
    out[:, :48, :128] = grad_qkv[:, :128].astype(BF16).reshape(N_EXPERT, 48, 128)
    out[:, :48, 128:256] = middle.astype(BF16).reshape(N_EXPERT, 48, 128)
    out[:, :48, 256:] = grad_qkv[:, 256:].astype(BF16).reshape(N_EXPERT, 48, 512)
    row, column = iota((256, 256), 0), iota((256, 256), 1)
    spread = ((row & 15) < 12) & (column == (row >> 4) * 12 + (row & 15))
    spread = jnp.where(spread, 1.0, 0.0).astype(BF16)
    out[:, 48:, :] = dot(spread, grad_attn.astype(BF16)).astype(BF16).reshape(N_EXPERT, 16, D)


def sum_shared(ids, arrived, out, attn, total):
    me = ids[1]
    summed = arrived[0].astype(F32)
    for n in range(1, N_EXPERT):
        summed = summed + arrived[n].astype(F32)
    total[...] = summed
    for s in range(N_SHARD):
        out[(s - me) & (N_SHARD - 1), :12, :] = total[s * 12 : s * 12 + 12, :]
    attn[...] = total[48:, :]


def finish(ids, q0, q1, q2, q3, attn_in, stays, arrives, qkv, attn, one, two, router, acts, grads, held):
    mine, me = ids[0], ids[1]
    acts[mine] = stays[0]
    acts[1 - mine] = arrives[0]
    grads[mine] = stays[1]
    grads[1 - mine] = arrives[1]
    attn[...] = attn_in[:12, :]
    for k, piece in enumerate((q0, q1, q2, q3)):
        held[(me - k) & (N_SHARD - 1)] = piece[...]
    total = None
    for a in range(N_SHARD):
        for j in range(3):
            qkv[:, j * D + a * 192 : j * D + a * 192 + 192] = held[a, :12, j * 256 : j * 256 + 192]
        part = held[a, :12, 128:256]
        total = part if total is None else total + part
    diagonal = iota((12, 12), 0) == iota((12, 12), 1)
    one[...] = jnp.sum(jnp.where(diagonal, total[:, 96:97], 0.0), 0, keepdims=True)
    two[...] = jnp.sum(jnp.where(diagonal, total[:, 97:98], 0.0), 0, keepdims=True)
    router[...] = total[:, 64:96]


def along(value, axis, by):
    count = lax.axis_size(axis)
    return lax.ppermute(value, axis, [(i, (i + by) % count) for i in range(count)])


def gather_shards(value):
    return [value] + [along(value, "shard", k) for k in range(1, N_SHARD)]


def return_shards(pieces):
    return [pieces[0]] + [along(pieces[k], "shard", -k) for k in range(1, N_SHARD)]


def send_shards(pieces):
    return [pieces[0]] + [along(pieces[k], "shard", k) for k in range(1, N_SHARD)]


def exchange(value):
    rows = value.size // (N_ALL * 128)
    return lax.all_to_all(value.reshape(N_ALL, rows, 128), ("expert", "shard"), 0, 0, tiled=True)


def swap(value):
    return lax.ppermute(value, "section", [(0, 1), (1, 0)])


def up(value):
    return lax.ppermute(value, "section", [(0, 1)])


def down(value):
    return lax.ppermute(value, "section", [(1, 0)])


def after(first, *values):
    return lax.optimization_barrier((first, *values))


def dma(*shape):
    return pltpu.SemaphoreType.DMA(shape)


def local(inputs, cotangent, w_qkv, w_attn, gain_one, gain_two, router, w_in, w_out, routes):
    section = lax.axis_index("section")
    me = lax.axis_index("shard")
    ids = jnp.stack([section, me]).astype(jnp.int32)
    rows_shape = ((T, D), BF16)
    wide_shape = ((T, D), F32)
    per_expert = N_SHARD * GROUP
    w_scratch = pltpu.VMEM((N_SHARD, 192, D), BF16)
    expert_scratch = [pltpu.VMEM((D, 2 * D), BF16), pltpu.VMEM((2 * D, D), BF16)]
    staged_scratch = pltpu.VMEM((N_SHARD, ORDERED, 128), BF16)

    place = jnp.arange(ORDERED, dtype=jnp.int32)
    source = ((place % GROUP) // CAP) * SIDE + (place // GROUP) * CAP + place % CAP
    arriving = jnp.arange(N_EXPERT * SIDE, dtype=jnp.int32)
    order = (source[:, None] == arriving[None, :]).astype(BF16)
    back_order = (source[None, :] == arriving[:, None]).astype(BF16)

    p0, p1, p2, p3 = call(
        begin,
        [((1344, 128), BF16)] * 4,
        [ids, inputs, w_qkv[0], gain_one, gain_two, router[0].T],
        [pltpu.VMEM((T, D), F32), pltpu.VMEM((3, 192, D), BF16), pltpu.VMEM((1, 192), BF16), pltpu.VMEM((1, 192), BF16), dma(6)],
        anywhere=(1, 2, 3, 4),
        mib=56,
    )
    square = ((D, D), BF16)
    keep, to_after, to_before = call(
        split_experts,
        [((2, D, D), BF16), square, square],
        [ids, w_in[0], w_out[0]],
        [dma(8)],
        anywhere=(1, 2),
        outs_anywhere=(0, 1, 2),
    )
    own_routes = routes.reshape(2, T, 2)
    other_routes = swap(own_routes)
    p0, p1, p2, p3 = send_shards([p0, p1, p2, p3])
    p0, p1, p2, order, back_order, keep, other_routes = after(
        p0, p1, p2, order, back_order, keep, other_routes
    )
    own_w, units = call(
        join,
        [((5, 192, D), BF16), ((4 * T, D), BF16)],
        [ids, p0, p1, p2, p3],
        [pltpu.VMEM((N_SHARD, 64, 256), BF16)],
    )
    other_w = swap(own_w)
    own_a, own_w = after(w_attn[0], own_w)
    other_a = swap(own_a)
    weights = (own_w, other_w, own_a, other_a)
    attention_scratch = [w_scratch, pltpu.VMEM((192, D), BF16), dma(5)]

    o0, o1, o2, o3, kept_one, projected_one, small, h_one = call(
        attention_one,
        [rows_shape] * 4 + [((256, D + 256), BF16), ((256, D), BF16), ((2, 128, D), BF16), wide_shape],
        [ids, units, *weights, inputs],
        attention_scratch,
        anywhere=(2, 3, 4, 5, 6),
        mib=24,
    )
    keep = after(keep, o0)[0]
    other_keep = swap(keep)
    packed_shape = ((N_EXPERT, N_SHARD, SIDE, 128), BF16)
    state_shape = ((2 * T + 8, META + D), F32)
    half_shape = ((3, per_expert, D), BF16)
    slope_shape = ((2, per_expert, D), BF16)
    both_shape = ((6, per_expert, D), BF16)
    pieces = return_shards([o0, o1, o2, o3])
    to_after, to_before = after(to_after, to_before, *pieces)[:2]
    own_before, own_after = along(to_after, "shard", 1), along(to_before, "shard", -1)
    sent, state_one = call(
        functools.partial(dispatch, 0),
        [packed_shape, state_shape],
        [ids, h_one, *pieces, small, own_routes, other_routes],
    )
    arrived = exchange(sent)
    own_before, own_after = after(own_before, own_after, arrived)[:2]
    experts = (keep, other_keep, own_before, swap(own_before), own_after, swap(own_after))
    sent, fwd_one, slope = call(
        expert_forward,
        [((N_ALL, SIDE, 128), BF16), half_shape, slope_shape],
        [ids, arrived, order, back_order, *experts],
        [*expert_scratch, staged_scratch, dma(3), dma(5)],
        anywhere=(4, 5, 6, 7, 8, 9),
        mib=24,
    )
    result_one, taken, normed = call(
        combine_next,
        [wide_shape, ((2 * T, D), BF16), rows_shape],
        [ids, exchange(sent).reshape(packed_shape[0]), state_one, small],
    )

    o0, o1, o2, o3, kept_two, projected_two = call(
        attention_two,
        [rows_shape] * 4 + [((256, D + 256), BF16), ((256, D), BF16)],
        [ids, *gather_shards(normed), *weights],
        attention_scratch,
        anywhere=(5, 6, 7, 8),
        mib=24,
    )
    double_shape = ((N_EXPERT, N_SHARD, 2 * SIDE, 128), BF16)
    sent, state_two = call(
        functools.partial(dispatch, 1),
        [double_shape, state_shape],
        [ids, result_one, *return_shards([o0, o1, o2, o3]), small, own_routes, other_routes, cotangent],
    )
    sent, both_two = call(
        expert_both,
        [((N_ALL, 2 * SIDE, 128), BF16), both_shape],
        [ids, exchange(sent), order, back_order, *experts],
        [*expert_scratch, staged_scratch, staged_scratch, dma(3), dma(5)],
        anywhere=(4, 5, 6, 7, 8, 9),
        mib=28,
    )
    routed_shape = ((T + 16, D + 256), BF16)
    returned, r_both_two = after(exchange(sent), up(both_two))
    result_two, grad_middle, sent, routed = call(
        turn,
        [wide_shape, wide_shape, rows_shape, routed_shape],
        [ids, returned.reshape(double_shape[0]), state_two, cotangent, small],
    )

    def attention_grads(s, rows, kept, projected, routed):
        return call(
            functools.partial(attention_backward, s),
            [rows_shape] * 4 + [((352, 3 * D + 256), BF16)],
            [ids, *rows, routed, small, kept, projected, *weights],
            [w_scratch, pltpu.VMEM((256, D), BF16), dma(2)],
            anywhere=(9, 10, 11, 12),
            mib=24,
        )

    n0, n1, n2, n3, packed_two = attention_grads(1, gather_shards(sent), kept_two, projected_two, routed)
    grad_two, sent = call(
        input_backward_next,
        [wide_shape, packed_shape],
        [ids, *return_shards([n0, n1, n2, n3]), grad_middle, small, result_one, state_one],
    )

    arrived, r_packed_two = after(exchange(sent), up(packed_two))
    sent, both_one = call(
        expert_backward,
        [((N_ALL, SIDE, 128), BF16), both_shape],
        [ids, arrived, order, back_order, slope, fwd_one, *experts],
        [*expert_scratch, staged_scratch, pltpu.VMEM(*slope_shape), dma(3), dma(5), dma(2)],
        anywhere=(4, 5, 6, 7, 8, 9, 10, 11),
        mib=28,
    )
    returned, r_both_one = after(exchange(sent), down(both_one))
    grad_middle, sent, routed = call(
        middle_backward,
        [wide_shape, rows_shape, routed_shape],
        [ids, returned.reshape(packed_shape[0]), state_one, grad_two, taken, small],
    )
    n0, n1, n2, n3, packed_one = attention_grads(0, gather_shards(sent), kept_one, projected_one, routed)

    r_packed_one = down(packed_one)
    both_one = after(both_one, packed_one)[0]
    operands = [both_one, r_both_one, both_two, r_both_two]
    held_scratch = pltpu.VMEM((4, 2 * per_expert, D), BF16)
    grad_before, grad_after = call(
        outer_grads,
        [square] * 2,
        [ids, *operands],
        [held_scratch, dma(4, 2)],
        anywhere=(1, 2, 3, 4),
        mib=24,
    )
    pieces = return_shards([n0, n1, n2, n3])
    r_packed_one = after(r_packed_one, grad_before, *pieces)[0]
    grad_before, grad_after = after(grad_before, grad_after, *pieces)[:2]
    low, high = along(grad_before, "shard", -1), along(grad_after, "shard", 1)
    payload = call(
        shared_weight_grads,
        [((N_EXPERT, 64, D), BF16)],
        [ids, packed_one, packed_two, r_packed_one, r_packed_two],
        [pltpu.VMEM((2, 352, 3 * D + 256), BF16), dma(2)],
        anywhere=(1, 2, 3, 4),
        mib=24,
    )[0]
    stays, leaves = call(
        input_backward_last,
        [((2, T, D), F32)] * 2,
        [ids, *pieces, inputs, grad_middle, small, grad_two, result_one, result_two],
    )
    summed = lax.all_to_all(payload, "expert", 0, 0, tiled=True)
    grads_shape = ((2, D, D), F32)
    grad_in, grad_out = call(
        inner_grads,
        [grads_shape] * 2,
        [ids, *operands],
        [held_scratch, pltpu.VMEM((2, D, D), F32), dma(4, 2), dma(2)],
        anywhere=(1, 2, 3, 4),
        outs_anywhere=(0, 1),
        mib=48,
    )
    summed, grad_in = after(summed, grad_in)
    arrives = swap(leaves)
    shares, attn = call(
        sum_shared,
        [((N_SHARD, 16, D), F32), ((16, D), F32)],
        [ids, summed],
        [pltpu.VMEM((64, D), F32)],
    )
    grad_in, grad_out = call(
        fill_grads,
        [grads_shape] * 2,
        [ids, low, high, after(grad_in, shares)[0], grad_out],
        [pltpu.VMEM((2, D, D), F32), dma(2)],
        anywhere=(3, 4),
        outs_anywhere=(0, 1),
        aliases={3: 0, 4: 1},
        mib=24,
    )
    pairs = [
        (e * N_SHARD + s, (N_SHARD * s + e // N_SHARD) * N_SHARD + e % N_SHARD)
        for e in range(N_EXPERT)
        for s in range(N_SHARD)
    ]
    attn_in = lax.ppermute(attn, ("expert", "shard"), pairs)
    q0, q1, q2, q3, attn_in, grad_in, grad_out = after(*send_shards(shares), attn_in, grad_in, grad_out)
    grad_qkv, grad_attn, grad_one, grad_two, grad_router, acts, grads = call(
        finish,
        [
            ((12, 3 * D), F32),
            ((12, D), F32),
            ((1, 12), F32),
            ((1, 12), F32),
            ((12, 32), F32),
            ((2, T, D), F32),
            ((2, T, D), F32),
        ],
        [ids, q0, q1, q2, q3, attn_in, stays, arrives],
        [pltpu.VMEM((N_SHARD, 16, D), F32)],
    )
    return (
        acts.reshape(1, 2, 1, T, D),
        grads.reshape(1, 2, 1, T, D),
        grad_qkv[None],
        grad_attn[None],
        grad_one,
        grad_two,
        grad_router[None],
        grad_in[None],
        grad_out[None],
    )


def solution(mesh):
    return jax.shard_map(
        local,
        mesh=mesh,
        in_specs=(
            P(None, "expert", "shard", None),
            P(None, "expert", "shard", None),
            P("section", "shard", None),
            P("section", "shard", None),
            P("section", "shard"),
            P("section", "shard"),
            P("section", "shard", None),
            P("section", "expert", None, "shard"),
            P("section", "expert", "shard", None),
            P("section", None, "expert", "shard", None, None),
        ),
        out_specs=(
            P("section", None, "expert", "shard", None),
            P("section", None, "expert", "shard", None),
            P("section", ("expert", "shard"), None),
            P("section", ("expert", "shard"), None),
            P("section", ("expert", "shard")),
            P("section", ("expert", "shard")),
            P("section", ("expert", "shard"), None),
            P("section", "expert", None, "shard"),
            P("section", "expert", "shard", None),
        ),
        check_vma=False,
    )
```

```python
import functools
import math

import jax
import jax.numpy as jnp
from jax import lax
from jax.experimental import pallas as pl
from jax.experimental.pallas import tpu as pltpu
from jax.sharding import PartitionSpec as P

F32 = jnp.float32
BF16 = jnp.bfloat16
D = 768
HEADS_OWN = 3
HDIM = 64
T = 64
CAP = 5
CHUNKS = 6
N_EXPERT = 16
N_SHARD = 4
N_ALL = N_EXPERT * N_SHARD
SIDE = 32
BLOCK = 2 * N_EXPERT * SIDE
GROUP = N_EXPERT * CAP
ORDERED = CHUNKS * GROUP
HALF = D // 2
META = 128
EPS = 1e-06
SCALE = 1.0 / math.sqrt(HDIM)


def dot(a, b):
    return lax.dot_general(a, b, (((1,), (0,)), ((), ())), preferred_element_type=F32)


def dot_nt(a, b):
    return lax.dot_general(a, b, (((1,), (1,)), ((), ())), preferred_element_type=F32)


def dot_tn(a, b):
    return lax.dot_general(a, b, (((0,), (0,)), ((), ())), preferred_element_type=F32)


def iota(shape, dim):
    return lax.broadcasted_iota(jnp.int32, shape, dim)


def call(body, outs, ins, scratch=(), anywhere=(), scalars=1, mib=12, outs_anywhere=(), aliases=None):
    specs = []
    for place in range(len(ins)):
        if place < scalars:
            specs.append(pl.BlockSpec(memory_space=pltpu.SMEM))
        elif place in anywhere:
            specs.append(pl.BlockSpec(memory_space=pltpu.HBM))
        else:
            specs.append(pl.BlockSpec(memory_space=pltpu.VMEM))
    return pl.pallas_call(
        body,
        out_shape=tuple(jax.ShapeDtypeStruct(shape, kind) for shape, kind in outs),
        in_specs=specs,
        out_specs=tuple(
            pl.BlockSpec(memory_space=pltpu.HBM if place in outs_anywhere else pltpu.VMEM)
            for place in range(len(outs))
        ),
        scratch_shapes=list(scratch),
        input_output_aliases=aliases or {},
        compiler_params=pltpu.CompilerParams(vmem_limit_bytes=mib * 1024 * 1024),
    )(*ins)


def fetch(mine, own, other, target, sem):
    @pl.when(mine)
    def _():
        pltpu.make_async_copy(own, target, sem).start()

    @pl.when(jnp.logical_not(mine))
    def _():
        pltpu.make_async_copy(other, target, sem).start()


def arrive(own, target, sem):
    pltpu.make_async_copy(own, target, sem).wait()


def move(source, target, sem):
    pltpu.make_async_copy(source, target, sem).start()


def norm_parts(rows):
    centered = rows - jnp.mean(rows, -1, keepdims=True)
    inverse = lax.rsqrt(jnp.mean(centered * centered, -1, keepdims=True) + EPS)
    return centered * inverse, inverse


def norm_back(grad, gain, unit, inverse):
    scaled = grad * gain
    return inverse * (
        scaled
        - jnp.mean(scaled, -1, keepdims=True)
        - unit * jnp.mean(scaled * unit, -1, keepdims=True)
    )


def split_pair(values):
    upper = values.astype(BF16)
    return upper, (values - upper.astype(F32)).astype(BF16)


def row_of(column):
    size = column.shape[0]
    diagonal = iota((size, size), 0) == iota((size, size), 1)
    return jnp.sum(jnp.where(diagonal, column, 0.0), 0, keepdims=True)


def slots_of(route_column):
    named = (iota((2 * T, 32), 1) == route_column).astype(F32)
    earlier = ((iota((2 * T, 2 * T), 1) & (T - 1)) < (iota((2 * T, 2 * T), 0) & (T - 1))).astype(BF16)
    before = dot(earlier, named.astype(BF16))
    return route_column.astype(F32) * CAP + jnp.sum(before * named, 1, keepdims=True)


def packed_place(index):
    within = index & (SIDE - 1)
    chunk = (within * 205) >> 10
    return (index >> 5) * CAP + within - chunk * CAP, chunk


def to_packed(slot_row, rows):
    slot, chunk = packed_place(iota((BLOCK, 2 * T), 0))
    hit = slot.astype(F32) == slot_row
    total = None
    for c in range(CHUNKS):
        mask = jnp.where(hit & (chunk == c), 1.0, 0.0).astype(BF16)
        part = dot(mask, rows[:, c * 128 : (c + 1) * 128])
        total = part if total is None else total + part
    return total.astype(BF16)


def from_packed(slot_column, packed):
    slot, chunk = packed_place(iota((2 * T, BLOCK), 1))
    hit = slot.astype(F32) == slot_column
    parts = []
    for c in range(CHUNKS):
        mask = jnp.where(hit & (chunk == c), 1.0, 0.0).astype(BF16)
        parts.append(dot(mask, packed))
    return jnp.concatenate(parts, 1)


def send_to_holders(packed, out_ref, start):
    blocks = packed.reshape(N_EXPERT, 2, SIDE, 128)
    for s in range(N_SHARD):
        out_ref[:, s, start : start + SIDE, :] = blocks[:, s % 2]


def sum_of_holders(in_ref, start):
    parts = []
    for j in range(2):
        total = in_ref[:, j, start : start + SIDE, :].astype(F32)
        total = total + in_ref[:, j + 2, start : start + SIDE, :].astype(F32)
        parts.append(total.astype(BF16).reshape(N_EXPERT, 1, SIDE, 128))
    return jnp.concatenate(parts, 1).reshape(BLOCK, 128)


def group_of(packed_ref, group, start):
    rows = packed_ref[group * N_EXPERT : (group + 1) * N_EXPERT, start : start + SIDE, :]
    return rows.reshape(N_EXPERT * SIDE, 128)


def order_pair(order, first, second):
    return dot(order, jnp.concatenate([first, second], 1)).astype(BF16)


def place_rows(ordered, half, group, kept_ref):
    for c in range(CHUNKS):
        kept_ref[group * GROUP : (group + 1) * GROUP, c * 128 : (c + 1) * 128] = ordered[
            c * GROUP : (c + 1) * GROUP, half * 128 : half * 128 + 128
        ]


def stage_rows(rows, staged_ref):
    for group in range(N_SHARD):
        for c in range(CHUNKS):
            staged_ref[group, c * GROUP : (c + 1) * GROUP, :] = rows[
                group * GROUP : (group + 1) * GROUP, c * 128 : (c + 1) * 128
            ]


def unorder_pair(back_order, first, second, out_ref, places):
    packed = dot(back_order, jnp.concatenate([first, second], 1)).astype(BF16)
    for half, (group, start) in enumerate(places):
        out_ref[group * N_EXPERT : (group + 1) * N_EXPERT, start : start + SIDE, :] = packed[
            :, half * 128 : half * 128 + 128
        ].reshape(N_EXPERT, SIDE, 128)


def head_mask(h):
    lane = iota((1, 256), 1)
    return ((lane >= h * HDIM) & (lane < (h + 1) * HDIM)).astype(BF16)


def fold(value):
    half = value.shape[0] // 2
    return jnp.concatenate([value[:half, :], value[half:, :]], 1)


def unfold(value):
    return jnp.concatenate([value[:, :64], value[:, 64:]], 0)


def begin(ids, inputs, w, gain_one, gain_two, router, p0, p1, p2, p3, h, held, thin_one, thin_two, sems):
    mine, me = ids[0], ids[1]
    move(inputs.at[mine, 0], h, sems.at[0])
    for j in range(3):
        move(w.at[:, pl.ds(j * D, D)], held.at[j], sems.at[1 + j])
    move(gain_one, thin_one, sems.at[4])
    move(gain_two, thin_two, sems.at[5])
    arrive(gain_one, thin_one, sems.at[4])
    arrive(gain_two, thin_two, sems.at[5])
    rows = iota((32, 192), 0)
    gains = jnp.where(rows == 0, thin_one[...].astype(F32), jnp.where(rows == 1, thin_two[...].astype(F32), 0.0))
    thin = jnp.concatenate([router[...], gains.astype(BF16)], 0)
    arrive(inputs.at[mine, 0], h, sems.at[0])
    unit, _ = norm_parts(h[...])
    unit = unit.astype(BF16)
    for j in range(3):
        arrive(w.at[:, pl.ds(j * D, D)], held.at[j], sems.at[1 + j])
    for piece in (p0, p1, p2, p3):
        piece[864:928, :] = thin[:, :128]
        piece[928:960, :] = fold(thin[:, 128:])
        for c in range(CHUNKS):
            piece[960 + 64 * c : 1024 + 64 * c, :] = unit[:, c * 128 : (c + 1) * 128]
    for s in range(N_SHARD):
        for k, piece in enumerate((p0, p1, p2, p3)):

            @pl.when(((s - me) & (N_SHARD - 1)) == k)
            def _(s=s, piece=piece):
                parts = [held[j, :, s * 192 : s * 192 + 192] for j in range(3)]
                for j in range(3):
                    piece[192 * j : 192 * j + 192, :] = parts[j][:, :128]
                piece[576:768, :] = jnp.concatenate([parts[0][:, 128:], parts[1][:, 128:]], 1)
                piece[768:864, :] = fold(parts[2][:, 128:])


def join(ids, p0, p1, p2, p3, out, units, held):
    me = ids[1]
    none = jnp.zeros((192, 64), BF16)
    for k, piece in enumerate((p0, p1, p2, p3)):
        place = (me - k) & (N_SHARD - 1)
        rest = piece[576:768, :]
        rests = (rest[:, :64], rest[:, 64:], unfold(piece[768:864, :]))
        for j in range(3):
            out[place, :, 256 * j : 256 * j + 128] = piece[192 * j : 192 * j + 192, :]
            out[place, :, 256 * j + 128 : 256 * j + 256] = jnp.concatenate([rests[j], none], 1)
        held[place, :, :128] = piece[864:928, :]
        held[place, :, 128:] = jnp.concatenate([unfold(piece[928:960, :]), none[:64]], 1)
        for c in range(CHUNKS):
            units[k * T : (k + 1) * T, c * 128 : (c + 1) * 128] = piece[960 + 64 * c : 1024 + 64 * c, :]
    out[4] = jnp.zeros((192, D), BF16)
    for a in range(N_SHARD):
        out[4, 64:128, a * 192 : (a + 1) * 192] = held[a, :, :192]


def attend(x, w, a, kept, projected, outs):
    kept[:, :D] = x
    whole = dot(x, w[...].reshape(D, D)).astype(BF16)
    projected[...] = whole
    query, key, value = whole[:, :256], whole[:, 256:512], whole[:, 512:]
    attended = None
    for h in range(HEADS_OWN):
        mask = head_mask(h)
        scores = dot_nt(query * mask, key) * SCALE
        raised = jnp.exp(scores - jnp.max(scores, -1, keepdims=True))
        probs = (raised / jnp.sum(raised, -1, keepdims=True)).astype(BF16)
        part = dot(probs, value * mask)
        attended = part if attended is None else attended + part
    attended = attended.astype(BF16)
    kept[:, D:] = attended
    result = dot(attended[:, :192], a[...]).astype(BF16)
    for k, out in enumerate(outs):
        out[...] = result[k * T : (k + 1) * T, :]


def attention_one(ids, units, own_w, other_w, own_a, other_a, inputs, o0, o1, o2, o3, kept, projected, small, h, w, a, sems):
    mine = ids[0] == 0
    rows, extra = pl.ds(0, 4), pl.ds(0, 128)
    fetch(mine, own_w.at[4, extra], other_w.at[4, extra], small.at[0], sems.at[2])
    fetch(mine, own_w.at[rows], other_w.at[rows], w, sems.at[0])
    fetch(mine, own_a, other_a, a, sems.at[1])
    fetch(mine, other_w.at[4, extra], own_w.at[4, extra], small.at[1], sems.at[3])
    move(inputs.at[ids[0], 0], h, sems.at[4])
    arrive(own_w.at[4, extra], small.at[0], sems.at[2])
    x = (units[...].astype(F32) * small[0, 96:97, :].astype(F32)).astype(BF16)
    arrive(own_w.at[rows], w, sems.at[0])
    arrive(own_a, a, sems.at[1])
    attend(x, w, a, kept, projected, (o0, o1, o2, o3))
    arrive(own_w.at[4, extra], small.at[1], sems.at[3])
    arrive(inputs.at[ids[0], 0], h, sems.at[4])


def attention_two(ids, x0, x1, x2, x3, own_w, other_w, own_a, other_a, o0, o1, o2, o3, kept, projected, w, a, sems):
    mine = ids[0] == 1
    rows = pl.ds(0, 4)
    fetch(mine, own_w.at[rows], other_w.at[rows], w, sems.at[0])
    fetch(mine, own_a, other_a, a, sems.at[1])
    x = jnp.concatenate([x0[...], x1[...], x2[...], x3[...]], 0)
    arrive(own_w.at[rows], w, sems.at[0])
    arrive(own_a, a, sems.at[1])
    attend(x, w, a, kept, projected, (o0, o1, o2, o3))


def dispatch(section, ids, h, o0, o1, o2, o3, small, own_routes, other_routes, *refs):
    if section == 1:
        seed, out, held = refs
        start = h[...].astype(BF16).astype(F32)
    else:
        out, held = refs
        start = h[...]
    middle = start + (
        (o0[...].astype(F32) + o1[...].astype(F32)) + (o2[...].astype(F32) + o3[...].astype(F32))
    )
    held[:T, META:] = middle
    held[T:, META:] = jnp.zeros((T + 8, D), F32)
    unit, _ = norm_parts(middle)
    normed = (unit * small[section, 97:98, :].astype(F32)).astype(BF16)
    route = jnp.where(ids[0] == section, own_routes[ids[0]], other_routes[ids[0]])
    column = jnp.concatenate([route[:, 0:1], route[:, 1:2]], 0)
    slot_column = slots_of(column)
    slot_row = row_of(slot_column)
    send_to_holders(to_packed(slot_row, jnp.concatenate([normed, normed], 0)), out, 0)
    logits = dot_nt(normed, small[section])
    logits = jnp.concatenate([logits, logits], 0)
    lanes = iota((2 * T, 128), 1)
    chosen = jnp.sum(jnp.where(lanes == column + 64, logits, 0.0), 1, keepdims=True)
    one, two = chosen[:T], chosen[T:]
    top = jnp.maximum(one, two)
    one, two = jnp.exp(one - top), jnp.exp(two - top)
    total = one + two
    gates = jnp.concatenate([one / total, two / total], 0)
    held[: 2 * T, :META] = jnp.where(
        lanes == 0, gates, jnp.where(lanes == 1, slot_column, column.astype(F32) + 64.0)
    )
    held[2 * T :, :META] = jnp.broadcast_to(slot_row, (8, META))
    if section == 1:
        grad = seed[ids[0], 0]
        rows = jnp.concatenate([grad, grad], 0) * gates
        send_to_holders(to_packed(slot_row, rows.astype(BF16)), out, SIDE)


def split_experts(ids, w_in, w_out, keep, after, before, sems):
    j = ids[1] & 1
    other = 1 - j
    low, high = pl.ds(0, HALF), pl.ds(HALF, HALF)
    copies = [(w_in.at[j], keep.at[0]), (w_out.at[j], keep.at[1])]
    for part, target in ((low, after), (high, before)):
        copies.append((w_in.at[other, :, part], target.at[:, low]))
        copies.append((w_out.at[other, part, low], target.at[low, high]))
        copies.append((w_out.at[other, part, high], target.at[high, high]))
    for n, (source, target) in enumerate(copies):
        move(source, target, sems.at[n])
    for n, (source, target) in enumerate(copies):
        arrive(source, target, sems.at[n])


def expert_copies(keep, before, after, w_in, w_out):
    low, high = pl.ds(0, HALF), pl.ds(HALF, HALF)
    inner = [(keep, lambda r: r.at[0], w_in.at[:, pl.ds(0, D)])]
    outer = [(keep, lambda r: r.at[1], w_out.at[pl.ds(0, D), :])]
    for n, pair in enumerate((before, after)):
        place = pl.ds(D + n * HALF, HALF)
        inner.append((pair, lambda r: r.at[:, low], w_in.at[:, place]))
        outer.append((pair, lambda r: r.at[low, high], w_out.at[place, low]))
        outer.append((pair, lambda r: r.at[high, high], w_out.at[place, high]))
    return inner, outer


def load_experts(copies, mine, sems):
    for n, ((own, other), part, target) in enumerate(copies):
        fetch(mine, part(own), part(other), target, sems.at[n])


def wait_experts(copies, sems):
    for n, ((own, _), part, target) in enumerate(copies):
        arrive(part(own), target, sems.at[n])


def gelu_parts(up):
    share = 0.5 * (1.0 + lax.erf(up * math.sqrt(0.5)))
    return (up * share).astype(BF16), share + up * jnp.exp(-0.5 * up * up) * (1.0 / math.sqrt(2.0 * math.pi))


def expert_forward(ids, arrived, order, back_order, k0, k1, b0, b1, a0, a1, out, kept, slope, w_in, w_out, staged, sems_in, sems_out):
    inner, outer = expert_copies((k0, k1), (b0, b1), (a0, a1), w_in, w_out)
    load_experts(inner, ids[0] == 0, sems_in)
    load_experts(outer, ids[0] == 0, sems_out)
    for pair in (0, 2):
        ordered = order_pair(order[...], group_of(arrived, pair, 0), group_of(arrived, pair + 1, 0))
        place_rows(ordered, 0, pair, kept.at[0])
        place_rows(ordered, 1, pair + 1, kept.at[0])
    wait_experts(inner, sems_in)
    result = None
    for q in range(2):
        hidden, scale = gelu_parts(dot(kept[0], w_in[:, q * D : (q + 1) * D]))
        kept[1 + q] = hidden
        slope[q] = scale.astype(BF16)
        if q == 0:
            wait_experts(outer, sems_out)
        part = dot(hidden, w_out[q * D : (q + 1) * D, :])
        result = part if result is None else result + part
    stage_rows(result.astype(BF16), staged)
    for pair in (0, 2):
        unorder_pair(back_order[...], staged[pair], staged[pair + 1], out, ((pair, 0), (pair + 1, 0)))


def expert_both(ids, arrived, order, back_order, k0, k1, b0, b1, a0, a1, out, kept, w_in, w_out, staged, staged_back, sems_in, sems_out):
    inner, outer = expert_copies((k0, k1), (b0, b1), (a0, a1), w_in, w_out)
    load_experts(inner, ids[0] == 1, sems_in)
    load_experts(outer, ids[0] == 1, sems_out)
    for group in range(N_SHARD):
        ordered = order_pair(order[...], group_of(arrived, group, 0), group_of(arrived, group, SIDE))
        place_rows(ordered, 0, group, kept.at[0])
        place_rows(ordered, 1, group, kept.at[3])
    wait_experts(inner, sems_in)
    wait_experts(outer, sems_out)
    result, back = None, None
    for q in range(2):
        part_in, part_out = w_in[:, q * D : (q + 1) * D], w_out[q * D : (q + 1) * D, :]
        hidden, scale = gelu_parts(dot(kept[0], part_in))
        kept[1 + q] = hidden
        grad_up = (dot_nt(kept[3], part_out) * scale).astype(BF16)
        kept[4 + q] = grad_up
        parts = (dot(hidden, part_out), dot_nt(grad_up, part_in))
        result = parts[0] if q == 0 else result + parts[0]
        back = parts[1] if q == 0 else back + parts[1]
    stage_rows(result.astype(BF16), staged)
    stage_rows(back.astype(BF16), staged_back)
    for group in range(N_SHARD):
        unorder_pair(back_order[...], staged[group], staged_back[group], out, ((group, 0), (group, SIDE)))


def expert_backward(ids, arrived, order, back_order, slope_in, fwd, k0, k1, b0, b1, a0, a1, out, kept, w_in, w_out, staged, slope, sems_in, sems_out, sems):
    inner, outer = expert_copies((k0, k1), (b0, b1), (a0, a1), w_in, w_out)
    load_experts(outer, ids[0] == 0, sems_out)
    load_experts(inner, ids[0] == 0, sems_in)
    move(slope_in, slope, sems.at[0])
    move(fwd, kept.at[pl.ds(0, 3)], sems.at[1])
    for pair in (0, 2):
        ordered = order_pair(order[...], group_of(arrived, pair, 0), group_of(arrived, pair + 1, 0))
        place_rows(ordered, 0, pair, kept.at[3])
        place_rows(ordered, 1, pair + 1, kept.at[3])
    arrive(slope_in, slope, sems.at[0])
    wait_experts(outer, sems_out)
    back = None
    for q in range(2):
        grad_up = (dot_nt(kept[3], w_out[q * D : (q + 1) * D, :]) * slope[q].astype(F32)).astype(BF16)
        kept[4 + q] = grad_up
        if q == 0:
            wait_experts(inner, sems_in)
        part = dot_nt(grad_up, w_in[:, q * D : (q + 1) * D])
        back = part if q == 0 else back + part
    stage_rows(back.astype(BF16), staged)
    for pair in (0, 2):
        unorder_pair(back_order[...], staged[pair], staged[pair + 1], out, ((pair, 0), (pair + 1, 0)))
    arrive(fwd, kept.at[pl.ds(0, 3)], sems.at[1])


def mixed(rows, held):
    weighted = rows * held[: 2 * T, 0:1]
    return held[:T, META:] + weighted[:T] + weighted[T:]


def combine_next(ids, returned, held, small, result, taken, normed):
    rows = from_packed(held[: 2 * T, 1:2], sum_of_holders(returned, 0))
    taken[...] = rows.astype(BF16)
    total = mixed(rows, held)
    result[...] = total
    unit, _ = norm_parts(total.astype(BF16).astype(F32))
    normed[...] = (unit * small[1, 96:97, :].astype(F32)).astype(BF16)


def middle_grads(section, rows, grad_rows, grad, meta, small, grad_middle, sent, routed):
    gates = meta[: 2 * T, 0:1]
    gate_grads = jnp.sum(jnp.concatenate([grad, grad], 0) * rows, 1, keepdims=True)
    weighted = gates * gate_grads
    mean = weighted[:T] + weighted[T:]
    chosen = gates * (gate_grads - jnp.concatenate([mean, mean], 0))
    lanes = iota((2 * T, 128), 1).astype(F32)
    spread = jnp.where(lanes == meta[: 2 * T, 2:3], chosen, 0.0)
    logits_upper, logits_lower = split_pair(spread[:T] + spread[T:])
    part = dot(logits_upper, small[section]) + dot(logits_lower, small[section])
    grad_normed = part + grad_rows[:T] + grad_rows[T:]
    unit, inverse = norm_parts(meta[:T, META:])
    gain = small[section, 97:98, :].astype(F32)
    value = grad + norm_back(grad_normed, gain, unit, inverse)
    grad_middle[...] = value
    sent[...] = value.astype(BF16)
    upper, lower = split_pair(jnp.sum(grad_normed * unit, 0, keepdims=True))
    routed[:T, :D] = (unit * gain).astype(BF16)
    routed[:T, D : D + 128] = logits_upper
    routed[:T, D + 128 :] = logits_lower
    place = iota((16, D), 0)
    routed[T:, :D] = jnp.where(place == 0, upper, jnp.where(place == 1, lower, 0.0)).astype(BF16)
    named = (iota((16, 128), 1) == 97) & (iota((16, 128), 0) < 2)
    routed[T:, D : D + 128] = jnp.where(named, 1.0, 0.0).astype(BF16)
    routed[T:, D + 128 :] = jnp.zeros((16, 128), BF16)


def turn(ids, returned, held, seed, small, result, grad_middle, sent, routed):
    slot = held[: 2 * T, 1:2]
    rows = from_packed(slot, sum_of_holders(returned, 0))
    result[...] = mixed(rows, held)
    grad_rows = from_packed(slot, sum_of_holders(returned, SIDE))
    middle_grads(1, rows, grad_rows, seed[ids[0], 0], held, small, grad_middle, sent, routed)


def middle_backward(ids, returned, held, grad, taken, small, grad_middle, sent, routed):
    grad_rows = from_packed(held[: 2 * T, 1:2], sum_of_holders(returned, 0))
    middle_grads(0, taken[...].astype(F32), grad_rows, grad[...], held, small, grad_middle, sent, routed)


def attention_backward(section, ids, g0, g1, g2, g3, routed, small, kept, projected, own_w, other_w, own_a, other_a, n0, n1, n2, n3, packed, w, a, sems):
    mine = ids[0] == section
    rows = pl.ds(0, 4)
    fetch(mine, own_a, other_a, a.at[pl.ds(0, 192), :], sems.at[1])
    fetch(mine, own_w.at[rows], other_w.at[rows], w, sems.at[0])
    packed[:256, 2 * D :] = kept[...]
    packed[256:, 2 * D :] = jnp.zeros((96, D + 256), BF16)
    a[192:, :] = jnp.zeros((64, D), BF16)
    packed[272:, : D + 256] = routed[...]
    packed[272:, D + 256 : 2 * D] = jnp.zeros((80, D - 256), BF16)
    grad = jnp.concatenate([g0[...], g1[...], g2[...], g3[...]], 0)
    packed[:256, D : 2 * D] = grad
    arrive(own_a, a.at[pl.ds(0, 192), :], sems.at[1])
    grad_attended = dot_nt(grad, a[...]).astype(BF16)
    query, key, value = projected[:, :256], projected[:, 256:512], projected[:, 512:]
    grad_query, grad_key, grad_value = None, None, None
    for h in range(HEADS_OWN):
        mask = head_mask(h)
        query_part, grad_part = query * mask, grad_attended * mask
        scores = dot_nt(query_part, key) * SCALE
        raised = jnp.exp(scores - jnp.max(scores, -1, keepdims=True))
        probs = raised / jnp.sum(raised, -1, keepdims=True)
        grad_probs = dot_nt(grad_part, value)
        grad_scores = probs * (grad_probs - jnp.sum(grad_probs * probs, -1, keepdims=True))
        grad_scores = grad_scores.astype(BF16)
        parts = (
            dot(grad_scores, key * mask),
            dot_tn(grad_scores, query_part),
            dot_tn(probs.astype(BF16), grad_part),
        )
        if h == 0:
            grad_query, grad_key, grad_value = parts
        else:
            grad_query, grad_key, grad_value = (
                grad_query + parts[0],
                grad_key + parts[1],
                grad_value + parts[2],
            )
    grad_projected = jnp.concatenate([grad_query * SCALE, grad_key * SCALE, grad_value], 1).astype(BF16)
    packed[:256, :D] = grad_projected
    arrive(own_w.at[rows], w, sems.at[0])
    grad_normed = dot_nt(grad_projected, w[...].reshape(D, D))
    result = grad_normed.astype(BF16)
    for k, out in enumerate((n0, n1, n2, n3)):
        out[...] = result[k * T : (k + 1) * T, :]
    gain = jnp.sum(grad_normed * kept[:, :D].astype(F32), 0, keepdims=True)
    upper, lower = split_pair(gain / small[section, 96:97, :].astype(F32))
    place = iota((16, D), 0)
    packed[256:272, :D] = jnp.where(place == 0, upper, jnp.where(place == 1, lower, 0.0)).astype(BF16)
    named = (iota((16, D), 1) == 96) & (iota((16, D), 0) < 2)
    packed[256:272, D : 2 * D] = jnp.where(named, 1.0, 0.0).astype(BF16)


def input_grad(section, n0, n1, n2, n3, h, grad_middle, small):
    grad_normed = (n0[...].astype(F32) + n1[...].astype(F32)) + (n2[...].astype(F32) + n3[...].astype(F32))
    unit, inverse = norm_parts(h)
    return grad_middle[...] + norm_back(grad_normed, small[section, 96:97, :].astype(F32), unit, inverse)


def input_backward_next(ids, n0, n1, n2, n3, grad_middle, small, result, held, grad_out, out):
    h = result[...].astype(BF16).astype(F32)
    grad = input_grad(1, n0, n1, n2, n3, h, grad_middle, small).astype(BF16).astype(F32)
    grad_out[...] = grad
    rows = jnp.concatenate([grad, grad], 0) * held[: 2 * T, 0:1]
    send_to_holders(to_packed(held[2 * T : 2 * T + 1, :META], rows.astype(BF16)), out, 0)


def input_backward_last(ids, n0, n1, n2, n3, inputs, grad_middle, small, grad_two, one, two, stays, leaves):
    grad_one = input_grad(0, n0, n1, n2, n3, inputs[ids[0], 0], grad_middle, small)
    mine = ids[0] == 0
    stays[0] = jnp.where(mine, one[...], two[...])
    leaves[0] = jnp.where(mine, two[...], one[...])
    stays[1] = jnp.where(mine, grad_one, grad_two[...])
    leaves[1] = jnp.where(mine, grad_two[...], grad_one)


def gather_operands(parts, mine, one, r_one, two, r_two, held, sems):
    for n, part in enumerate(parts):
        fetch(mine, one.at[part], two.at[part], held.at[n, pl.ds(0, 320), :], sems.at[n, 0])
        fetch(mine, r_one.at[part], r_two.at[part], held.at[n, pl.ds(320, 320), :], sems.at[n, 1])


def wait_operands(places, one, held, sems):
    for n in places:
        arrive(one.at[0], held.at[n, pl.ds(0, 320), :], sems.at[n, 0])
        arrive(one.at[0], held.at[n, pl.ds(320, 320), :], sems.at[n, 1])


def outer_grads(ids, one, r_one, two, r_two, before, after, held, sems):
    gather_operands((0, 5, 2, 3), ids[0] == 0, one, r_one, two, r_two, held, sems)
    wait_operands((0, 1), one, held, sems)
    value = dot_tn(held[0], held[1]).astype(BF16)
    before[:, :HALF] = value[:, :HALF]
    after[:, :HALF] = value[:, HALF:]
    wait_operands((2, 3), one, held, sems)
    value = dot_tn(held[2], held[3]).astype(BF16)
    before[:HALF, HALF:] = value[:HALF, :HALF]
    before[HALF:, HALF:] = value[:HALF, HALF:]
    after[:HALF, HALF:] = value[HALF:, :HALF]
    after[HALF:, HALF:] = value[HALF:, HALF:]


def inner_grads(ids, one, r_one, two, r_two, grad_in, grad_out, held, result, sems, out_sems):
    j = ids[1] & 1
    gather_operands((0, 4, 1, 3), ids[0] == 0, one, r_one, two, r_two, held, sems)
    for n, grad in enumerate((grad_in, grad_out)):
        wait_operands((2 * n, 2 * n + 1), one, held, sems)
        result[n] = dot_tn(held[2 * n], held[2 * n + 1])
        move(result.at[n], grad.at[j], out_sems.at[n])
    for n, grad in enumerate((grad_in, grad_out)):
        arrive(result.at[n], grad.at[j], out_sems.at[n])


def fill_grads(ids, low, high, _in, _out, grad_in, grad_out, result, sems):
    other = 1 - (ids[1] & 1)
    for n, piece in enumerate((low, high)):
        place = slice(n * HALF, (n + 1) * HALF)
        result[0, :, place] = piece[:, :HALF].astype(F32)
        result[1, place, :HALF] = piece[:HALF, HALF:].astype(F32)
        result[1, place, HALF:] = piece[HALF:, HALF:].astype(F32)
    for n, grad in enumerate((grad_in, grad_out)):
        move(result.at[n], grad.at[other], sems.at[n])
    for n, grad in enumerate((grad_in, grad_out)):
        arrive(result.at[n], grad.at[other], sems.at[n])


def shared_weight_grads(ids, p0, p1, rp0, rp1, out, packed, sems):
    mine = ids[0] == 0
    fetch(mine, p0, p1, packed.at[0], sems.at[0])
    fetch(mine, rp0, rp1, packed.at[1], sems.at[1])
    arrive(p0, packed.at[0], sems.at[0])
    arrive(p0, packed.at[1], sems.at[1])
    grad_qkv, grad_attn, extra = None, None, None
    for m in range(2):
        whole = (
            dot_tn(packed[m, :256, 2 * D : 3 * D], packed[m, :256, :D]),
            dot_tn(packed[m, :256, 3 * D :], packed[m, :256, D : 2 * D]),
            dot_tn(packed[m, 272:, :D], packed[m, 272:, D : D + 128])
            + dot_tn(packed[m, 272:, :D], packed[m, 272:, D + 128 : D + 256])
            + dot_tn(packed[m, 256:272, :D], packed[m, 256:272, D : D + 128]),
        )
        if m == 0:
            grad_qkv, grad_attn, extra = whole
        else:
            grad_qkv, grad_attn, extra = grad_qkv + whole[0], grad_attn + whole[1], extra + whole[2]
    middle = grad_qkv[:, 128:256] + extra
    out[:, :48, :128] = grad_qkv[:, :128].astype(BF16).reshape(N_EXPERT, 48, 128)
    out[:, :48, 128:256] = middle.astype(BF16).reshape(N_EXPERT, 48, 128)
    out[:, :48, 256:] = grad_qkv[:, 256:].astype(BF16).reshape(N_EXPERT, 48, 512)
    row, column = iota((256, 256), 0), iota((256, 256), 1)
    spread = ((row & 15) < 12) & (column == (row >> 4) * 12 + (row & 15))
    spread = jnp.where(spread, 1.0, 0.0).astype(BF16)
    out[:, 48:, :] = dot(spread, grad_attn.astype(BF16)).astype(BF16).reshape(N_EXPERT, 16, D)


def sum_shared(ids, arrived, out, attn, total):
    me = ids[1]
    summed = arrived[0].astype(F32)
    for n in range(1, N_EXPERT):
        summed = summed + arrived[n].astype(F32)
    total[...] = summed
    for s in range(N_SHARD):
        out[(s - me) & (N_SHARD - 1), :12, :] = total[s * 12 : s * 12 + 12, :]
    attn[...] = total[48:, :]


def finish(ids, q0, q1, q2, q3, attn_in, stays, arrives, qkv, attn, one, two, router, acts, grads, held):
    mine, me = ids[0], ids[1]
    acts[mine] = stays[0]
    acts[1 - mine] = arrives[0]
    grads[mine] = stays[1]
    grads[1 - mine] = arrives[1]
    attn[...] = attn_in[:12, :]
    for k, piece in enumerate((q0, q1, q2, q3)):
        held[(me - k) & (N_SHARD - 1)] = piece[...]
    total = None
    for a in range(N_SHARD):
        for j in range(3):
            qkv[:, j * D + a * 192 : j * D + a * 192 + 192] = held[a, :12, j * 256 : j * 256 + 192]
        part = held[a, :12, 128:256]
        total = part if total is None else total + part
    diagonal = iota((12, 12), 0) == iota((12, 12), 1)
    one[...] = jnp.sum(jnp.where(diagonal, total[:, 96:97], 0.0), 0, keepdims=True)
    two[...] = jnp.sum(jnp.where(diagonal, total[:, 97:98], 0.0), 0, keepdims=True)
    router[...] = total[:, 64:96]


def along(value, axis, by):
    count = lax.axis_size(axis)
    return lax.ppermute(value, axis, [(i, (i + by) % count) for i in range(count)])


def gather_shards(value):
    return [value] + [along(value, "shard", k) for k in range(1, N_SHARD)]


def return_shards(pieces):
    return [pieces[0]] + [along(pieces[k], "shard", -k) for k in range(1, N_SHARD)]


def send_shards(pieces):
    return [pieces[0]] + [along(pieces[k], "shard", k) for k in range(1, N_SHARD)]


def exchange(value):
    rows = value.size // (N_ALL * 128)
    return lax.all_to_all(value.reshape(N_ALL, rows, 128), ("expert", "shard"), 0, 0, tiled=True)


def swap(value):
    return lax.ppermute(value, "section", [(0, 1), (1, 0)])


def up(value):
    return lax.ppermute(value, "section", [(0, 1)])


def down(value):
    return lax.ppermute(value, "section", [(1, 0)])


def after(first, *values):
    return lax.optimization_barrier((first, *values))


def dma(*shape):
    return pltpu.SemaphoreType.DMA(shape)


def local(inputs, cotangent, w_qkv, w_attn, gain_one, gain_two, router, w_in, w_out, routes):
    section = lax.axis_index("section")
    me = lax.axis_index("shard")
    ids = jnp.stack([section, me]).astype(jnp.int32)
    rows_shape = ((T, D), BF16)
    wide_shape = ((T, D), F32)
    per_expert = N_SHARD * GROUP
    w_scratch = pltpu.VMEM((N_SHARD, 192, D), BF16)
    expert_scratch = [pltpu.VMEM((D, 2 * D), BF16), pltpu.VMEM((2 * D, D), BF16)]
    staged_scratch = pltpu.VMEM((N_SHARD, ORDERED, 128), BF16)

    place = jnp.arange(ORDERED, dtype=jnp.int32)
    source = ((place % GROUP) // CAP) * SIDE + (place // GROUP) * CAP + place % CAP
    arriving = jnp.arange(N_EXPERT * SIDE, dtype=jnp.int32)
    order = (source[:, None] == arriving[None, :]).astype(BF16)
    back_order = (source[None, :] == arriving[:, None]).astype(BF16)

    p0, p1, p2, p3 = call(
        begin,
        [((1344, 128), BF16)] * 4,
        [ids, inputs, w_qkv[0], gain_one, gain_two, router[0].T],
        [pltpu.VMEM((T, D), F32), pltpu.VMEM((3, 192, D), BF16), pltpu.VMEM((1, 192), BF16), pltpu.VMEM((1, 192), BF16), dma(6)],
        anywhere=(1, 2, 3, 4),
        mib=56,
    )
    square = ((D, D), BF16)
    keep, to_after, to_before = call(
        split_experts,
        [((2, D, D), BF16), square, square],
        [ids, w_in[0], w_out[0]],
        [dma(8)],
        anywhere=(1, 2),
        outs_anywhere=(0, 1, 2),
    )
    own_routes = after(routes, p0)[0].reshape(2, T, 2)
    other_routes = swap(own_routes)
    p0, p1, p2, p3 = send_shards([p0, p1, p2, p3])
    p0, p1, p2, order, back_order, keep, other_routes = after(
        p0, p1, p2, order, back_order, keep, other_routes
    )
    own_w, units = call(
        join,
        [((5, 192, D), BF16), ((4 * T, D), BF16)],
        [ids, p0, p1, p2, p3],
        [pltpu.VMEM((N_SHARD, 64, 256), BF16)],
    )
    other_w = swap(own_w)
    own_a, own_w = after(w_attn[0], own_w)
    other_a = swap(own_a)
    weights = (own_w, other_w, own_a, other_a)
    attention_scratch = [w_scratch, pltpu.VMEM((192, D), BF16), dma(5)]

    o0, o1, o2, o3, kept_one, projected_one, small, h_one = call(
        attention_one,
        [rows_shape] * 4 + [((256, D + 256), BF16), ((256, D), BF16), ((2, 128, D), BF16), wide_shape],
        [ids, units, *weights, inputs],
        attention_scratch,
        anywhere=(2, 3, 4, 5, 6),
        mib=24,
    )
    keep = after(keep, o0)[0]
    other_keep = swap(keep)
    packed_shape = ((N_EXPERT, N_SHARD, SIDE, 128), BF16)
    state_shape = ((2 * T + 8, META + D), F32)
    half_shape = ((3, per_expert, D), BF16)
    slope_shape = ((2, per_expert, D), BF16)
    both_shape = ((6, per_expert, D), BF16)
    pieces = return_shards([o0, o1, o2, o3])
    to_after, to_before = after(to_after, to_before, *pieces)[:2]
    own_before, own_after = along(to_after, "shard", 1), along(to_before, "shard", -1)
    sent, state_one = call(
        functools.partial(dispatch, 0),
        [packed_shape, state_shape],
        [ids, h_one, *pieces, small, own_routes, other_routes],
    )
    arrived = exchange(sent)
    own_before, own_after = after(own_before, own_after, arrived)[:2]
    experts = (keep, other_keep, own_before, swap(own_before), own_after, swap(own_after))
    sent, fwd_one, slope = call(
        expert_forward,
        [((N_ALL, SIDE, 128), BF16), half_shape, slope_shape],
        [ids, arrived, order, back_order, *experts],
        [*expert_scratch, staged_scratch, dma(3), dma(5)],
        anywhere=(4, 5, 6, 7, 8, 9),
        mib=24,
    )
    result_one, taken, normed = call(
        combine_next,
        [wide_shape, ((2 * T, D), BF16), rows_shape],
        [ids, exchange(sent).reshape(packed_shape[0]), state_one, small],
    )

    o0, o1, o2, o3, kept_two, projected_two = call(
        attention_two,
        [rows_shape] * 4 + [((256, D + 256), BF16), ((256, D), BF16)],
        [ids, *gather_shards(normed), *weights],
        attention_scratch,
        anywhere=(5, 6, 7, 8),
        mib=24,
    )
    double_shape = ((N_EXPERT, N_SHARD, 2 * SIDE, 128), BF16)
    sent, state_two = call(
        functools.partial(dispatch, 1),
        [double_shape, state_shape],
        [ids, result_one, *return_shards([o0, o1, o2, o3]), small, own_routes, other_routes, cotangent],
    )
    sent, both_two = call(
        expert_both,
        [((N_ALL, 2 * SIDE, 128), BF16), both_shape],
        [ids, exchange(sent), order, back_order, *experts],
        [*expert_scratch, staged_scratch, staged_scratch, dma(3), dma(5)],
        anywhere=(4, 5, 6, 7, 8, 9),
        mib=28,
    )
    routed_shape = ((T + 16, D + 256), BF16)
    returned, r_both_two = after(exchange(sent), up(both_two))
    result_two, grad_middle, sent, routed = call(
        turn,
        [wide_shape, wide_shape, rows_shape, routed_shape],
        [ids, returned.reshape(double_shape[0]), state_two, cotangent, small],
    )

    def attention_grads(s, rows, kept, projected, routed):
        return call(
            functools.partial(attention_backward, s),
            [rows_shape] * 4 + [((352, 3 * D + 256), BF16)],
            [ids, *rows, routed, small, kept, projected, *weights],
            [w_scratch, pltpu.VMEM((256, D), BF16), dma(2)],
            anywhere=(9, 10, 11, 12),
            mib=24,
        )

    n0, n1, n2, n3, packed_two = attention_grads(1, gather_shards(sent), kept_two, projected_two, routed)
    grad_two, sent = call(
        input_backward_next,
        [wide_shape, packed_shape],
        [ids, *return_shards([n0, n1, n2, n3]), grad_middle, small, result_one, state_one],
    )

    arrived, r_packed_two = after(exchange(sent), up(packed_two))
    sent, both_one = call(
        expert_backward,
        [((N_ALL, SIDE, 128), BF16), both_shape],
        [ids, arrived, order, back_order, slope, fwd_one, *experts],
        [*expert_scratch, staged_scratch, pltpu.VMEM(*slope_shape), dma(3), dma(5), dma(2)],
        anywhere=(4, 5, 6, 7, 8, 9, 10, 11),
        mib=28,
    )
    returned, r_both_one = after(exchange(sent), down(both_one))
    grad_middle, sent, routed = call(
        middle_backward,
        [wide_shape, rows_shape, routed_shape],
        [ids, returned.reshape(packed_shape[0]), state_one, grad_two, taken, small],
    )
    rows = gather_shards(sent)
    both_one = after(both_one, sent)[0]
    operands = [both_one, r_both_one, both_two, r_both_two]
    held_scratch = pltpu.VMEM((4, 2 * per_expert, D), BF16)
    grad_before, grad_after = call(
        outer_grads,
        [square] * 2,
        [ids, *operands],
        [held_scratch, dma(4, 2)],
        anywhere=(1, 2, 3, 4),
        mib=24,
    )
    kept_one = after(kept_one, grad_before)[0]
    n0, n1, n2, n3, packed_one = attention_grads(0, rows, kept_one, projected_one, routed)

    r_packed_one = down(packed_one)
    pieces = return_shards([n0, n1, n2, n3])
    grad_before, grad_after = after(grad_before, grad_after, *pieces)[:2]
    low, high = along(grad_before, "shard", -1), along(grad_after, "shard", 1)
    payload = call(
        shared_weight_grads,
        [((N_EXPERT, 64, D), BF16)],
        [ids, packed_one, packed_two, r_packed_one, r_packed_two],
        [pltpu.VMEM((2, 352, 3 * D + 256), BF16), dma(2)],
        anywhere=(1, 2, 3, 4),
        mib=24,
    )[0]
    payload, *pieces = after(payload, *pieces)
    stays, leaves = call(
        input_backward_last,
        [((2, T, D), F32)] * 2,
        [ids, *pieces, inputs, grad_middle, small, grad_two, result_one, result_two],
    )
    summed = lax.all_to_all(payload, "expert", 0, 0, tiled=True)
    grads_shape = ((2, D, D), F32)
    grad_in, grad_out = call(
        inner_grads,
        [grads_shape] * 2,
        [ids, *operands],
        [held_scratch, pltpu.VMEM((2, D, D), F32), dma(4, 2), dma(2)],
        anywhere=(1, 2, 3, 4),
        outs_anywhere=(0, 1),
        mib=48,
    )
    summed, grad_in = after(summed, grad_in)
    arrives = swap(leaves)
    shares, attn = call(
        sum_shared,
        [((N_SHARD, 16, D), F32), ((16, D), F32)],
        [ids, summed],
        [pltpu.VMEM((64, D), F32)],
    )
    grad_in, grad_out = call(
        fill_grads,
        [grads_shape] * 2,
        [ids, low, high, after(grad_in, shares)[0], grad_out],
        [pltpu.VMEM((2, D, D), F32), dma(2)],
        anywhere=(3, 4),
        outs_anywhere=(0, 1),
        aliases={3: 0, 4: 1},
        mib=24,
    )
    pairs = [
        (e * N_SHARD + s, (N_SHARD * s + e // N_SHARD) * N_SHARD + e % N_SHARD)
        for e in range(N_EXPERT)
        for s in range(N_SHARD)
    ]
    attn_in = lax.ppermute(attn, ("expert", "shard"), pairs)
    q0, q1, q2, q3, attn_in, grad_in, grad_out = after(*send_shards(shares), attn_in, grad_in, grad_out)
    grad_qkv, grad_attn, grad_one, grad_two, grad_router, acts, grads = call(
        finish,
        [
            ((12, 3 * D), F32),
            ((12, D), F32),
            ((1, 12), F32),
            ((1, 12), F32),
            ((12, 32), F32),
            ((2, T, D), F32),
            ((2, T, D), F32),
        ],
        [ids, q0, q1, q2, q3, attn_in, stays, arrives],
        [pltpu.VMEM((N_SHARD, 16, D), F32)],
    )
    return (
        acts.reshape(1, 2, 1, T, D),
        grads.reshape(1, 2, 1, T, D),
        grad_qkv[None],
        grad_attn[None],
        grad_one,
        grad_two,
        grad_router[None],
        grad_in[None],
        grad_out[None],
    )


def solution(mesh):
    return jax.shard_map(
        local,
        mesh=mesh,
        in_specs=(
            P(None, "expert", "shard", None),
            P(None, "expert", "shard", None),
            P("section", "shard", None),
            P("section", "shard", None),
            P("section", "shard"),
            P("section", "shard"),
            P("section", "shard", None),
            P("section", "expert", None, "shard"),
            P("section", "expert", "shard", None),
            P("section", None, "expert", "shard", None, None),
        ),
        out_specs=(
            P("section", None, "expert", "shard", None),
            P("section", None, "expert", "shard", None),
            P("section", ("expert", "shard"), None),
            P("section", ("expert", "shard"), None),
            P("section", ("expert", "shard")),
            P("section", ("expert", "shard")),
            P("section", ("expert", "shard"), None),
            P("section", "expert", None, "shard"),
            P("section", "expert", "shard", None),
        ),
        check_vma=False,
    )
```

```python
import functools
import math

import jax
import jax.numpy as jnp
from jax import lax
from jax.experimental import pallas as pl
from jax.experimental.pallas import tpu as pltpu
from jax.sharding import PartitionSpec as P

F32 = jnp.float32
BF16 = jnp.bfloat16
D = 768
HEADS_OWN = 3
HDIM = 64
T = 64
CAP = 5
CHUNKS = 6
N_EXPERT = 16
N_SHARD = 4
N_ALL = N_EXPERT * N_SHARD
SIDE = 32
BLOCK = 2 * N_EXPERT * SIDE
GROUP = N_EXPERT * CAP
ORDERED = CHUNKS * GROUP
HALF = D // 2
META = 128
EPS = 1e-06
SCALE = 1.0 / math.sqrt(HDIM)


def dot(a, b):
    return lax.dot_general(a, b, (((1,), (0,)), ((), ())), preferred_element_type=F32)


def dot_nt(a, b):
    return lax.dot_general(a, b, (((1,), (1,)), ((), ())), preferred_element_type=F32)


def dot_tn(a, b):
    return lax.dot_general(a, b, (((0,), (0,)), ((), ())), preferred_element_type=F32)


def iota(shape, dim):
    return lax.broadcasted_iota(jnp.int32, shape, dim)


def call(body, outs, ins, scratch=(), anywhere=(), scalars=1, mib=12, outs_anywhere=(), aliases=None):
    specs = []
    for place in range(len(ins)):
        if place < scalars:
            specs.append(pl.BlockSpec(memory_space=pltpu.SMEM))
        elif place in anywhere:
            specs.append(pl.BlockSpec(memory_space=pltpu.HBM))
        else:
            specs.append(pl.BlockSpec(memory_space=pltpu.VMEM))
    return pl.pallas_call(
        body,
        out_shape=tuple(jax.ShapeDtypeStruct(shape, kind) for shape, kind in outs),
        in_specs=specs,
        out_specs=tuple(
            pl.BlockSpec(memory_space=pltpu.HBM if place in outs_anywhere else pltpu.VMEM)
            for place in range(len(outs))
        ),
        scratch_shapes=list(scratch),
        input_output_aliases=aliases or {},
        compiler_params=pltpu.CompilerParams(vmem_limit_bytes=mib * 1024 * 1024),
    )(*ins)


def fetch(mine, own, other, target, sem):
    @pl.when(mine)
    def _():
        pltpu.make_async_copy(own, target, sem).start()

    @pl.when(jnp.logical_not(mine))
    def _():
        pltpu.make_async_copy(other, target, sem).start()


def arrive(own, target, sem):
    pltpu.make_async_copy(own, target, sem).wait()


def move(source, target, sem):
    pltpu.make_async_copy(source, target, sem).start()


def norm_parts(rows):
    centered = rows - jnp.mean(rows, -1, keepdims=True)
    inverse = lax.rsqrt(jnp.mean(centered * centered, -1, keepdims=True) + EPS)
    return centered * inverse, inverse


def norm_back(grad, gain, unit, inverse):
    scaled = grad * gain
    return inverse * (
        scaled
        - jnp.mean(scaled, -1, keepdims=True)
        - unit * jnp.mean(scaled * unit, -1, keepdims=True)
    )


def split_pair(values):
    upper = values.astype(BF16)
    return upper, (values - upper.astype(F32)).astype(BF16)


def row_of(column):
    size = column.shape[0]
    diagonal = iota((size, size), 0) == iota((size, size), 1)
    return jnp.sum(jnp.where(diagonal, column, 0.0), 0, keepdims=True)


def slots_of(route_column):
    named = (iota((2 * T, 32), 1) == route_column).astype(F32)
    earlier = ((iota((2 * T, 2 * T), 1) & (T - 1)) < (iota((2 * T, 2 * T), 0) & (T - 1))).astype(BF16)
    before = dot(earlier, named.astype(BF16))
    return route_column.astype(F32) * CAP + jnp.sum(before * named, 1, keepdims=True)


def packed_place(index):
    within = index & (SIDE - 1)
    chunk = (within * 205) >> 10
    return (index >> 5) * CAP + within - chunk * CAP, chunk


def to_packed(slot_row, rows):
    slot, chunk = packed_place(iota((BLOCK, 2 * T), 0))
    hit = slot.astype(F32) == slot_row
    total = None
    for c in range(CHUNKS):
        mask = jnp.where(hit & (chunk == c), 1.0, 0.0).astype(BF16)
        part = dot(mask, rows[:, c * 128 : (c + 1) * 128])
        total = part if total is None else total + part
    return total.astype(BF16)


def from_packed(slot_column, packed):
    slot, chunk = packed_place(iota((2 * T, BLOCK), 1))
    hit = slot.astype(F32) == slot_column
    parts = []
    for c in range(CHUNKS):
        mask = jnp.where(hit & (chunk == c), 1.0, 0.0).astype(BF16)
        parts.append(dot(mask, packed))
    return jnp.concatenate(parts, 1)


def send_to_holders(packed, out_ref, start):
    blocks = packed.reshape(N_EXPERT, 2, SIDE, 128)
    for s in range(N_SHARD):
        out_ref[:, s, start : start + SIDE, :] = blocks[:, s % 2]


def sum_of_holders(in_ref, start):
    parts = []
    for j in range(2):
        total = in_ref[:, j, start : start + SIDE, :].astype(F32)
        total = total + in_ref[:, j + 2, start : start + SIDE, :].astype(F32)
        parts.append(total.astype(BF16).reshape(N_EXPERT, 1, SIDE, 128))
    return jnp.concatenate(parts, 1).reshape(BLOCK, 128)


def group_of(packed_ref, group, start):
    rows = packed_ref[group * N_EXPERT : (group + 1) * N_EXPERT, start : start + SIDE, :]
    return rows.reshape(N_EXPERT * SIDE, 128)


def order_pair(order, first, second):
    return dot(order, jnp.concatenate([first, second], 1)).astype(BF16)


def place_rows(ordered, half, group, kept_ref):
    for c in range(CHUNKS):
        kept_ref[group * GROUP : (group + 1) * GROUP, c * 128 : (c + 1) * 128] = ordered[
            c * GROUP : (c + 1) * GROUP, half * 128 : half * 128 + 128
        ]


def stage_rows(rows, staged_ref):
    for group in range(N_SHARD):
        for c in range(CHUNKS):
            staged_ref[group, c * GROUP : (c + 1) * GROUP, :] = rows[
                group * GROUP : (group + 1) * GROUP, c * 128 : (c + 1) * 128
            ]


def unorder_pair(back_order, first, second, out_ref, places):
    packed = dot(back_order, jnp.concatenate([first, second], 1)).astype(BF16)
    for half, (group, start) in enumerate(places):
        out_ref[group * N_EXPERT : (group + 1) * N_EXPERT, start : start + SIDE, :] = packed[
            :, half * 128 : half * 128 + 128
        ].reshape(N_EXPERT, SIDE, 128)


def head_mask(h):
    lane = iota((1, 256), 1)
    return ((lane >= h * HDIM) & (lane < (h + 1) * HDIM)).astype(BF16)


def fold(value):
    half = value.shape[0] // 2
    return jnp.concatenate([value[:half, :], value[half:, :]], 1)


def unfold(value):
    return jnp.concatenate([value[:, :64], value[:, 64:]], 0)


def begin(ids, inputs, w, gain_one, gain_two, router, p0, p1, p2, p3, h, held, thin_one, thin_two, sems):
    mine, me = ids[0], ids[1]
    move(inputs.at[mine, 0], h, sems.at[0])
    for j in range(3):
        move(w.at[:, pl.ds(j * D, D)], held.at[j], sems.at[1 + j])
    move(gain_one, thin_one, sems.at[4])
    move(gain_two, thin_two, sems.at[5])
    arrive(gain_one, thin_one, sems.at[4])
    arrive(gain_two, thin_two, sems.at[5])
    rows = iota((32, 192), 0)
    gains = jnp.where(rows == 0, thin_one[...].astype(F32), jnp.where(rows == 1, thin_two[...].astype(F32), 0.0))
    thin = jnp.concatenate([router[...], gains.astype(BF16)], 0)
    arrive(inputs.at[mine, 0], h, sems.at[0])
    unit, _ = norm_parts(h[...])
    unit = unit.astype(BF16)
    for j in range(3):
        arrive(w.at[:, pl.ds(j * D, D)], held.at[j], sems.at[1 + j])
    for piece in (p0, p1, p2, p3):
        piece[864:928, :] = thin[:, :128]
        piece[928:960, :] = fold(thin[:, 128:])
        for c in range(CHUNKS):
            piece[960 + 64 * c : 1024 + 64 * c, :] = unit[:, c * 128 : (c + 1) * 128]
    for s in range(N_SHARD):
        for k, piece in enumerate((p0, p1, p2, p3)):

            @pl.when(((s - me) & (N_SHARD - 1)) == k)
            def _(s=s, piece=piece):
                parts = [held[j, :, s * 192 : s * 192 + 192] for j in range(3)]
                for j in range(3):
                    piece[192 * j : 192 * j + 192, :] = parts[j][:, :128]
                piece[576:768, :] = jnp.concatenate([parts[0][:, 128:], parts[1][:, 128:]], 1)
                piece[768:864, :] = fold(parts[2][:, 128:])


def join(ids, p0, p1, p2, p3, out, units, held):
    me = ids[1]
    none = jnp.zeros((192, 64), BF16)
    for k, piece in enumerate((p0, p1, p2, p3)):
        place = (me - k) & (N_SHARD - 1)
        rest = piece[576:768, :]
        rests = (rest[:, :64], rest[:, 64:], unfold(piece[768:864, :]))
        for j in range(3):
            out[place, :, 256 * j : 256 * j + 128] = piece[192 * j : 192 * j + 192, :]
            out[place, :, 256 * j + 128 : 256 * j + 256] = jnp.concatenate([rests[j], none], 1)
        held[place, :, :128] = piece[864:928, :]
        held[place, :, 128:] = jnp.concatenate([unfold(piece[928:960, :]), none[:64]], 1)
        for c in range(CHUNKS):
            units[k * T : (k + 1) * T, c * 128 : (c + 1) * 128] = piece[960 + 64 * c : 1024 + 64 * c, :]
    out[4] = jnp.zeros((192, D), BF16)
    for a in range(N_SHARD):
        out[4, 64:128, a * 192 : (a + 1) * 192] = held[a, :, :192]


def attend(x, w, a, kept, projected, outs):
    kept[:, :D] = x
    whole = dot(x, w[...].reshape(D, D)).astype(BF16)
    projected[...] = whole
    query, key, value = whole[:, :256], whole[:, 256:512], whole[:, 512:]
    attended = None
    for h in range(HEADS_OWN):
        mask = head_mask(h)
        scores = dot_nt(query * mask, key) * SCALE
        raised = jnp.exp(scores - jnp.max(scores, -1, keepdims=True))
        probs = (raised / jnp.sum(raised, -1, keepdims=True)).astype(BF16)
        part = dot(probs, value * mask)
        attended = part if attended is None else attended + part
    attended = attended.astype(BF16)
    kept[:, D:] = attended
    result = dot(attended[:, :192], a[...]).astype(BF16)
    for k, out in enumerate(outs):
        out[...] = result[k * T : (k + 1) * T, :]


def attention_one(ids, units, own_w, other_w, own_a, other_a, inputs, o0, o1, o2, o3, kept, projected, small, h, w, a, sems):
    mine = ids[0] == 0
    rows, extra = pl.ds(0, 4), pl.ds(0, 128)
    fetch(mine, own_w.at[4, extra], other_w.at[4, extra], small.at[0], sems.at[2])
    fetch(mine, own_w.at[rows], other_w.at[rows], w, sems.at[0])
    fetch(mine, own_a, other_a, a, sems.at[1])
    fetch(mine, other_w.at[4, extra], own_w.at[4, extra], small.at[1], sems.at[3])
    move(inputs.at[ids[0], 0], h, sems.at[4])
    arrive(own_w.at[4, extra], small.at[0], sems.at[2])
    x = (units[...].astype(F32) * small[0, 96:97, :].astype(F32)).astype(BF16)
    arrive(own_w.at[rows], w, sems.at[0])
    arrive(own_a, a, sems.at[1])
    attend(x, w, a, kept, projected, (o0, o1, o2, o3))
    arrive(own_w.at[4, extra], small.at[1], sems.at[3])
    arrive(inputs.at[ids[0], 0], h, sems.at[4])


def attention_two(ids, x0, x1, x2, x3, own_w, other_w, own_a, other_a, o0, o1, o2, o3, kept, projected, w, a, sems):
    mine = ids[0] == 1
    rows = pl.ds(0, 4)
    fetch(mine, own_w.at[rows], other_w.at[rows], w, sems.at[0])
    fetch(mine, own_a, other_a, a, sems.at[1])
    x = jnp.concatenate([x0[...], x1[...], x2[...], x3[...]], 0)
    arrive(own_w.at[rows], w, sems.at[0])
    arrive(own_a, a, sems.at[1])
    attend(x, w, a, kept, projected, (o0, o1, o2, o3))


def dispatch(section, ids, h, o0, o1, o2, o3, small, own_routes, other_routes, *refs):
    if section == 1:
        seed, out, held = refs
        start = h[...].astype(BF16).astype(F32)
    else:
        out, held = refs
        start = h[...]
    middle = start + (
        (o0[...].astype(F32) + o1[...].astype(F32)) + (o2[...].astype(F32) + o3[...].astype(F32))
    )
    held[:T, META:] = middle
    held[T:, META:] = jnp.zeros((T + 8, D), F32)
    unit, _ = norm_parts(middle)
    normed = (unit * small[section, 97:98, :].astype(F32)).astype(BF16)
    route = jnp.where(ids[0] == section, own_routes[ids[0]], other_routes[ids[0]])
    column = jnp.concatenate([route[:, 0:1], route[:, 1:2]], 0)
    slot_column = slots_of(column)
    slot_row = row_of(slot_column)
    send_to_holders(to_packed(slot_row, jnp.concatenate([normed, normed], 0)), out, 0)
    logits = dot_nt(normed, small[section])
    logits = jnp.concatenate([logits, logits], 0)
    lanes = iota((2 * T, 128), 1)
    chosen = jnp.sum(jnp.where(lanes == column + 64, logits, 0.0), 1, keepdims=True)
    one, two = chosen[:T], chosen[T:]
    top = jnp.maximum(one, two)
    one, two = jnp.exp(one - top), jnp.exp(two - top)
    total = one + two
    gates = jnp.concatenate([one / total, two / total], 0)
    held[: 2 * T, :META] = jnp.where(
        lanes == 0, gates, jnp.where(lanes == 1, slot_column, column.astype(F32) + 64.0)
    )
    held[2 * T :, :META] = jnp.broadcast_to(slot_row, (8, META))
    if section == 1:
        grad = seed[ids[0], 0]
        rows = jnp.concatenate([grad, grad], 0) * gates
        send_to_holders(to_packed(slot_row, rows.astype(BF16)), out, SIDE)


def split_experts(ids, w_in, w_out, keep, after, before, sems):
    j = ids[1] & 1
    other = 1 - j
    low, high = pl.ds(0, HALF), pl.ds(HALF, HALF)
    copies = [(w_in.at[j], keep.at[0]), (w_out.at[j], keep.at[1])]
    for part, target in ((low, after), (high, before)):
        copies.append((w_in.at[other, :, part], target.at[:, low]))
        copies.append((w_out.at[other, part, low], target.at[low, high]))
        copies.append((w_out.at[other, part, high], target.at[high, high]))
    for n, (source, target) in enumerate(copies):
        move(source, target, sems.at[n])
    for n, (source, target) in enumerate(copies):
        arrive(source, target, sems.at[n])


def expert_copies(keep, before, after, w_in, w_out):
    low, high = pl.ds(0, HALF), pl.ds(HALF, HALF)
    inner = [(keep, lambda r: r.at[0], w_in.at[:, pl.ds(0, D)])]
    outer = [(keep, lambda r: r.at[1], w_out.at[pl.ds(0, D), :])]
    for n, pair in enumerate((before, after)):
        place = pl.ds(D + n * HALF, HALF)
        inner.append((pair, lambda r: r.at[:, low], w_in.at[:, place]))
        outer.append((pair, lambda r: r.at[low, high], w_out.at[place, low]))
        outer.append((pair, lambda r: r.at[high, high], w_out.at[place, high]))
    return inner, outer


def load_experts(copies, mine, sems):
    for n, ((own, other), part, target) in enumerate(copies):
        fetch(mine, part(own), part(other), target, sems.at[n])


def wait_experts(copies, sems):
    for n, ((own, _), part, target) in enumerate(copies):
        arrive(part(own), target, sems.at[n])


def gelu_parts(up):
    share = 0.5 * (1.0 + lax.erf(up * math.sqrt(0.5)))
    return (up * share).astype(BF16), share + up * jnp.exp(-0.5 * up * up) * (1.0 / math.sqrt(2.0 * math.pi))


def expert_forward(ids, arrived, order, back_order, k0, k1, b0, b1, a0, a1, out, kept, slope, w_in, w_out, staged, sems_in, sems_out):
    inner, outer = expert_copies((k0, k1), (b0, b1), (a0, a1), w_in, w_out)
    load_experts(inner, ids[0] == 0, sems_in)
    load_experts(outer, ids[0] == 0, sems_out)
    for pair in (0, 2):
        ordered = order_pair(order[...], group_of(arrived, pair, 0), group_of(arrived, pair + 1, 0))
        place_rows(ordered, 0, pair, kept.at[0])
        place_rows(ordered, 1, pair + 1, kept.at[0])
    wait_experts(inner, sems_in)
    result = None
    for q in range(2):
        hidden, scale = gelu_parts(dot(kept[0], w_in[:, q * D : (q + 1) * D]))
        kept[1 + q] = hidden
        slope[q] = scale.astype(BF16)
        if q == 0:
            wait_experts(outer, sems_out)
        part = dot(hidden, w_out[q * D : (q + 1) * D, :])
        result = part if result is None else result + part
    stage_rows(result.astype(BF16), staged)
    for pair in (0, 2):
        unorder_pair(back_order[...], staged[pair], staged[pair + 1], out, ((pair, 0), (pair + 1, 0)))


def expert_both(ids, arrived, order, back_order, k0, k1, b0, b1, a0, a1, out, kept, w_in, w_out, staged, staged_back, sems_in, sems_out):
    inner, outer = expert_copies((k0, k1), (b0, b1), (a0, a1), w_in, w_out)
    load_experts(inner, ids[0] == 1, sems_in)
    load_experts(outer, ids[0] == 1, sems_out)
    for group in range(N_SHARD):
        ordered = order_pair(order[...], group_of(arrived, group, 0), group_of(arrived, group, SIDE))
        place_rows(ordered, 0, group, kept.at[0])
        place_rows(ordered, 1, group, kept.at[3])
    wait_experts(inner, sems_in)
    wait_experts(outer, sems_out)
    result, back = None, None
    for q in range(2):
        part_in, part_out = w_in[:, q * D : (q + 1) * D], w_out[q * D : (q + 1) * D, :]
        hidden, scale = gelu_parts(dot(kept[0], part_in))
        kept[1 + q] = hidden
        grad_up = (dot_nt(kept[3], part_out) * scale).astype(BF16)
        kept[4 + q] = grad_up
        parts = (dot(hidden, part_out), dot_nt(grad_up, part_in))
        result = parts[0] if q == 0 else result + parts[0]
        back = parts[1] if q == 0 else back + parts[1]
    stage_rows(result.astype(BF16), staged)
    stage_rows(back.astype(BF16), staged_back)
    for group in range(N_SHARD):
        unorder_pair(back_order[...], staged[group], staged_back[group], out, ((group, 0), (group, SIDE)))


def expert_backward(ids, arrived, order, back_order, slope_in, fwd, k0, k1, b0, b1, a0, a1, out, kept, w_in, w_out, staged, slope, sems_in, sems_out, sems):
    inner, outer = expert_copies((k0, k1), (b0, b1), (a0, a1), w_in, w_out)
    load_experts(outer, ids[0] == 0, sems_out)
    load_experts(inner, ids[0] == 0, sems_in)
    move(slope_in, slope, sems.at[0])
    move(fwd, kept.at[pl.ds(0, 3)], sems.at[1])
    for pair in (0, 2):
        ordered = order_pair(order[...], group_of(arrived, pair, 0), group_of(arrived, pair + 1, 0))
        place_rows(ordered, 0, pair, kept.at[3])
        place_rows(ordered, 1, pair + 1, kept.at[3])
    arrive(slope_in, slope, sems.at[0])
    wait_experts(outer, sems_out)
    back = None
    for q in range(2):
        grad_up = (dot_nt(kept[3], w_out[q * D : (q + 1) * D, :]) * slope[q].astype(F32)).astype(BF16)
        kept[4 + q] = grad_up
        if q == 0:
            wait_experts(inner, sems_in)
        part = dot_nt(grad_up, w_in[:, q * D : (q + 1) * D])
        back = part if q == 0 else back + part
    stage_rows(back.astype(BF16), staged)
    for pair in (0, 2):
        unorder_pair(back_order[...], staged[pair], staged[pair + 1], out, ((pair, 0), (pair + 1, 0)))
    arrive(fwd, kept.at[pl.ds(0, 3)], sems.at[1])


def mixed(rows, held):
    weighted = rows * held[: 2 * T, 0:1]
    return held[:T, META:] + weighted[:T] + weighted[T:]


def combine_next(ids, returned, held, small, result, taken, normed):
    rows = from_packed(held[: 2 * T, 1:2], sum_of_holders(returned, 0))
    taken[...] = rows.astype(BF16)
    total = mixed(rows, held)
    result[...] = total
    unit, _ = norm_parts(total.astype(BF16).astype(F32))
    normed[...] = (unit * small[1, 96:97, :].astype(F32)).astype(BF16)


def middle_grads(section, rows, grad_rows, grad, meta, small, grad_middle, sent, routed):
    gates = meta[: 2 * T, 0:1]
    gate_grads = jnp.sum(jnp.concatenate([grad, grad], 0) * rows, 1, keepdims=True)
    weighted = gates * gate_grads
    mean = weighted[:T] + weighted[T:]
    chosen = gates * (gate_grads - jnp.concatenate([mean, mean], 0))
    lanes = iota((2 * T, 128), 1).astype(F32)
    spread = jnp.where(lanes == meta[: 2 * T, 2:3], chosen, 0.0)
    logits_upper, logits_lower = split_pair(spread[:T] + spread[T:])
    part = dot(logits_upper, small[section]) + dot(logits_lower, small[section])
    grad_normed = part + grad_rows[:T] + grad_rows[T:]
    unit, inverse = norm_parts(meta[:T, META:])
    gain = small[section, 97:98, :].astype(F32)
    value = grad + norm_back(grad_normed, gain, unit, inverse)
    grad_middle[...] = value
    sent[...] = value.astype(BF16)
    upper, lower = split_pair(jnp.sum(grad_normed * unit, 0, keepdims=True))
    routed[:T, :D] = (unit * gain).astype(BF16)
    routed[:T, D : D + 128] = logits_upper
    routed[:T, D + 128 :] = logits_lower
    place = iota((16, D), 0)
    routed[T:, :D] = jnp.where(place == 0, upper, jnp.where(place == 1, lower, 0.0)).astype(BF16)
    named = (iota((16, 128), 1) == 97) & (iota((16, 128), 0) < 2)
    routed[T:, D : D + 128] = jnp.where(named, 1.0, 0.0).astype(BF16)
    routed[T:, D + 128 :] = jnp.zeros((16, 128), BF16)


def turn(ids, returned, held, seed, small, result, grad_middle, sent, routed):
    slot = held[: 2 * T, 1:2]
    rows = from_packed(slot, sum_of_holders(returned, 0))
    result[...] = mixed(rows, held)
    grad_rows = from_packed(slot, sum_of_holders(returned, SIDE))
    middle_grads(1, rows, grad_rows, seed[ids[0], 0], held, small, grad_middle, sent, routed)


def middle_backward(ids, returned, held, grad, taken, small, grad_middle, sent, routed):
    grad_rows = from_packed(held[: 2 * T, 1:2], sum_of_holders(returned, 0))
    middle_grads(0, taken[...].astype(F32), grad_rows, grad[...], held, small, grad_middle, sent, routed)


def attention_backward(section, ids, g0, g1, g2, g3, routed, small, kept, projected, own_w, other_w, own_a, other_a, n0, n1, n2, n3, packed, w, a, sems):
    mine = ids[0] == section
    rows = pl.ds(0, 4)
    fetch(mine, own_a, other_a, a.at[pl.ds(0, 192), :], sems.at[1])
    fetch(mine, own_w.at[rows], other_w.at[rows], w, sems.at[0])
    packed[:256, 2 * D :] = kept[...]
    packed[256:, 2 * D :] = jnp.zeros((96, D + 256), BF16)
    a[192:, :] = jnp.zeros((64, D), BF16)
    packed[272:, : D + 256] = routed[...]
    packed[272:, D + 256 : 2 * D] = jnp.zeros((80, D - 256), BF16)
    grad = jnp.concatenate([g0[...], g1[...], g2[...], g3[...]], 0)
    packed[:256, D : 2 * D] = grad
    arrive(own_a, a.at[pl.ds(0, 192), :], sems.at[1])
    grad_attended = dot_nt(grad, a[...]).astype(BF16)
    query, key, value = projected[:, :256], projected[:, 256:512], projected[:, 512:]
    grad_query, grad_key, grad_value = None, None, None
    for h in range(HEADS_OWN):
        mask = head_mask(h)
        query_part, grad_part = query * mask, grad_attended * mask
        scores = dot_nt(query_part, key) * SCALE
        raised = jnp.exp(scores - jnp.max(scores, -1, keepdims=True))
        probs = raised / jnp.sum(raised, -1, keepdims=True)
        grad_probs = dot_nt(grad_part, value)
        grad_scores = probs * (grad_probs - jnp.sum(grad_probs * probs, -1, keepdims=True))
        grad_scores = grad_scores.astype(BF16)
        parts = (
            dot(grad_scores, key * mask),
            dot_tn(grad_scores, query_part),
            dot_tn(probs.astype(BF16), grad_part),
        )
        if h == 0:
            grad_query, grad_key, grad_value = parts
        else:
            grad_query, grad_key, grad_value = (
                grad_query + parts[0],
                grad_key + parts[1],
                grad_value + parts[2],
            )
    grad_projected = jnp.concatenate([grad_query * SCALE, grad_key * SCALE, grad_value], 1).astype(BF16)
    packed[:256, :D] = grad_projected
    arrive(own_w.at[rows], w, sems.at[0])
    grad_normed = dot_nt(grad_projected, w[...].reshape(D, D))
    result = grad_normed.astype(BF16)
    for k, out in enumerate((n0, n1, n2, n3)):
        out[...] = result[k * T : (k + 1) * T, :]
    gain = jnp.sum(grad_normed * kept[:, :D].astype(F32), 0, keepdims=True)
    upper, lower = split_pair(gain / small[section, 96:97, :].astype(F32))
    place = iota((16, D), 0)
    packed[256:272, :D] = jnp.where(place == 0, upper, jnp.where(place == 1, lower, 0.0)).astype(BF16)
    named = (iota((16, D), 1) == 96) & (iota((16, D), 0) < 2)
    packed[256:272, D : 2 * D] = jnp.where(named, 1.0, 0.0).astype(BF16)


def input_grad(section, n0, n1, n2, n3, h, grad_middle, small):
    grad_normed = (n0[...].astype(F32) + n1[...].astype(F32)) + (n2[...].astype(F32) + n3[...].astype(F32))
    unit, inverse = norm_parts(h)
    return grad_middle[...] + norm_back(grad_normed, small[section, 96:97, :].astype(F32), unit, inverse)


def input_backward_next(ids, n0, n1, n2, n3, grad_middle, small, result, held, grad_out, out):
    h = result[...].astype(BF16).astype(F32)
    grad = input_grad(1, n0, n1, n2, n3, h, grad_middle, small).astype(BF16).astype(F32)
    grad_out[...] = grad
    rows = jnp.concatenate([grad, grad], 0) * held[: 2 * T, 0:1]
    send_to_holders(to_packed(held[2 * T : 2 * T + 1, :META], rows.astype(BF16)), out, 0)


def input_backward_last(ids, n0, n1, n2, n3, inputs, grad_middle, small, grad_two, one, two, stays, leaves):
    grad_one = input_grad(0, n0, n1, n2, n3, inputs[ids[0], 0], grad_middle, small)
    mine = ids[0] == 0
    stays[0] = jnp.where(mine, one[...], two[...])
    leaves[0] = jnp.where(mine, two[...], one[...])
    stays[1] = jnp.where(mine, grad_one, grad_two[...])
    leaves[1] = jnp.where(mine, grad_two[...], grad_one)


def gather_operands(parts, mine, one, r_one, two, r_two, held, sems):
    for n, part in enumerate(parts):
        fetch(mine, one.at[part], two.at[part], held.at[n, pl.ds(0, 320), :], sems.at[n, 0])
        fetch(mine, r_one.at[part], r_two.at[part], held.at[n, pl.ds(320, 320), :], sems.at[n, 1])


def wait_operands(places, one, held, sems):
    for n in places:
        arrive(one.at[0], held.at[n, pl.ds(0, 320), :], sems.at[n, 0])
        arrive(one.at[0], held.at[n, pl.ds(320, 320), :], sems.at[n, 1])


def outer_grads(ids, one, r_one, two, r_two, before, after, held, sems):
    gather_operands((0, 5, 2, 3), ids[0] == 0, one, r_one, two, r_two, held, sems)
    wait_operands((0, 1), one, held, sems)
    value = dot_tn(held[0], held[1]).astype(BF16)
    before[:, :HALF] = value[:, :HALF]
    after[:, :HALF] = value[:, HALF:]
    wait_operands((2, 3), one, held, sems)
    value = dot_tn(held[2], held[3]).astype(BF16)
    before[:HALF, HALF:] = value[:HALF, :HALF]
    before[HALF:, HALF:] = value[:HALF, HALF:]
    after[:HALF, HALF:] = value[HALF:, :HALF]
    after[HALF:, HALF:] = value[HALF:, HALF:]


def inner_grads(ids, one, r_one, two, r_two, grad_in, grad_out, held, result, sems, out_sems):
    j = ids[1] & 1
    gather_operands((0, 4, 1, 3), ids[0] == 0, one, r_one, two, r_two, held, sems)
    for n, grad in enumerate((grad_in, grad_out)):
        wait_operands((2 * n, 2 * n + 1), one, held, sems)
        result[n] = dot_tn(held[2 * n], held[2 * n + 1])
        move(result.at[n], grad.at[j], out_sems.at[n])
    for n, grad in enumerate((grad_in, grad_out)):
        arrive(result.at[n], grad.at[j], out_sems.at[n])


def fill_grads(ids, low, high, _in, _out, grad_in, grad_out, result, sems):
    other = 1 - (ids[1] & 1)
    for n, piece in enumerate((low, high)):
        place = slice(n * HALF, (n + 1) * HALF)
        result[0, :, place] = piece[:, :HALF].astype(F32)
        result[1, place, :HALF] = piece[:HALF, HALF:].astype(F32)
        result[1, place, HALF:] = piece[HALF:, HALF:].astype(F32)
    for n, grad in enumerate((grad_in, grad_out)):
        move(result.at[n], grad.at[other], sems.at[n])
    for n, grad in enumerate((grad_in, grad_out)):
        arrive(result.at[n], grad.at[other], sems.at[n])


def shared_weight_grads(ids, p0, p1, rp0, rp1, out, packed, sems):
    mine = ids[0] == 0
    fetch(mine, p0, p1, packed.at[0], sems.at[0])
    fetch(mine, rp0, rp1, packed.at[1], sems.at[1])
    arrive(p0, packed.at[0], sems.at[0])
    arrive(p0, packed.at[1], sems.at[1])
    grad_qkv, grad_attn, extra = None, None, None
    for m in range(2):
        whole = (
            dot_tn(packed[m, :256, 2 * D : 3 * D], packed[m, :256, :D]),
            dot_tn(packed[m, :256, 3 * D :], packed[m, :256, D : 2 * D]),
            dot_tn(packed[m, 272:, :D], packed[m, 272:, D : D + 128])
            + dot_tn(packed[m, 272:, :D], packed[m, 272:, D + 128 : D + 256])
            + dot_tn(packed[m, 256:272, :D], packed[m, 256:272, D : D + 128]),
        )
        if m == 0:
            grad_qkv, grad_attn, extra = whole
        else:
            grad_qkv, grad_attn, extra = grad_qkv + whole[0], grad_attn + whole[1], extra + whole[2]
    middle = grad_qkv[:, 128:256] + extra
    out[:, :48, :128] = grad_qkv[:, :128].astype(BF16).reshape(N_EXPERT, 48, 128)
    out[:, :48, 128:256] = middle.astype(BF16).reshape(N_EXPERT, 48, 128)
    out[:, :48, 256:] = grad_qkv[:, 256:].astype(BF16).reshape(N_EXPERT, 48, 512)
    row, column = iota((256, 256), 0), iota((256, 256), 1)
    spread = ((row & 15) < 12) & (column == (row >> 4) * 12 + (row & 15))
    spread = jnp.where(spread, 1.0, 0.0).astype(BF16)
    out[:, 48:, :] = dot(spread, grad_attn.astype(BF16)).astype(BF16).reshape(N_EXPERT, 16, D)


def sum_shared(ids, arrived, out, attn, total):
    me = ids[1]
    summed = arrived[0].astype(F32)
    for n in range(1, N_EXPERT):
        summed = summed + arrived[n].astype(F32)
    total[...] = summed
    for s in range(N_SHARD):
        out[(s - me) & (N_SHARD - 1), :12, :] = total[s * 12 : s * 12 + 12, :]
    attn[...] = total[48:, :]


def finish(ids, q0, q1, q2, q3, attn_in, stays, arrives, qkv, attn, one, two, router, acts, grads, held):
    mine, me = ids[0], ids[1]
    acts[mine] = stays[0]
    acts[1 - mine] = arrives[0]
    grads[mine] = stays[1]
    grads[1 - mine] = arrives[1]
    attn[...] = attn_in[:12, :]
    for k, piece in enumerate((q0, q1, q2, q3)):
        held[(me - k) & (N_SHARD - 1)] = piece[...]
    total = None
    for a in range(N_SHARD):
        for j in range(3):
            qkv[:, j * D + a * 192 : j * D + a * 192 + 192] = held[a, :12, j * 256 : j * 256 + 192]
        part = held[a, :12, 128:256]
        total = part if total is None else total + part
    diagonal = iota((12, 12), 0) == iota((12, 12), 1)
    one[...] = jnp.sum(jnp.where(diagonal, total[:, 96:97], 0.0), 0, keepdims=True)
    two[...] = jnp.sum(jnp.where(diagonal, total[:, 97:98], 0.0), 0, keepdims=True)
    router[...] = total[:, 64:96]


def along(value, axis, by):
    count = lax.axis_size(axis)
    return lax.ppermute(value, axis, [(i, (i + by) % count) for i in range(count)])


def gather_shards(value):
    return [value] + [along(value, "shard", k) for k in range(1, N_SHARD)]


def return_shards(pieces):
    return [pieces[0]] + [along(pieces[k], "shard", -k) for k in range(1, N_SHARD)]


def send_shards(pieces):
    return [pieces[0]] + [along(pieces[k], "shard", k) for k in range(1, N_SHARD)]


def exchange(value):
    rows = value.size // (N_ALL * 128)
    return lax.all_to_all(value.reshape(N_ALL, rows, 128), ("expert", "shard"), 0, 0, tiled=True)


def swap(value):
    return lax.ppermute(value, "section", [(0, 1), (1, 0)])


def up(value):
    return lax.ppermute(value, "section", [(0, 1)])


def down(value):
    return lax.ppermute(value, "section", [(1, 0)])


def after(first, *values):
    return lax.optimization_barrier((first, *values))


def dma(*shape):
    return pltpu.SemaphoreType.DMA(shape)


def local(inputs, cotangent, w_qkv, w_attn, gain_one, gain_two, router, w_in, w_out, routes):
    section = lax.axis_index("section")
    me = lax.axis_index("shard")
    ids = jnp.stack([section, me]).astype(jnp.int32)
    rows_shape = ((T, D), BF16)
    wide_shape = ((T, D), F32)
    per_expert = N_SHARD * GROUP
    w_scratch = pltpu.VMEM((N_SHARD, 192, D), BF16)
    expert_scratch = [pltpu.VMEM((D, 2 * D), BF16), pltpu.VMEM((2 * D, D), BF16)]
    staged_scratch = pltpu.VMEM((N_SHARD, ORDERED, 128), BF16)

    place = jnp.arange(ORDERED, dtype=jnp.int32)
    source = ((place % GROUP) // CAP) * SIDE + (place // GROUP) * CAP + place % CAP
    arriving = jnp.arange(N_EXPERT * SIDE, dtype=jnp.int32)
    order = (source[:, None] == arriving[None, :]).astype(BF16)
    back_order = (source[None, :] == arriving[:, None]).astype(BF16)

    p0, p1, p2, p3 = call(
        begin,
        [((1344, 128), BF16)] * 4,
        [ids, inputs, w_qkv[0], gain_one, gain_two, router[0].T],
        [pltpu.VMEM((T, D), F32), pltpu.VMEM((3, 192, D), BF16), pltpu.VMEM((1, 192), BF16), pltpu.VMEM((1, 192), BF16), dma(6)],
        anywhere=(1, 2, 3, 4),
        mib=56,
    )
    square = ((D, D), BF16)
    keep, to_after, to_before = call(
        split_experts,
        [((2, D, D), BF16), square, square],
        [ids, w_in[0], w_out[0]],
        [dma(8)],
        anywhere=(1, 2),
        outs_anywhere=(0, 1, 2),
    )
    own_routes = after(routes, p0)[0].reshape(2, T, 2)
    other_routes = swap(own_routes)
    p0, p1, p2, p3 = send_shards([p0, p1, p2, p3])
    p0, p1, p2, order, back_order, keep, other_routes = after(
        p0, p1, p2, order, back_order, keep, other_routes
    )
    own_w, units = call(
        join,
        [((5, 192, D), BF16), ((4 * T, D), BF16)],
        [ids, p0, p1, p2, p3],
        [pltpu.VMEM((N_SHARD, 64, 256), BF16)],
    )
    other_w = swap(own_w)
    own_a, own_w = after(w_attn[0], own_w)
    other_a = swap(own_a)
    weights = (own_w, other_w, own_a, other_a)
    attention_scratch = [w_scratch, pltpu.VMEM((192, D), BF16), dma(5)]

    o0, o1, o2, o3, kept_one, projected_one, small, h_one = call(
        attention_one,
        [rows_shape] * 4 + [((256, D + 256), BF16), ((256, D), BF16), ((2, 128, D), BF16), wide_shape],
        [ids, units, *weights, inputs],
        attention_scratch,
        anywhere=(2, 3, 4, 5, 6),
        mib=24,
    )
    keep = after(keep, o0)[0]
    other_keep = swap(keep)
    packed_shape = ((N_EXPERT, N_SHARD, SIDE, 128), BF16)
    state_shape = ((2 * T + 8, META + D), F32)
    half_shape = ((3, per_expert, D), BF16)
    slope_shape = ((2, per_expert, D), BF16)
    both_shape = ((6, per_expert, D), BF16)
    pieces = return_shards([o0, o1, o2, o3])
    to_after, to_before = after(to_after, to_before, *pieces)[:2]
    own_before, own_after = along(to_after, "shard", 1), along(to_before, "shard", -1)
    sent, state_one = call(
        functools.partial(dispatch, 0),
        [packed_shape, state_shape],
        [ids, h_one, *pieces, small, own_routes, other_routes],
    )
    arrived = exchange(sent)
    own_before, own_after = after(own_before, own_after, arrived)[:2]
    experts = (keep, other_keep, own_before, swap(own_before), own_after, swap(own_after))
    sent, fwd_one, slope = call(
        expert_forward,
        [((N_ALL, SIDE, 128), BF16), half_shape, slope_shape],
        [ids, arrived, order, back_order, *experts],
        [*expert_scratch, staged_scratch, dma(3), dma(5)],
        anywhere=(4, 5, 6, 7, 8, 9),
        mib=24,
    )
    result_one, taken, normed = call(
        combine_next,
        [wide_shape, ((2 * T, D), BF16), rows_shape],
        [ids, exchange(sent).reshape(packed_shape[0]), state_one, small],
    )

    o0, o1, o2, o3, kept_two, projected_two = call(
        attention_two,
        [rows_shape] * 4 + [((256, D + 256), BF16), ((256, D), BF16)],
        [ids, *gather_shards(normed), *weights],
        attention_scratch,
        anywhere=(5, 6, 7, 8),
        mib=24,
    )
    double_shape = ((N_EXPERT, N_SHARD, 2 * SIDE, 128), BF16)
    sent, state_two = call(
        functools.partial(dispatch, 1),
        [double_shape, state_shape],
        [ids, result_one, *return_shards([o0, o1, o2, o3]), small, own_routes, other_routes, cotangent],
    )
    sent, both_two = call(
        expert_both,
        [((N_ALL, 2 * SIDE, 128), BF16), both_shape],
        [ids, exchange(sent), order, back_order, *experts],
        [*expert_scratch, staged_scratch, staged_scratch, dma(3), dma(5)],
        anywhere=(4, 5, 6, 7, 8, 9),
        mib=28,
    )
    routed_shape = ((T + 16, D + 256), BF16)
    returned, r_both_two = after(exchange(sent), up(both_two))
    result_two, grad_middle, sent, routed = call(
        turn,
        [wide_shape, wide_shape, rows_shape, routed_shape],
        [ids, returned.reshape(double_shape[0]), state_two, cotangent, small],
    )

    def attention_grads(s, rows, kept, projected, routed):
        return call(
            functools.partial(attention_backward, s),
            [rows_shape] * 4 + [((352, 3 * D + 256), BF16)],
            [ids, *rows, routed, small, kept, projected, *weights],
            [w_scratch, pltpu.VMEM((256, D), BF16), dma(2)],
            anywhere=(9, 10, 11, 12),
            mib=24,
        )

    n0, n1, n2, n3, packed_two = attention_grads(1, gather_shards(sent), kept_two, projected_two, routed)
    grad_two, sent = call(
        input_backward_next,
        [wide_shape, packed_shape],
        [ids, *return_shards([n0, n1, n2, n3]), grad_middle, small, result_one, state_one],
    )

    arrived, r_packed_two = after(exchange(sent), up(packed_two))
    sent, both_one = call(
        expert_backward,
        [((N_ALL, SIDE, 128), BF16), both_shape],
        [ids, arrived, order, back_order, slope, fwd_one, *experts],
        [*expert_scratch, staged_scratch, pltpu.VMEM(*slope_shape), dma(3), dma(5), dma(2)],
        anywhere=(4, 5, 6, 7, 8, 9, 10, 11),
        mib=28,
    )
    returned = exchange(sent)
    r_both_one = down(after(both_one, returned)[0])
    grad_middle, sent, routed = call(
        middle_backward,
        [wide_shape, rows_shape, routed_shape],
        [ids, returned.reshape(packed_shape[0]), state_one, grad_two, taken, small],
    )
    rows = gather_shards(sent)
    both_one = after(both_one, sent)[0]
    operands = [both_one, r_both_one, both_two, r_both_two]
    held_scratch = pltpu.VMEM((4, 2 * per_expert, D), BF16)
    grad_before, grad_after = call(
        outer_grads,
        [square] * 2,
        [ids, *operands],
        [held_scratch, dma(4, 2)],
        anywhere=(1, 2, 3, 4),
        mib=24,
    )
    kept_one = after(kept_one, grad_before)[0]
    n0, n1, n2, n3, packed_one = attention_grads(0, rows, kept_one, projected_one, routed)

    r_packed_one = down(packed_one)
    pieces = return_shards([n0, n1, n2, n3])
    grad_before, grad_after = after(grad_before, grad_after, *pieces)[:2]
    low, high = along(grad_before, "shard", -1), along(grad_after, "shard", 1)
    payload = call(
        shared_weight_grads,
        [((N_EXPERT, 64, D), BF16)],
        [ids, packed_one, packed_two, r_packed_one, r_packed_two],
        [pltpu.VMEM((2, 352, 3 * D + 256), BF16), dma(2)],
        anywhere=(1, 2, 3, 4),
        mib=24,
    )[0]
    payload, *pieces = after(payload, *pieces)
    stays, leaves = call(
        input_backward_last,
        [((2, T, D), F32)] * 2,
        [ids, *pieces, inputs, grad_middle, small, grad_two, result_one, result_two],
    )
    summed = lax.all_to_all(payload, "expert", 0, 0, tiled=True)
    grads_shape = ((2, D, D), F32)
    grad_in, grad_out = call(
        inner_grads,
        [grads_shape] * 2,
        [ids, *operands],
        [held_scratch, pltpu.VMEM((2, D, D), F32), dma(4, 2), dma(2)],
        anywhere=(1, 2, 3, 4),
        outs_anywhere=(0, 1),
        mib=48,
    )
    summed, grad_in = after(summed, grad_in)
    arrives = swap(leaves)
    shares, attn = call(
        sum_shared,
        [((N_SHARD, 16, D), F32), ((16, D), F32)],
        [ids, summed],
        [pltpu.VMEM((64, D), F32)],
    )
    grad_in, grad_out = call(
        fill_grads,
        [grads_shape] * 2,
        [ids, low, high, after(grad_in, shares)[0], grad_out],
        [pltpu.VMEM((2, D, D), F32), dma(2)],
        anywhere=(3, 4),
        outs_anywhere=(0, 1),
        aliases={3: 0, 4: 1},
        mib=24,
    )
    pairs = [
        (e * N_SHARD + s, (N_SHARD * s + e // N_SHARD) * N_SHARD + e % N_SHARD)
        for e in range(N_EXPERT)
        for s in range(N_SHARD)
    ]
    attn_in = lax.ppermute(attn, ("expert", "shard"), pairs)
    q0, q1, q2, q3, attn_in, grad_in, grad_out = after(*send_shards(shares), attn_in, grad_in, grad_out)
    grad_qkv, grad_attn, grad_one, grad_two, grad_router, acts, grads = call(
        finish,
        [
            ((12, 3 * D), F32),
            ((12, D), F32),
            ((1, 12), F32),
            ((1, 12), F32),
            ((12, 32), F32),
            ((2, T, D), F32),
            ((2, T, D), F32),
        ],
        [ids, q0, q1, q2, q3, attn_in, stays, arrives],
        [pltpu.VMEM((N_SHARD, 16, D), F32)],
    )
    return (
        acts.reshape(1, 2, 1, T, D),
        grads.reshape(1, 2, 1, T, D),
        grad_qkv[None],
        grad_attn[None],
        grad_one,
        grad_two,
        grad_router[None],
        grad_in[None],
        grad_out[None],
    )


def solution(mesh):
    return jax.shard_map(
        local,
        mesh=mesh,
        in_specs=(
            P(None, "expert", "shard", None),
            P(None, "expert", "shard", None),
            P("section", "shard", None),
            P("section", "shard", None),
            P("section", "shard"),
            P("section", "shard"),
            P("section", "shard", None),
            P("section", "expert", None, "shard"),
            P("section", "expert", "shard", None),
            P("section", None, "expert", "shard", None, None),
        ),
        out_specs=(
            P("section", None, "expert", "shard", None),
            P("section", None, "expert", "shard", None),
            P("section", ("expert", "shard"), None),
            P("section", ("expert", "shard"), None),
            P("section", ("expert", "shard")),
            P("section", ("expert", "shard")),
            P("section", ("expert", "shard"), None),
            P("section", "expert", None, "shard"),
            P("section", "expert", "shard", None),
        ),
        check_vma=False,
    )
```
